32 devices in a mesh: lat: 8 (over z, y), lon: 4 (over x, core).
Axes of the slice: x: 2, y: 2, z: 4, core: 2. Of those that a mesh axis runs over, the one named last changes fastest.
Arguments:
- inputs: bfloat16 [320, 720, 256], P('lat', 'lon'), may hold values from -6 to 6
- w_enc: bfloat16 [3, 3, 256, 256], replicated, may hold values from -0.125 to 0.125
- w_proj: bfloat16 [256, 128], replicated, may hold values from -0.375 to 0.375
- film_scale: float32 [720, 128], replicated, may hold values from -3 to 3
- film_shift: float32 [720, 128], replicated, may hold values from -3 to 3
- lead_ids: int32 [8], replicated, may hold values from 0 to 719
- w_head: bfloat16 [3, 3, 128, 128], replicated, may hold values from -0.1875 to 0.1875
- zonal_mix: bfloat16 [360, 360], replicated, may hold values from -0.3125 to 0.3125
Outputs:
- forecast: bfloat16 [8, 160, 360, 128], P('lon', 'lat')
The draws below stay inside these ranges and needn't reach their ends.
Inputs may be any that keep to these rules, and one draw needn't show every extreme that they name: `lead_ids`: rows of the tables; repeats may occur.
All inputs are finite; a program needn't handle non-finite values.
Results may differ from the reference program's by a relative error of at most 0.015.
Values may be sent and summed in bfloat16 or wider, within the bound.
No kernel may reach another device: no remote copies, remote signals or barrier semaphores. Data moves between devices by JAX's collectives and lax.ppermute only.
A program may use at most 128 MiB of HBM per device.

```python
import jax
import jax.numpy as jnp
from jax import lax

C = 256
H = 128
LEAD_TABLE = 720
LEADS = 8
LAT = 320
LON = 720
LONP = 360


def with_ends(values, key, least, top_value):
    spot = [jax.random.randint(jax.random.fold_in(key, axis), (), 0, length) for axis, length in enumerate(values.shape)]
    widest = values.shape.index(max(values.shape))
    beside = spot[:widest] + [(spot[widest] + 1) % values.shape[widest]] + spot[widest + 1:]
    return values.at[tuple(spot)].set(least).at[tuple(beside)].set(top_value)


def levels(key, dims, pieces, least, high):
    loudness = 1.0
    for axis_at, parts in pieces:
        steps = jax.random.uniform(jax.random.fold_in(jax.random.fold_in(key, 6), axis_at), (parts,), jnp.float32, least / len(pieces), high / len(pieces))
        loudness = loudness * jnp.repeat(jnp.exp(steps), dims[axis_at] // parts).reshape((-1,) + (1,) * (len(dims) - 1 - axis_at))
    return loudness


def bell_draw(own_key, shape, deviation, bound, split=(), held_as=jnp.bfloat16):
    entries = deviation * jax.random.normal(own_key, shape, jnp.float32)
    if split:
        entries = entries * levels(own_key, shape, split, -0.22, 0.18)
    return jnp.clip(entries, -bound, bound).astype(held_as)


def setup_inputs(seed: int = 0) -> dict:
    streams_of = jax.random.split(jax.random.key(seed), 9)
    inputs = bell_draw(streams_of[0], (LAT, LON, C), 1.0, 6.0, ((0, 8), (1, 4)))
    w_enc = bell_draw(streams_of[1], (3, 3, C, C), (9 * C) ** -0.5, 0.125)
    w_proj = bell_draw(streams_of[2], (C, H), C ** -0.5, 0.375)
    film_scale = bell_draw(streams_of[3], (LEAD_TABLE, H), 0.5, 3.0, (), jnp.float32)
    film_shift = bell_draw(streams_of[4], (LEAD_TABLE, H), 0.5, 3.0, (), jnp.float32)
    lead_ids = with_ends(jax.random.randint(streams_of[5], (LEADS,), 0, LEAD_TABLE), jax.random.fold_in(streams_of[5], 1), 0, LEAD_TABLE - 1).astype(jnp.int32)
    w_head = bell_draw(streams_of[6], (3, 3, H, H), (9 * H) ** -0.5, 0.1875)
    zonal_mix = bell_draw(streams_of[7], (LONP, LONP), LONP ** -0.5, 0.3125)
    return dict(inputs=inputs, w_enc=w_enc, w_proj=w_proj, film_scale=film_scale, film_shift=film_shift, lead_ids=lead_ids, w_head=w_head, zonal_mix=zonal_mix)


def conv_three(padded, weight):
    batched = padded if padded.ndim == 4 else padded[None]
    result = lax.conv_general_dilated(batched, weight, (1, 1), "VALID", dimension_numbers=("NHWC", "HWIO", "NHWC"), preferred_element_type=jnp.float32)
    return result if padded.ndim == 4 else result[0]


def pool_pairs(field):
    summed = lax.reduce_window(field, jnp.array(0, field.dtype), lax.add, (2, 2, 1), (2, 2, 1), "VALID")
    return summed * 0.25


def wrap_columns(field):
    return jnp.concatenate([field[..., -1:, :], field, field[..., :1, :]], axis=-2)


def reference(inputs, w_enc, w_proj, film_scale, film_shift, lead_ids, w_head, zonal_mix):
    lat_rows, lon_cols, channels = inputs.shape
    padded = wrap_columns(jnp.pad(inputs, ((1, 1), (0, 0), (0, 0))))
    encoded = jax.nn.gelu(conv_three(padded, w_enc))
    pooled = pool_pairs(encoded).astype(jnp.bfloat16)
    head_width = w_proj.shape[1]
    projected = jnp.dot(pooled.reshape(-1, channels), w_proj, preferred_element_type=jnp.float32).astype(jnp.bfloat16)
    projected = projected.reshape(lat_rows // 2, lon_cols // 2, head_width)
    scales = film_scale[lead_ids]
    shifts = film_shift[lead_ids]

    def one_head(pair):
        scale_row, shift_row = pair
        modulated = (projected.astype(jnp.float32) * (1.0 + scale_row) + shift_row).astype(jnp.bfloat16)
        padded_head = wrap_columns(jnp.pad(modulated, ((1, 1), (0, 0), (0, 0))))
        hidden = jax.nn.gelu(conv_three(padded_head, w_head)).astype(jnp.bfloat16)
        mixed = jnp.einsum("ij,ajc->aic", zonal_mix.astype(jnp.float32), hidden.astype(jnp.float32))
        return (modulated.astype(jnp.float32) + mixed).astype(jnp.bfloat16)

    return lax.map(one_head, (scales, shifts))
```

```python
import functools

import jax
import jax.numpy as jnp
from jax import lax
from jax.experimental import pallas as pl
from jax.experimental.pallas import tpu as pltpu
from jax.sharding import PartitionSpec as P

BF = jnp.bfloat16
F32 = jnp.float32
VMEM_LIMIT = 56 * 1024 * 1024


def up16(n):
    return -(-n // 16) * 16


def gelu_twice(x):
    inner = x * (0.7978845608028654 + 0.035677408136300125 * (x * x))
    return x + x * jnp.tanh(inner)


def encoder_kernel(x_ref, up_ref, dn_ref, west_ref, east_ref, g_ref, wp_ref, out_ref, xs, ts, mt, *, pairs):
    rows, cols, ch = x_ref.shape
    wide = xs.shape[1]
    halfw = wide // 2

    def stage(slot, row, r):
        west = west_ref[r : r + 1, :]
        east = east_ref[r : r + 1, :]
        xs[slot, :cols, ch : 2 * ch] = row
        xs[slot, :cols, :ch] = jnp.concatenate([west, row[:-1]], axis=0)
        xs[slot, :cols, 2 * ch :] = jnp.concatenate([row[1:], east], axis=0)

    at = lax.broadcasted_iota(jnp.int32, (halfw, wide), 0)
    of = lax.broadcasted_iota(jnp.int32, (halfw, wide), 1)
    pool = jnp.where((of == 2 * at) | (of == 2 * at + 1), 0.125, 0.0).astype(BF)
    if wide > cols:
        xs[:, cols:, :] = jnp.zeros((rows + 2, wide - cols, 3 * ch), BF)
    stage(0, up_ref[0], 0)
    stage(rows + 1, dn_ref[0], rows + 1)
    for r in range(rows):
        stage(r + 1, x_ref[r], r + 1)
    @pl.loop(0, rows // (2 * pairs))
    def _(c):
        for k in range(4):
            for q in range(pairs):
                d = [xs.at[2 * (c * pairs + q) + i] for i in range(4)]
                pick = ((0, 2), (1, 2), (2, 1), (1, 3))[k]
                one, two = d[pick[0]][...], d[pick[1]][...]
                ts[q * wide : (q + 1) * wide] = one + two if k == 1 else one - two
            mt[k] = jnp.dot(ts[...], g_ref[k], preferred_element_type=F32)
        for q in range(pairs):
            part = pl.ds(q * wide, wide)
            y0 = mt[0, part] + mt[1, part] + mt[2, part]
            y1 = mt[1, part] - mt[2, part] - mt[3, part]
            both = (gelu_twice(y0) + gelu_twice(y1)).astype(BF)
            pooled = jnp.dot(pool, both, preferred_element_type=F32).astype(BF)
            proj = jnp.dot(pooled, wp_ref[...], preferred_element_type=F32).astype(BF)
            out_ref[c * pairs + q] = proj[: cols // 2]


def encode(x, up, dn, west, east, g, wp, pairs):
    rows, cols, ch = x.shape
    head = wp.shape[1]
    wide = -(-cols // 32) * 32
    return pl.pallas_call(
        functools.partial(encoder_kernel, pairs=pairs),
        out_shape=jax.ShapeDtypeStruct((rows // 2, cols // 2, head), BF),
        scratch_shapes=[
            pltpu.VMEM((rows + 2, wide, 3 * ch), BF),
            pltpu.VMEM((pairs * wide, 3 * ch), BF),
            pltpu.VMEM((4, pairs * wide, ch), F32),
        ],
        compiler_params=pltpu.CompilerParams(vmem_limit_bytes=VMEM_LIMIT),
        name="encode",
    )(x, up, dn, west, east, g, wp)


def head_kernel(meta_ref, p_ref, halo_ref, scale_ref, shift_ref, w_ref, z_ref, out_ref, ps, ws, bs, zs, ms, *, rows_step):
    shards, rows, piece, ch = p_ref.shape
    cols = shards * piece
    wide = ps.shape[1]
    leads = out_ref.shape[0]
    step = pl.program_id(0)

    def stage(slot, parts):
        row = jnp.concatenate(parts, axis=0)
        ps[slot, :cols, ch : 2 * ch] = row
        ps[slot, :cols, :ch] = jnp.concatenate([row[-1:], row[:-1]], axis=0)
        ps[slot, :cols, 2 * ch :] = jnp.concatenate([row[1:], row[:1]], axis=0)

    @pl.when(step == 0)
    def _():
        if wide > cols:
            ps[:, cols:, :] = jnp.zeros((rows + 2, wide - cols, 3 * ch), BF)
        zs[...] = jnp.zeros(zs.shape, BF)
        zs[:cols, :cols] = z_ref[...]
        stage(0, [halo_ref[s, 0] for s in range(shards)])
        stage(rows + 1, [halo_ref[s, 1] for s in range(shards)])
        for r in range(rows):
            stage(r + 1, [p_ref[s, r] for s in range(shards)])
        for lead in range(leads):
            row_at = meta_ref[2 + lead]
            gain = 1.0 + scale_ref[pl.ds(row_at, 1), :]
            shift = shift_ref[pl.ds(row_at, 1), :]
            ms[2 * lead : 2 * lead + 1, :] = gain
            ms[2 * lead + 1 : 2 * lead + 2, :] = shift
            gain_t = jnp.transpose(jnp.broadcast_to(gain, (ch, ch)))
            shift_t = jnp.transpose(jnp.broadcast_to(shift, (ch, ch)))
            for dr in range(3):
                total = jnp.zeros((ch, ch), F32)
                for dc in range(3):
                    at = (dr * 3 + dc) * ch
                    w = w_ref[at : at + ch, :].astype(F32)
                    ws[at : at + ch, lead * ch : (lead + 1) * ch] = (w * gain_t).astype(BF)
                    total = total + w * shift_t
                bs[dr : dr + 1, lead * ch : (lead + 1) * ch] = jnp.sum(total, axis=0, keepdims=True)

    first = jnp.where(step == 0, meta_ref[0], 0).astype(F32)
    last = jnp.where(step == pl.num_programs(0) - 1, meta_ref[1], 0).astype(F32)
    bias = bs[0:1, :] + bs[1:2, :] + bs[2:3, :]
    bias_first = bias - first * bs[0:1, :]
    bias_last = bias - last * bs[2:3, :]
    base = step * rows_step
    lhs = jnp.concatenate(
        [jnp.concatenate([ps[base + i + dr] for dr in range(3)], axis=1) for i in range(rows_step)],
        axis=0,
    )
    conv = jnp.dot(lhs, ws[...], preferred_element_type=F32)
    for i in range(rows_step):
        row_bias = bias_first if i == 0 else (bias_last if i == rows_step - 1 else bias)
        y = conv[i * wide : (i + 1) * wide] + row_bias
        hidden = (0.5 * gelu_twice(y)).astype(BF)
        mixed = jnp.dot(zs[...], hidden, preferred_element_type=F32)
        center = ps[base + i + 1, :, ch : 2 * ch].astype(F32)
        for lead in range(leads):
            mod = center * ms[2 * lead : 2 * lead + 1, :] + ms[2 * lead + 1 : 2 * lead + 2, :]
            res = (mod + mixed[:, lead * ch : (lead + 1) * ch]).astype(BF)
            out_ref[lead, i] = res[:cols]


def forecast_heads(meta, band, halo, scale, shift, w, z, leads, rows_step):
    shards, rows, piece, ch = band.shape
    cols = shards * piece
    wide = up16(cols)
    full = lambda a: pl.BlockSpec(a.shape, lambda i, m: (0,) * a.ndim)
    return pl.pallas_call(
        functools.partial(head_kernel, rows_step=rows_step),
        grid_spec=pltpu.PrefetchScalarGridSpec(
            num_scalar_prefetch=1,
            grid=(rows // rows_step,),
            in_specs=[full(a) for a in (band, halo, scale, shift, w, z)],
            out_specs=pl.BlockSpec((leads, rows_step, cols, ch), lambda i, m: (0, i, 0, 0)),
            scratch_shapes=[
                pltpu.VMEM((rows + 2, wide, 3 * ch), BF),
                pltpu.VMEM((9 * ch, leads * ch), BF),
                pltpu.VMEM((8, leads * ch), F32),
                pltpu.VMEM((wide, wide), BF),
                pltpu.VMEM((8, ch), F32),
            ],
        ),
        out_shape=jax.ShapeDtypeStruct((leads, rows, cols, ch), BF),
        compiler_params=pltpu.CompilerParams(vmem_limit_bytes=VMEM_LIMIT),
        name="heads",
    )(meta, band, halo, scale, shift, w, z)


def neighbours(axis, size, wrap):
    count = size if wrap else size - 1
    up = [(i, (i + 1) % size) for i in range(count)]
    return up, [(j, i) for i, j in up]


def shards(inputs, w_enc, w_proj, film_scale, film_shift, lead_ids, w_head, zonal_mix):
    rows, cols, ch = inputs.shape
    lat = lax.axis_size("lat")
    lon = lax.axis_size("lon")
    lat_up, lat_dn = neighbours("lat", lat, False)
    lon_up, lon_dn = neighbours("lon", lon, True)
    above = lax.ppermute(inputs[-1:], "lat", lat_up)
    below = lax.ppermute(inputs[:1], "lat", lat_dn)
    west_out = jnp.concatenate([above[:, -1], inputs[:, -1], below[:, -1]], axis=0)
    east_out = jnp.concatenate([above[:, 0], inputs[:, 0], below[:, 0]], axis=0)
    west = lax.ppermute(west_out, "lon", lon_up)
    east = lax.ppermute(east_out, "lon", lon_dn)
    w = w_enc.astype(F32)
    half = 0.5 * (w[0] + w[2])
    g = jnp.stack([w[0], half + 0.5 * w[1], half - 0.5 * w[1], w[2]]).astype(BF)
    g = g.reshape(4, 3 * ch, w_enc.shape[-1])
    proj = encode(inputs, above, below, west, east, g, w_proj, 4)
    band = lax.all_gather(proj, "lon", axis=0, tiled=False)
    p_above = lax.ppermute(proj[-1:], "lat", lat_up)
    p_below = lax.ppermute(proj[:1], "lat", lat_dn)
    halo = lax.all_gather(jnp.concatenate([p_above, p_below], axis=0), "lon", axis=0, tiled=False)
    leads = lead_ids.shape[0] // lon
    mine = lax.dynamic_slice_in_dim(lead_ids, lax.axis_index("lon") * leads, leads)
    lat_at = lax.axis_index("lat")
    flags = jnp.stack([lat_at == 0, lat_at == lat - 1]).astype(jnp.int32)
    meta = jnp.concatenate([flags, mine])
    wh = w_head.reshape(-1, w_head.shape[-1])
    return forecast_heads(meta, band, halo, film_scale, film_shift, wh, zonal_mix, leads, 4)


def solution(mesh):
    in_specs = (P("lat", "lon", None), P(), P(), P(), P(), P(), P(), P())
    out_specs = P("lon", "lat", None, None)
    return jax.shard_map(shards, mesh=mesh, in_specs=in_specs, out_specs=out_specs, check_vma=False)
```

```python
import functools

import jax
import jax.numpy as jnp
from jax import lax
from jax.experimental import pallas as pl
from jax.experimental.pallas import tpu as pltpu
from jax.sharding import PartitionSpec as P

BF = jnp.bfloat16
F32 = jnp.float32
VMEM_LIMIT = 36 * 1024 * 1024
EDGE = 2
STEP = 4
BIAS, GAIN, SHIFT = 0, 3, 4


def up_to(n, unit):
    return -(-n // unit) * unit


def gelu_twice(x):
    inner = x * (0.7978845608028654 + 0.035677408136300125 * (x * x))
    return x + x * jnp.tanh(inner)


def params():
    return pltpu.CompilerParams(vmem_limit_bytes=VMEM_LIMIT)


def weights_kernel(ids_ref, we_ref, wh_ref, scale_ref, shift_ref, z_ref, g_ref, ws_ref, vec_ref, zs_ref):
    ch = we_ref.shape[-1]
    head = wh_ref.shape[-1]
    leads = ws_ref.shape[1] // head
    cols = z_ref.shape[0]
    for dc in range(3):
        at = slice(dc * ch, (dc + 1) * ch)
        w = [we_ref[dr, dc].astype(F32) for dr in range(3)]
        half = 0.5 * (w[0] + w[2])
        g_ref[0, at] = we_ref[0, dc]
        g_ref[1, at] = (half + 0.5 * w[1]).astype(BF)
        g_ref[2, at] = (half - 0.5 * w[1]).astype(BF)
        g_ref[3, at] = we_ref[2, dc]
    zs_ref[...] = jnp.zeros(zs_ref.shape, BF)
    zs_ref[:cols, :cols] = z_ref[...]
    for lead in range(leads):
        lanes = slice(lead * head, (lead + 1) * head)
        gain = 1.0 + scale_ref[pl.ds(ids_ref[lead], 1), :]
        shift = shift_ref[pl.ds(ids_ref[lead], 1), :]
        vec_ref[GAIN : GAIN + 1, lanes] = gain
        vec_ref[SHIFT : SHIFT + 1, lanes] = shift
        gain_t = jnp.transpose(jnp.broadcast_to(gain, (head, head)))
        shift_t = jnp.transpose(jnp.broadcast_to(shift, (head, head)))
        for dr in range(3):
            total = jnp.zeros((head, head), F32)
            for dc in range(3):
                at = (dr * 3 + dc) * head
                w = wh_ref[dr, dc].astype(F32)
                ws_ref[at : at + head, lanes] = (w * gain_t).astype(BF)
                total = total + w * shift_t
            vec_ref[BIAS + dr : BIAS + dr + 1, lanes] = jnp.sum(total, axis=0, keepdims=True)


def prepare(ids, w_enc, w_head, scale, shift, z):
    leads = ids.shape[0]
    ch, head, cols = w_enc.shape[-1], w_head.shape[-1], z.shape[0]
    wide = up_to(cols, 16)
    vmem = pl.BlockSpec(memory_space=pltpu.VMEM)
    return pl.pallas_call(
        weights_kernel,
        in_specs=[pl.BlockSpec(memory_space=pltpu.SMEM)] + [vmem] * 5,
        out_specs=[vmem] * 4,
        out_shape=[
            jax.ShapeDtypeStruct((4, 3 * ch, ch), BF),
            jax.ShapeDtypeStruct((9 * head, leads * head), BF),
            jax.ShapeDtypeStruct((8, leads * head), F32),
            jax.ShapeDtypeStruct((wide, wide), BF),
        ],
        compiler_params=params(),
        name="weights",
    )(ids, w_enc, w_head, scale, shift, z)


def encoder_kernel(meta_ref, x_ref, west_ref, east_ref, above_ref, below_ref, g_ref, wp_ref, out_ref, xs, xr, ys, sem, *, first, runs, group):
    rows, cols, ch = x_ref.shape
    wide = xs.shape[1]
    halfw = wide // 2
    here = [(max(a, 0), min(b, rows)) for a, b in runs]
    copies, at = [], 0
    for i, (a, b) in enumerate(here):
        copies.append(pltpu.make_async_copy(x_ref.at[a:b], xr.at[at : at + b - a], sem.at[i]))
        at += b - a
    for c in copies:
        c.start()
    if wide > cols:
        xs[:, cols:, :] = jnp.zeros((xs.shape[0], wide - cols, 3 * ch), BF)
    at = lax.broadcasted_iota(jnp.int32, (halfw, wide), 0)
    of = lax.broadcasted_iota(jnp.int32, (halfw, wide), 1)
    pool = jnp.where((of == 2 * at) | (of == 2 * at + 1), 0.125, 0.0).astype(BF)

    def put(slot, left, center, right):
        xs[slot, :cols, :ch] = left
        xs[slot, :cols, ch : 2 * ch] = center
        xs[slot, :cols, 2 * ch :] = right

    slot = held = 0
    for (a, b), copy in zip(runs, copies):
        waited = False
        for r in range(a, b):
            if r < 0 or r >= rows:
                halo = above_ref if r < 0 else below_ref
                row = halo[r + halo.shape[0] if r < 0 else r - rows]
                put(slot, row[:cols], row[1 : cols + 1], row[2:])
            else:
                if not waited:
                    copy.wait()
                    waited = True
                row = xr[held]
                held += 1
                west, east = west_ref[r : r + 1, :], east_ref[r : r + 1, :]
                put(slot, jnp.concatenate([west, row[:-1]], axis=0), row, jnp.concatenate([row[1:], east], axis=0))
            slot += 1

    per_run = (runs[0][1] - runs[0][0] - 2) // 2
    pairs = per_run * len(runs)

    def multiply(c):
        d = []
        for q in range(c * group, (c + 1) * group):
            base = (q // per_run) * (2 * per_run + 2) + 2 * (q % per_run)
            d.append([xs.at[base + i] for i in range(4)])
        t = [
            [e[0][...] - e[2][...] for e in d],
            [e[1][...] + e[2][...] for e in d],
            [e[2][...] - e[1][...] for e in d],
            [e[1][...] - e[3][...] for e in d],
        ]
        for k in range(4):
            ys[c % 2, k] = jnp.dot(jnp.concatenate(t[k], axis=0), g_ref[k], preferred_element_type=F32)

    def finish(c):
        for i in range(group):
            part = slice(i * wide, (i + 1) * wide)
            m = [ys.at[c % 2, k, part] for k in range(4)]
            both = gelu_twice(m[0][...] + m[1][...] + m[2][...])
            both = both + gelu_twice(m[1][...] - m[2][...] - m[3][...])
            pooled = jnp.dot(pool, both.astype(BF), preferred_element_type=F32).astype(BF)
            proj = jnp.dot(pooled, wp_ref[...], preferred_element_type=F32)[: cols // 2]
            q = c * group + i
            row = (runs[q // per_run][0] + 1) // 2 + q % per_run
            if row < 0:
                proj = jnp.where(meta_ref[0] == 0, proj, 0.0)
            elif row >= rows // 2:
                proj = jnp.where(meta_ref[1] == 0, proj, 0.0)
            out_ref[q] = proj.astype(BF)

    for c in range(pairs // group):
        multiply(c)
        if c:
            finish(c - 1)
    finish(pairs // group - 1)


def encode(meta, x, west, east, above, below, g, wp, runs, group):
    rows, cols, ch = x.shape
    head = wp.shape[1]
    wide = up_to(cols, 32)
    slots = sum(b - a for a, b in runs)
    held = sum(min(b, rows) - max(a, 0) for a, b in runs)
    vmem = pl.BlockSpec(memory_space=pltpu.VMEM)
    return pl.pallas_call(
        functools.partial(encoder_kernel, first=0, runs=runs, group=group),
        in_specs=[pl.BlockSpec(memory_space=pltpu.SMEM), pl.BlockSpec(memory_space=pl.ANY)] + [vmem] * 6,
        out_specs=vmem,
        out_shape=jax.ShapeDtypeStruct(((slots - 2 * len(runs)) // 2, cols // 2, head), BF),
        scratch_shapes=[
            pltpu.VMEM((slots, wide, 3 * ch), BF),
            pltpu.VMEM((held, cols, ch), BF),
            pltpu.VMEM((2, 4, group * wide, ch), F32),
            pltpu.SemaphoreType.DMA((len(runs),)),
        ],
        compiler_params=params(),
        name="encode",
    )(meta, x, west, east, above, below, g, wp)


def head_kernel(meta_ref, *refs, moves, blocks, rows, shards):
    sources = refs[: len(moves)]
    ws_ref, vec_ref, zs_ref = refs[len(moves) : len(moves) + 3]
    out_ref, band, ps, sem = refs[-4:]
    ch = ps.shape[2] // 3
    wide = ps.shape[1]
    leads = out_ref.shape[0]
    cols = out_ref.shape[2]
    step = pl.program_id(0)
    block = blocks[0] + step * (blocks[1] - blocks[0] if len(blocks) > 1 else 0)

    @pl.when(step == 0)
    def _():
        copies = []
        for source, (slot, pieces) in zip(sources, moves):
            for a, b, to in pieces:
                copies.append(
                    pltpu.make_async_copy(
                        source.at[:, a:b],
                        band.at[pl.ds(meta_ref[slot], source.shape[0]), to : to + b - a],
                        sem.at[len(copies)],
                    )
                )
        for c in copies:
            c.start()
        if wide > cols:
            ps[:, cols:, :] = jnp.zeros((ps.shape[0], wide - cols, 3 * ch), BF)
        for c in copies:
            c.wait()

    base = block * STEP
    for i in range(STEP + 2):
        row = jnp.concatenate([band[s, base + i] for s in range(shards)], axis=0)
        ps[i, :cols, ch : 2 * ch] = row
        ps[i, :cols, :ch] = jnp.concatenate([row[-1:], row[:-1]], axis=0)
        ps[i, :cols, 2 * ch :] = jnp.concatenate([row[1:], row[:1]], axis=0)

    first = jnp.where(block == 0, meta_ref[0], 0).astype(F32)
    last = jnp.where(block == rows // STEP - 1, meta_ref[1], 0).astype(F32)
    bias = vec_ref[BIAS : BIAS + 1, :] + vec_ref[BIAS + 1 : BIAS + 2, :] + vec_ref[BIAS + 2 : BIAS + 3, :]
    bias_first = bias - first * vec_ref[BIAS : BIAS + 1, :]
    bias_last = bias - last * vec_ref[BIAS + 2 : BIAS + 3, :]

    def conv(i):
        lhs = jnp.concatenate([ps[i], ps[i + 1], ps[i + 2]], axis=1)
        return jnp.dot(lhs, ws_ref[...], preferred_element_type=F32)

    def finish(i, y):
        y = y + (bias_first if i == 0 else (bias_last if i == STEP - 1 else bias))
        hidden = (0.5 * gelu_twice(y)).astype(BF)
        mixed = jnp.dot(zs_ref[...], hidden, preferred_element_type=F32)
        center = ps[i + 1, :, ch : 2 * ch].astype(F32)
        for lead in range(leads):
            lanes = slice(lead * ch, (lead + 1) * ch)
            mod = center * vec_ref[GAIN : GAIN + 1, lanes] + vec_ref[SHIFT : SHIFT + 1, lanes]
            out_ref[lead, i] = (mod + mixed[:, lanes]).astype(BF)[:cols]

    before = None
    for i in range(STEP):
        y = conv(i)
        if before is not None:
            finish(i - 1, before)
        before = y
    finish(STEP - 1, before)


def forecast_heads(meta, sources, moves, ws, vec, zs, so_far, blocks, shape):
    leads, rows, cols, ch = shape
    shards = cols // sources[0].shape[2]
    wide = zs.shape[0]
    full = lambda a: pl.BlockSpec(a.shape, lambda i, m: (0,) * a.ndim)
    anywhere = pl.BlockSpec(memory_space=pl.ANY)
    operands = [*sources, ws, vec, zs]
    in_specs = [anywhere] * len(sources) + [full(a) for a in (ws, vec, zs)]
    alias = {}
    if so_far is not None:
        alias = {len(operands) + 1: 0}
        operands.append(so_far)
        in_specs.append(anywhere)
    stride = blocks[1] - blocks[0] if len(blocks) > 1 else 0
    start = blocks[0]
    return pl.pallas_call(
        functools.partial(head_kernel, moves=moves, blocks=blocks, rows=rows, shards=shards),
        grid_spec=pltpu.PrefetchScalarGridSpec(
            num_scalar_prefetch=1,
            grid=(len(blocks),),
            in_specs=in_specs,
            out_specs=pl.BlockSpec((leads, STEP, cols, ch), lambda i, m: (0, start + i * stride, 0, 0)),
            scratch_shapes=[
                pltpu.VMEM((shards, rows + 2, cols // shards, ch), BF),
                pltpu.VMEM((STEP + 2, wide, 3 * ch), BF),
                pltpu.SemaphoreType.DMA((sum(len(m[1]) for m in moves),)),
            ],
        ),
        out_shape=jax.ShapeDtypeStruct(shape, BF),
        input_output_aliases=alias,
        compiler_params=params(),
        name="heads",
    )(meta, *operands)


def neighbours(size, wrap):
    count = size if wrap else size - 1
    up = [(i, (i + 1) % size) for i in range(count)]
    return up, [(j, i) for i, j in up]


def swap(size, bit):
    return [(i, i ^ bit) for i in range(size)]


def shards(inputs, w_enc, w_proj, film_scale, film_shift, lead_ids, w_head, zonal_mix):
    rows, cols, ch = inputs.shape
    lat, lon = lax.axis_size("lat"), lax.axis_size("lon")
    lat_at, lon_at = lax.axis_index("lat"), lax.axis_index("lon")
    lat_up, lat_dn = neighbours(lat, False)
    lon_up, lon_dn = neighbours(lon, True)
    two_level = lon == 4
    reach = 2 * EDGE - 1
    leads = lead_ids.shape[0] // lon
    head = w_proj.shape[1]
    band_rows = rows // 2

    west = lax.ppermute(inputs[:, -1], "lon", lon_up)
    east = lax.ppermute(inputs[:, 0], "lon", lon_dn)

    def slab(part):
        return jnp.concatenate([west[part][:, None], inputs[part], east[part][:, None]], axis=1)

    above = lax.ppermute(slab(slice(rows - reach, rows)), "lat", lat_up)
    below = lax.ppermute(slab(slice(0, reach)), "lat", lat_dn)

    mine = lax.dynamic_slice_in_dim(lead_ids, lon_at * leads, leads)
    meta = jnp.stack(
        [lat_at == 0, lat_at == lat - 1, lon_at, lon_at ^ 2, lon_at ^ 1, lon_at ^ 3, 0]
    ).astype(jnp.int32)
    g, ws, vec, zs = prepare(mine, w_enc, w_head, film_scale, film_shift, zonal_mix)

    middle = band_rows // 2
    plan = [
        (((2 * EDGE - 1, 2 * middle + 1),), 2),
        (((2 * middle - 1, 2 * (band_rows - EDGE) + 1),), 2),
        (((-3, 2 * EDGE + 1), (rows - 2 * EDGE - 1, rows + 3)), EDGE + 1),
    ]
    none = jnp.zeros((reach, cols + 2, ch), BF)
    proj = []
    for k, (runs, group) in enumerate(plan):
        halos = (above, below) if k == 2 else (none, none)
        proj.append(encode(meta, inputs, west, east, *halos, g, w_proj, runs, group))

    sent = []
    for own in proj:
        if two_level:
            across = lax.ppermute(own, "lon", swap(lon, 2))
            beside = lax.ppermute(own, "lon", swap(lon, 1))
            both = lax.ppermute(across, "lon", swap(lon, 1))
            sent.append([(2, own[None]), (3, across[None]), (4, beside[None]), (5, both[None])])
        else:
            sent.append([(6, lax.all_gather(own, "lon", axis=0, tiled=False))])

    def sources(ranges):
        arrays, moves = [], []
        for group, pieces in zip(sent, ranges):
            for slot, a in group if pieces else ():
                arrays.append(a)
                moves.append((slot, pieces))
        return arrays, moves

    shape = (leads, band_rows, cols // 2 * lon, head)
    upper, lower = middle - EDGE, band_rows - EDGE - middle
    blocks = band_rows // STEP
    arrays, moves = sources([[(0, upper, EDGE + 1)], [(0, lower, middle + 1)], []])
    out = forecast_heads(meta, arrays, moves, ws, vec, zs, None, list(range(1, blocks - 1)), shape)
    keep = STEP + 1 - EDGE
    arrays, moves = sources(
        [
            [(0, keep, EDGE + 1)],
            [(lower - keep, lower, band_rows - EDGE + 1 - keep)],
            [(0, EDGE + 1, 0), (EDGE + 1, 2 * EDGE + 2, band_rows + 1 - EDGE)],
        ]
    )
    return forecast_heads(meta, arrays, moves, ws, vec, zs, out, [0, blocks - 1], shape)


def solution(mesh):
    in_specs = (P("lat", "lon", None), P(), P(), P(), P(), P(), P(), P())
    out_specs = P("lon", "lat", None, None)
    return jax.shard_map(shards, mesh=mesh, in_specs=in_specs, out_specs=out_specs, check_vma=False)
```

```python
import functools

import jax
import jax.numpy as jnp
from jax import lax
from jax.experimental import pallas as pl
from jax.experimental.pallas import tpu as pltpu
from jax.sharding import PartitionSpec as P

BF = jnp.bfloat16
F32 = jnp.float32
MIB = 1024 * 1024
EDGE = 2
STEP = 4
BIAS, GAIN, SHIFT = 0, 3, 4


def up_to(n, unit):
    return -(-n // unit) * unit


def gelu_twice(x):
    inner = x * (0.7978845608028654 + 0.035677408136300125 * (x * x))
    return x + x * jnp.tanh(inner)


def params(mib):
    return pltpu.CompilerParams(vmem_limit_bytes=mib * MIB)


def weights_kernel(
    ids_ref, x_ref, west_ref, east_ref, we_hbm, wh_hbm, scale_hbm, shift_hbm, z_hbm,
    g_ref, ws_ref, vec_ref, zs_ref, up_ref, dn_ref,
    edge, we_ref, wh_ref, tab, z_ref, sem,
):
    ch = we_ref.shape[-1]
    head = wh_ref.shape[-1]
    leads = ws_ref.shape[1] // head
    cols = z_ref.shape[0]
    rows, xcols, _ = x_ref.shape
    reach = up_ref.shape[0]
    copies = [
        (x_ref.at[:reach], edge.at[:reach]),
        (x_ref.at[rows - reach :], edge.at[reach:]),
        (we_hbm, we_ref),
        (z_hbm, z_ref),
        (wh_hbm, wh_ref),
    ]
    for lead in range(leads):
        block = pl.multiple_of((ids_ref[lead] // 8) * 8, 8)
        copies.append((scale_hbm.at[pl.ds(block, 8)], tab.at[lead, 0]))
        copies.append((shift_hbm.at[pl.ds(block, 8)], tab.at[lead, 1]))
    copies = [pltpu.make_async_copy(one, two, sem.at[i]) for i, (one, two) in enumerate(copies)]
    for c in copies:
        c.start()
    copies[0].wait()
    copies[1].wait()
    for i in range(reach):
        for slab, r, at in ((dn_ref, i, i), (up_ref, rows - reach + i, reach + i)):
            slab[i] = jnp.concatenate([west_ref[r : r + 1, :], edge[at], east_ref[r : r + 1, :]], axis=0)
    copies[2].wait()
    for dc in range(3):
        at = slice(dc * ch, (dc + 1) * ch)
        w = [we_ref[dr, dc].astype(F32) for dr in range(3)]
        half = 0.5 * (w[0] + w[2])
        g_ref[0, at] = we_ref[0, dc]
        g_ref[1, at] = (half + 0.5 * w[1]).astype(BF)
        g_ref[2, at] = (half - 0.5 * w[1]).astype(BF)
        g_ref[3, at] = we_ref[2, dc]
    for c in copies[3:]:
        c.wait()
    zs_ref[...] = jnp.zeros(zs_ref.shape, BF)
    zs_ref[:cols, :cols] = z_ref[...] * jnp.asarray(0.5, BF)
    for lead in range(leads):
        lanes = slice(lead * head, (lead + 1) * head)
        at = ids_ref[lead] % 8
        gain = 1.0 + tab[lead, 0, pl.ds(at, 1), :]
        shift = tab[lead, 1, pl.ds(at, 1), :]
        vec_ref[GAIN : GAIN + 1, lanes] = gain
        vec_ref[SHIFT : SHIFT + 1, lanes] = shift
        gain_t = jnp.transpose(jnp.broadcast_to(gain, (head, head)))
        shift_t = jnp.transpose(jnp.broadcast_to(shift, (head, head)))
        for dr in range(3):
            total = jnp.zeros((head, head), F32)
            for dc in range(3):
                at = (dr * 3 + dc) * head
                w = wh_ref[dr, dc].astype(F32)
                ws_ref[at : at + head, lanes] = (w * gain_t).astype(BF)
                total = total + w * shift_t
            vec_ref[BIAS + dr : BIAS + dr + 1, lanes] = jnp.sum(total, axis=0, keepdims=True)


def prepare(ids, x, west, east, w_enc, w_head, scale, shift, z, reach):
    leads = ids.shape[0]
    ch, head, cols = w_enc.shape[-1], w_head.shape[-1], z.shape[0]
    xcols = x.shape[1]
    wide = up_to(cols, 16)
    vmem = pl.BlockSpec(memory_space=pltpu.VMEM)
    anywhere = pl.BlockSpec(memory_space=pl.ANY)
    return pl.pallas_call(
        weights_kernel,
        in_specs=[pl.BlockSpec(memory_space=pltpu.SMEM), anywhere, vmem, vmem] + [anywhere] * 5,
        out_specs=[vmem] * 6,
        out_shape=[
            jax.ShapeDtypeStruct((4, 3 * ch, ch), BF),
            jax.ShapeDtypeStruct((9 * head, leads * head), BF),
            jax.ShapeDtypeStruct((8, leads * head), F32),
            jax.ShapeDtypeStruct((wide, wide), BF),
            jax.ShapeDtypeStruct((reach, xcols + 2, ch), BF),
            jax.ShapeDtypeStruct((reach, xcols + 2, ch), BF),
        ],
        scratch_shapes=[
            pltpu.VMEM((2 * reach, xcols, ch), BF),
            pltpu.VMEM(w_enc.shape, BF),
            pltpu.VMEM(w_head.shape, BF),
            pltpu.VMEM((leads, 2, 8, head), F32),
            pltpu.VMEM(z.shape, BF),
            pltpu.SemaphoreType.DMA((5 + 2 * leads,)),
        ],
        compiler_params=params(16),
        name="weights",
    )(ids, x, west, east, w_enc, w_head, scale, shift, z)


def encoder_kernel(meta_ref, x_ref, west_ref, east_ref, above_ref, below_ref, g_ref, wp_ref, out_ref, xs, xr, ys, st, sem, *, runs, group):
    rows, cols, ch = x_ref.shape
    wide = xs.shape[1]
    halfw = wide // 2
    here = [(max(a, 0), min(b, rows)) for a, b in runs]
    copies, at = [], 0
    for i, (a, b) in enumerate(here):
        copies.append(pltpu.make_async_copy(x_ref.at[a:b], xr.at[at : at + b - a], sem.at[i]))
        at += b - a
    for c in copies:
        c.start()
    if wide > cols:
        xs[:, cols:, :] = jnp.zeros((xs.shape[0], wide - cols, 3 * ch), BF)
    def put(slot, left, center, right):
        xs[slot, :cols, :ch] = left
        xs[slot, :cols, ch : 2 * ch] = center
        xs[slot, :cols, 2 * ch :] = right

    slot = held = 0
    for (a, b), copy in zip(runs, copies):
        waited = False
        for r in range(a, b):
            if r < 0 or r >= rows:
                halo = above_ref if r < 0 else below_ref
                row = halo[r + halo.shape[0] if r < 0 else r - rows]
                put(slot, row[:cols], row[1 : cols + 1], row[2:])
            else:
                if not waited:
                    copy.wait()
                    waited = True
                row = xr[held]
                held += 1
                west, east = west_ref[r : r + 1, :], east_ref[r : r + 1, :]
                put(slot, jnp.concatenate([west, row[:-1]], axis=0), row, jnp.concatenate([row[1:], east], axis=0))
            slot += 1

    per_run = (runs[0][1] - runs[0][0] - 2) // 2
    pairs = per_run * len(runs)

    def multiply(c):
        d = []
        for q in range(c * group, (c + 1) * group):
            base = (q // per_run) * (2 * per_run + 2) + 2 * (q % per_run)
            d.append([xs.at[base + i] for i in range(4)])
        t = [
            [e[0][...] - e[2][...] for e in d],
            [e[1][...] + e[2][...] for e in d],
            [e[2][...] - e[1][...] for e in d],
            [e[1][...] - e[3][...] for e in d],
        ]
        for k in range(4):
            ys[c % 2, k] = jnp.dot(jnp.concatenate(t[k], axis=0), g_ref[k], preferred_element_type=F32)

    def finish(c):
        n = group * wide
        for i in range(group):
            part = slice(i * wide, (i + 1) * wide)
            m = [ys.at[c % 2, k, part] for k in range(4)]
            both = gelu_twice(m[0][...] + m[1][...] + m[2][...])
            both = both + gelu_twice(m[1][...] - m[2][...] - m[3][...])
            for j in range(ch // 128):
                st[j, part] = both[:, j * 128 : (j + 1) * 128]
        pooled = [
            st[j, pl.ds(0, n // 2, stride=2), :] + st[j, pl.ds(1, n // 2, stride=2), :] for j in range(ch // 128)
        ]
        pooled = (jnp.concatenate(pooled, axis=1) * 0.125).astype(BF)
        proj = jnp.dot(pooled, wp_ref[...], preferred_element_type=F32)
        for i in range(group):
            part = proj[i * halfw : i * halfw + cols // 2]
            q = c * group + i
            row = (runs[q // per_run][0] + 1) // 2 + q % per_run
            if row < 0:
                part = jnp.where(meta_ref[0] == 0, part, 0.0)
            elif row >= rows // 2:
                part = jnp.where(meta_ref[1] == 0, part, 0.0)
            out_ref[q] = part.astype(BF)

    for c in range(pairs // group):
        multiply(c)
        if c:
            finish(c - 1)
    finish(pairs // group - 1)


def encode(meta, x, west, east, above, below, g, wp, runs, group):
    rows, cols, ch = x.shape
    head = wp.shape[1]
    wide = up_to(cols, 32)
    slots = sum(b - a for a, b in runs)
    held = sum(min(b, rows) - max(a, 0) for a, b in runs)
    vmem = pl.BlockSpec(memory_space=pltpu.VMEM)
    return pl.pallas_call(
        functools.partial(encoder_kernel, runs=runs, group=group),
        in_specs=[pl.BlockSpec(memory_space=pltpu.SMEM), pl.BlockSpec(memory_space=pl.ANY)] + [vmem] * 6,
        out_specs=vmem,
        out_shape=jax.ShapeDtypeStruct(((slots - 2 * len(runs)) // 2, cols // 2, head), BF),
        scratch_shapes=[
            pltpu.VMEM((slots, wide, 3 * ch), BF),
            pltpu.VMEM((held, cols, ch), BF),
            pltpu.VMEM((2, 4, group * wide, ch), F32),
            pltpu.VMEM((ch // 128, group * wide, 128), F32),
            pltpu.SemaphoreType.DMA((len(runs),)),
        ],
        compiler_params=params(24),
        name="encode",
    )(meta, x, west, east, above, below, g, wp)


def head_kernel(meta_ref, *refs, moves, blocks, shards, aliased):
    sources = refs[: len(moves)]
    ws_ref, vec_ref, zs_ref = refs[len(moves) : len(moves) + 3]
    out_ref, band, ps, cs, outs, sem, out_sem = refs[len(moves) + 3 + aliased :]
    ch = ps.shape[3] // 3
    wide = ps.shape[2]
    leads, rows, cols, _ = out_ref.shape

    copies = []
    for source, (slot, pieces) in zip(sources, moves):
        for a, b, to in pieces:
            copies.append(
                pltpu.make_async_copy(
                    source.at[:, a:b],
                    band.at[pl.ds(meta_ref[slot], source.shape[0]), to : to + b - a],
                    sem.at[len(copies)],
                )
            )
    for c in copies:
        c.start()
    if wide > cols:
        ps[:, :, cols:, :] = jnp.zeros((*ps.shape[:2], wide - cols, 3 * ch), BF)
    for c in copies:
        c.wait()

    bias = vec_ref[BIAS : BIAS + 1, :] + vec_ref[BIAS + 1 : BIAS + 2, :] + vec_ref[BIAS + 2 : BIAS + 3, :]
    first = (meta_ref[0] == 1).astype(F32) * vec_ref[BIAS : BIAS + 1, :]
    last = (meta_ref[1] == 1).astype(F32) * vec_ref[BIAS + 2 : BIAS + 3, :]

    def stage(n):
        for i in range(STEP + 2):
            row = jnp.concatenate([band[s, blocks[n] * STEP + i] for s in range(shards)], axis=0)
            ps[n % 2, i, :cols, ch : 2 * ch] = row
            ps[n % 2, i, :cols, :ch] = jnp.concatenate([row[-1:], row[:-1]], axis=0)
            ps[n % 2, i, :cols, 2 * ch :] = jnp.concatenate([row[1:], row[:1]], axis=0)

    def conv(n):
        p = [ps[n % 2, i] for i in range(STEP + 2)]
        lhs = [jnp.concatenate(p[i : i + 3], axis=1) for i in range(STEP)]
        cs[n % 2] = jnp.dot(jnp.concatenate(lhs, axis=0), ws_ref[...], preferred_element_type=F32)

    def finish(n, i):
        row = blocks[n] * STEP + i
        y = cs[n % 2, i * wide : (i + 1) * wide] + (bias - first if row == 0 else (bias - last if row == rows - 1 else bias))
        mixed = jnp.dot(zs_ref[...], gelu_twice(y).astype(BF), preferred_element_type=F32)
        center = ps[n % 2, i + 1, :, ch : 2 * ch].astype(F32)
        for lead in range(leads):
            lanes = slice(lead * ch, (lead + 1) * ch)
            mod = center * vec_ref[GAIN : GAIN + 1, lanes] + vec_ref[SHIFT : SHIFT + 1, lanes]
            outs[n, lead, i] = (mod + mixed[:, lanes]).astype(BF)[:cols]

    sends = []

    def send(n):
        for lead in range(leads):
            sends.append(
                pltpu.make_async_copy(
                    outs.at[n, lead],
                    out_ref.at[lead, blocks[n] * STEP : (blocks[n] + 1) * STEP],
                    out_sem.at[n, lead],
                )
            )
            sends[-1].start()

    for n in range(len(blocks) + 1):
        if n < len(blocks):
            stage(n)
            conv(n)
        if n:
            for i in range(STEP):
                finish(n - 1, i)
            send(n - 1)
    for c in sends:
        c.wait()


def forecast_heads(meta, sources, moves, ws, vec, zs, so_far, blocks, shape):
    leads, rows, cols, ch = shape
    shards = cols // sources[0].shape[2]
    wide = zs.shape[0]
    vmem = pl.BlockSpec(memory_space=pltpu.VMEM)
    anywhere = pl.BlockSpec(memory_space=pl.ANY)
    operands = [meta, *sources, ws, vec, zs]
    in_specs = [pl.BlockSpec(memory_space=pltpu.SMEM)] + [anywhere] * len(sources) + [vmem] * 3
    alias = {}
    if so_far is not None:
        alias = {len(operands): 0}
        operands.append(so_far)
        in_specs.append(anywhere)
    return pl.pallas_call(
        functools.partial(head_kernel, moves=moves, blocks=blocks, shards=shards, aliased=len(alias)),
        in_specs=in_specs,
        out_specs=anywhere,
        out_shape=jax.ShapeDtypeStruct(shape, BF),
        scratch_shapes=[
            pltpu.VMEM((shards, rows + 2, cols // shards, ch), BF),
            pltpu.VMEM((2, STEP + 2, wide, 3 * ch), BF),
            pltpu.VMEM((2, STEP * wide, leads * ch), F32),
            pltpu.VMEM((len(blocks), leads, STEP, cols, ch), BF),
            pltpu.SemaphoreType.DMA((sum(len(m[1]) for m in moves),)),
            pltpu.SemaphoreType.DMA((len(blocks), leads)),
        ],
        input_output_aliases=alias,
        compiler_params=params(24 * -(-cols // 360)),
        name="heads",
    )(*operands)


def neighbours(size, wrap):
    count = size if wrap else size - 1
    up = [(i, (i + 1) % size) for i in range(count)]
    return up, [(j, i) for i, j in up]


def swap(size, bit):
    return [(i, i ^ bit) for i in range(size)]


def shards(inputs, w_enc, w_proj, film_scale, film_shift, lead_ids, w_head, zonal_mix):
    rows, cols, ch = inputs.shape
    lat, lon = lax.axis_size("lat"), lax.axis_size("lon")
    lat_at, lon_at = lax.axis_index("lat"), lax.axis_index("lon")
    lat_up, lat_dn = neighbours(lat, False)
    lon_up, lon_dn = neighbours(lon, True)
    two_level = lon == 4
    reach = 2 * EDGE - 1
    leads = lead_ids.shape[0] // lon
    head = w_proj.shape[1]
    band_rows = rows // 2

    west = lax.ppermute(inputs[:, -1], "lon", lon_up)
    east = lax.ppermute(inputs[:, 0], "lon", lon_dn)

    mine = lax.dynamic_slice_in_dim(lead_ids, lon_at * leads, leads)
    meta = jnp.stack(
        [lat_at == 0, lat_at == lat - 1, lon_at, lon_at ^ 2, lon_at ^ 1, lon_at ^ 3, 0]
    ).astype(jnp.int32)
    g, ws, vec, zs, up, dn = prepare(
        mine, inputs, west, east, w_enc, w_head, film_scale, film_shift, zonal_mix, reach
    )
    above = lax.ppermute(up, "lat", lat_up)
    below = lax.ppermute(dn, "lat", lat_dn)

    middle = band_rows // 2
    plan = [
        (((2 * EDGE - 1, 2 * middle + 1),), 4),
        (((2 * middle - 1, 2 * (band_rows - EDGE) + 1),), 4),
        (((-3, 2 * EDGE + 1), (rows - 2 * EDGE - 1, rows + 3)), EDGE + 1),
    ]
    none = jnp.zeros((reach, cols + 2, ch), BF)
    proj = []
    for k, (runs, group) in enumerate(plan):
        halos = (above, below) if k == 2 else (none, none)
        proj.append(encode(meta, inputs, west, east, *halos, g, w_proj, runs, group))

    sent = []
    for k, own in enumerate(proj):
        if two_level:
            across = lax.ppermute(own, "lon", swap(lon, 2))
            beside = lax.ppermute(own, "lon", swap(lon, 1))
            both = lax.ppermute(own, "lon", swap(lon, 3)) if k == 2 else lax.ppermute(across, "lon", swap(lon, 1))
            sent.append([(2, own[None]), (3, across[None]), (4, beside[None]), (5, both[None])])
        else:
            sent.append([(6, lax.all_gather(own, "lon", axis=0, tiled=False))])

    def sources(ranges):
        arrays, moves = [], []
        for group, pieces in zip(sent, ranges):
            for slot, a in group if pieces else ():
                arrays.append(a)
                moves.append((slot, pieces))
        return arrays, moves

    shape = (leads, band_rows, cols // 2 * lon, head)
    upper, lower = middle - EDGE, band_rows - EDGE - middle
    blocks = band_rows // STEP
    arrays, moves = sources([[(0, upper, EDGE + 1)], [(0, lower, middle + 1)], []])
    out = forecast_heads(meta, arrays, moves, ws, vec, zs, None, list(range(1, blocks - 1)), shape)
    keep = STEP + 1 - EDGE
    arrays, moves = sources(
        [
            [(0, keep, EDGE + 1)],
            [(lower - keep, lower, band_rows - EDGE + 1 - keep)],
            [(0, EDGE + 1, 0), (EDGE + 1, 2 * EDGE + 2, band_rows + 1 - EDGE)],
        ]
    )
    return forecast_heads(meta, arrays, moves, ws, vec, zs, out, [0, blocks - 1], shape)


def solution(mesh):
    in_specs = (P("lat", "lon", None), P(), P(), P(), P(), P(), P(), P())
    out_specs = P("lon", "lat", None, None)
    return jax.shard_map(shards, mesh=mesh, in_specs=in_specs, out_specs=out_specs, check_vma=False)
```

```python
import functools

import jax
import jax.numpy as jnp
from jax import lax
from jax.experimental import pallas as pl
from jax.experimental.pallas import tpu as pltpu
from jax.sharding import PartitionSpec as P

BF = jnp.bfloat16
F32 = jnp.float32
MIB = 1024 * 1024
EDGE = 2
STEP = 4
BIAS, GAIN, SHIFT = 0, 3, 4


def up_to(n, unit):
    return -(-n // unit) * unit


def gelu_twice(x):
    inner = x * (0.7978845608028654 + 0.035677408136300125 * (x * x))
    return x + x * jnp.tanh(inner)


def params(mib):
    return pltpu.CompilerParams(vmem_limit_bytes=mib * MIB)


def weights_kernel(
    ids_ref, x_ref, west_ref, east_ref, we_hbm, wh_hbm, scale_hbm, shift_hbm, z_hbm,
    g_ref, ws_ref, vec_ref, zs_ref, up_ref, dn_ref,
    edge, flat, we_ref, wh_ref, tab, z_ref, sem,
):
    ch = we_ref.shape[-1]
    head = wh_ref.shape[-1]
    leads = ws_ref.shape[1] // head
    cols = z_ref.shape[0]
    xcols, rows, _ = x_ref.shape
    reach = up_ref.shape[0]
    copies = [
        (x_ref.at[:, :8], edge.at[0]),
        (x_ref.at[:, rows - 8 :], edge.at[1]),
        (we_hbm, we_ref),
        (z_hbm, z_ref),
        (wh_hbm, wh_ref),
    ]
    for lead in range(leads):
        block = pl.multiple_of((ids_ref[lead] // 8) * 8, 8)
        copies.append((scale_hbm.at[pl.ds(block, 8)], tab.at[lead, 0]))
        copies.append((shift_hbm.at[pl.ds(block, 8)], tab.at[lead, 1]))
    copies = [pltpu.make_async_copy(one, two, sem.at[i]) for i, (one, two) in enumerate(copies)]
    for c in copies:
        c.start()
    copies[0].wait()
    copies[1].wait()
    for k, (slab, start, r) in enumerate(((dn_ref, 0, 0), (up_ref, 8 - reach, rows - reach))):
        parts = []
        for j in range(ch // 128):
            lanes = slice(j * 128, (j + 1) * 128)
            flat[k, j] = edge[k, :, :, lanes].astype(F32).reshape(xcols * 8, 128)
            parts.append([flat[k, j, pl.ds(start + i, xcols, stride=8), :] for i in range(reach)])
        for i in range(reach):
            row = jnp.concatenate([p[i] for p in parts], axis=1).astype(BF)
            slab[i] = jnp.concatenate([west_ref[r + i : r + i + 1, :], row, east_ref[r + i : r + i + 1, :]], axis=0)
    copies[2].wait()
    for dr in range(3):
        at = slice(dr * ch, (dr + 1) * ch)
        w = [we_ref[dr, dc].astype(F32) for dc in range(3)]
        half = 0.5 * (w[0] + w[2])
        g_ref[0, at] = we_ref[dr, 0]
        g_ref[1, at] = (half + 0.5 * w[1]).astype(BF)
        g_ref[2, at] = (half - 0.5 * w[1]).astype(BF)
        g_ref[3, at] = we_ref[dr, 2]
    for c in copies[3:]:
        c.wait()
    zs_ref[...] = jnp.zeros(zs_ref.shape, BF)
    zs_ref[:cols, :cols] = z_ref[...] * jnp.asarray(0.5, BF)
    for lead in range(leads):
        lanes = slice(lead * head, (lead + 1) * head)
        at = ids_ref[lead] % 8
        gain = 1.0 + tab[lead, 0, pl.ds(at, 1), :]
        shift = tab[lead, 1, pl.ds(at, 1), :]
        vec_ref[GAIN : GAIN + 1, lanes] = gain
        vec_ref[SHIFT : SHIFT + 1, lanes] = shift
        gain_t = jnp.transpose(jnp.broadcast_to(gain, (head, head)))
        shift_t = jnp.transpose(jnp.broadcast_to(shift, (head, head)))
        for dr in range(3):
            total = jnp.zeros((head, head), F32)
            for dc in range(3):
                at = (dr * 3 + dc) * head
                w = wh_ref[dr, dc].astype(F32)
                ws_ref[at : at + head, lanes] = (w * gain_t).astype(BF)
                total = total + w * shift_t
            vec_ref[BIAS + dr : BIAS + dr + 1, lanes] = jnp.sum(total, axis=0, keepdims=True)


def prepare(ids, x, west, east, w_enc, w_head, scale, shift, z, reach):
    leads = ids.shape[0]
    ch, head, cols = w_enc.shape[-1], w_head.shape[-1], z.shape[0]
    xcols = x.shape[0]
    wide = up_to(cols, 16)
    vmem = pl.BlockSpec(memory_space=pltpu.VMEM)
    anywhere = pl.BlockSpec(memory_space=pl.ANY)
    return pl.pallas_call(
        weights_kernel,
        in_specs=[pl.BlockSpec(memory_space=pltpu.SMEM), anywhere, vmem, vmem] + [anywhere] * 5,
        out_specs=[vmem] * 6,
        out_shape=[
            jax.ShapeDtypeStruct((4, 3 * ch, ch), BF),
            jax.ShapeDtypeStruct((9 * head, leads * head), BF),
            jax.ShapeDtypeStruct((8, leads * head), F32),
            jax.ShapeDtypeStruct((wide, wide), BF),
            jax.ShapeDtypeStruct((reach, xcols + 2, ch), BF),
            jax.ShapeDtypeStruct((reach, xcols + 2, ch), BF),
        ],
        scratch_shapes=[
            pltpu.VMEM((2, xcols, 8, ch), BF),
            pltpu.VMEM((2, ch // 128, xcols * 8, 128), F32),
            pltpu.VMEM(w_enc.shape, BF),
            pltpu.VMEM(w_head.shape, BF),
            pltpu.VMEM((leads, 2, 8, head), F32),
            pltpu.VMEM(z.shape, BF),
            pltpu.SemaphoreType.DMA((5 + 2 * leads,)),
        ],
        compiler_params=params(16),
        name="weights",
    )(ids, x, west, east, w_enc, w_head, scale, shift, z)


def encoder_kernel(
    meta_ref, x_ref, west_ref, east_ref, *refs, first, group
):
    halos, refs = (refs[:2], refs[2:]) if first is None else ((), refs)
    g_ref, wp_ref, out_ref, xs, xr, ys, st, pt, sem = refs[:9]
    cols, rows, ch = x_ref.shape
    reach = 2 * EDGE - 1
    starts = (0, rows - 8) if first is None else ((first - 1) // 8 * 8,)
    tall = xr.shape[2]
    copies = [
        pltpu.make_async_copy(x_ref.at[:, a : a + tall], xr.at[i, 1 : cols + 1], sem.at[i])
        for i, a in enumerate(starts)
    ]
    for c in copies:
        c.start()
    for i, a in enumerate(starts):
        xr[i, 0] = west_ref[a : a + tall, :]
        xr[i, cols + 1] = east_ref[a : a + tall, :]
    block = next(n for n in range(32, 0, -1) if (cols + 2) % n == 0)
    if first is None:
        hf = refs[9]
        for k, halo in enumerate(halos):
            for j in range(ch // 128):
                lanes = slice(j * 128, (j + 1) * 128)
                for i in range(reach):
                    at = 8 - reach + i if k == 0 else i
                    hf[k, j, pl.ds(at, cols + 2, stride=8), :] = halo[i, :, lanes].astype(F32)
    for c in copies:
        c.wait()
    for a in range(0, cols + 2, block):
        at = slice(a, a + block)
        if first is None:
            far = []
            for k in range(2):
                h = [hf[k, j, a * 8 : (a + block) * 8].astype(BF).reshape(block, 8, 128) for j in range(ch // 128)]
                far.append(jnp.concatenate(h, axis=2))
            top = jnp.concatenate([far[0], xr[0, at]], axis=1)
            low = jnp.concatenate([xr[1, at], far[1]], axis=1)
            pad = jnp.zeros((block, 16 - 4 * (EDGE + 1), ch), BF)
            n = 2 * (EDGE + 1)
            for dr in range(3):
                t = top[:, 8 - reach + dr : 8 - reach + dr + n]
                b = low[:, 8 - reach - 2 + dr : 8 - reach - 2 + dr + n]
                xs[at, :, dr * ch : (dr + 1) * ch] = jnp.concatenate([t, b, pad], axis=1)
        else:
            rows_here = xr[0, at]
            for dr in range(3):
                off = first - 1 - starts[0] + dr
                xs[at, :, dr * ch : (dr + 1) * ch] = rows_here[:, off : off + 16]

    pairs = cols // 2

    def multiply(c):
        for k, (i, j) in enumerate(((0, 2), (1, 2), (2, 1), (1, 3))):
            t = []
            for q in range(c * group, (c + 1) * group):
                one, two = xs[2 * q + i], xs[2 * q + j]
                t.append(one + two if k == 1 else one - two)
            ys[c % 2, k] = jnp.dot(jnp.concatenate(t, axis=0), g_ref[k], preferred_element_type=F32)

    def finish(c):
        n = group * 16
        sub = next(v for v in range(12, 0, -1) if group % v == 0) * 16
        for a in range(0, n, sub):
            part = slice(a, a + sub)
            m = [ys.at[c % 2, k, part] for k in range(4)]
            both = gelu_twice(m[0][...] + m[1][...] + m[2][...])
            both = both + gelu_twice(m[1][...] - m[2][...] - m[3][...])
            for j in range(ch // 128):
                st[j, part] = both[:, j * 128 : (j + 1) * 128]
        pooled = [
            st[j, pl.ds(0, n // 2, stride=2), :] + st[j, pl.ds(1, n // 2, stride=2), :] for j in range(ch // 128)
        ]
        pooled = (jnp.concatenate(pooled, axis=1) * 0.125).astype(BF)
        pt[c * (n // 2) : (c + 1) * (n // 2)] = jnp.dot(pooled, wp_ref[...], preferred_element_type=F32)

    for c in range(pairs // group):
        multiply(c)
        if c:
            finish(c - 1)
    finish(pairs // group - 1)
    count = out_ref.shape[0]
    for r in range(count):
        row = pt[pl.ds(r, pairs, stride=8), :]
        if first is None and r in (0, count - 1):
            row = jnp.where(meta_ref[0 if r == 0 else 1] == 0, row, 0.0)
        out_ref[r] = row.astype(BF)


def encode(meta, x, west, east, halos, g, wp, first, count, group):
    cols, rows, ch = x.shape
    head = wp.shape[1]
    blocks = 1 if halos is None else 2
    tall = 24 if halos is None else 8
    vmem = pl.BlockSpec(memory_space=pltpu.VMEM)
    scratch = [
        pltpu.VMEM((cols + 2, 16, 3 * ch), BF),
        pltpu.VMEM((blocks, cols + 2, tall, ch), BF),
        pltpu.VMEM((2, 4, group * 16, ch), F32),
        pltpu.VMEM((ch // 128, group * 16, 128), F32),
        pltpu.VMEM((cols // 2 * 8, head), F32),
        pltpu.SemaphoreType.DMA((blocks,)),
    ]
    if halos is not None:
        scratch.append(pltpu.VMEM((2, ch // 128, (cols + 2) * 8, 128), F32))
    operands = [meta, x, west, east, *(halos or ()), g, wp]
    flops = 2 * cols * 16 * 6 * ch * ch
    return pl.pallas_call(
        functools.partial(encoder_kernel, first=first, group=group),
        in_specs=[pl.BlockSpec(memory_space=pltpu.SMEM), pl.BlockSpec(memory_space=pl.ANY)]
        + [vmem] * (len(operands) - 2),
        out_specs=vmem,
        out_shape=jax.ShapeDtypeStruct((count, cols // 2, head), BF),
        scratch_shapes=scratch,
        compiler_params=params(28),
        cost_estimate=pl.CostEstimate(flops=flops, transcendentals=cols * 16 * ch, bytes_accessed=8 * 1024 * 1024),
        name="encode",
    )(*operands)


def head_kernel(meta_ref, *refs, moves, blocks, shards, aliased):
    sources = refs[: len(moves)]
    ws_ref, vec_ref, zs_ref = refs[len(moves) : len(moves) + 3]
    out_ref, band, ps, cs, outs, sem, out_sem = refs[len(moves) + 3 + aliased :]
    ch = ps.shape[3] // 3
    wide = ps.shape[2]
    leads, rows, cols, _ = out_ref.shape

    copies = []
    for source, (slot, pieces) in zip(sources, moves):
        for a, b, to in pieces:
            copies.append(
                pltpu.make_async_copy(
                    source.at[:, a:b],
                    band.at[pl.ds(meta_ref[slot], source.shape[0]), to : to + b - a],
                    sem.at[len(copies)],
                )
            )
    for c in copies:
        c.start()
    if wide > cols:
        ps[:, :, cols:, :] = jnp.zeros((*ps.shape[:2], wide - cols, 3 * ch), BF)
    for c in copies:
        c.wait()

    bias = vec_ref[BIAS : BIAS + 1, :] + vec_ref[BIAS + 1 : BIAS + 2, :] + vec_ref[BIAS + 2 : BIAS + 3, :]
    first = (meta_ref[0] == 1).astype(F32) * vec_ref[BIAS : BIAS + 1, :]
    last = (meta_ref[1] == 1).astype(F32) * vec_ref[BIAS + 2 : BIAS + 3, :]

    def stage(n):
        for i in range(STEP + 2):
            row = jnp.concatenate([band[s, blocks[n] * STEP + i] for s in range(shards)], axis=0)
            ps[n % 2, i, :cols, ch : 2 * ch] = row
            ps[n % 2, i, :cols, :ch] = jnp.concatenate([row[-1:], row[:-1]], axis=0)
            ps[n % 2, i, :cols, 2 * ch :] = jnp.concatenate([row[1:], row[:1]], axis=0)

    def conv(n):
        p = [ps[n % 2, i] for i in range(STEP + 2)]
        lhs = [jnp.concatenate(p[i : i + 3], axis=1) for i in range(STEP)]
        cs[n % 2] = jnp.dot(jnp.concatenate(lhs, axis=0), ws_ref[...], preferred_element_type=F32)

    def finish(n, i):
        row = blocks[n] * STEP + i
        y = cs[n % 2, i * wide : (i + 1) * wide] + (bias - first if row == 0 else (bias - last if row == rows - 1 else bias))
        mixed = jnp.dot(zs_ref[...], gelu_twice(y).astype(BF), preferred_element_type=F32)
        center = ps[n % 2, i + 1, :, ch : 2 * ch].astype(F32)
        for lead in range(leads):
            lanes = slice(lead * ch, (lead + 1) * ch)
            mod = center * vec_ref[GAIN : GAIN + 1, lanes] + vec_ref[SHIFT : SHIFT + 1, lanes]
            outs[n, lead, i] = (mod + mixed[:, lanes]).astype(BF)[:cols]

    sends = []

    def send(n):
        for lead in range(leads):
            sends.append(
                pltpu.make_async_copy(
                    outs.at[n, lead],
                    out_ref.at[lead, blocks[n] * STEP : (blocks[n] + 1) * STEP],
                    out_sem.at[n, lead],
                )
            )
            sends[-1].start()

    for n in range(len(blocks) + 1):
        if n < len(blocks):
            stage(n)
            conv(n)
        if n:
            for i in range(STEP):
                finish(n - 1, i)
            send(n - 1)
    for c in sends:
        c.wait()


def forecast_heads(meta, sources, moves, ws, vec, zs, so_far, blocks, shape):
    leads, rows, cols, ch = shape
    shards = cols // sources[0].shape[2]
    wide = zs.shape[0]
    vmem = pl.BlockSpec(memory_space=pltpu.VMEM)
    anywhere = pl.BlockSpec(memory_space=pl.ANY)
    operands = [meta, *sources, ws, vec, zs]
    in_specs = [pl.BlockSpec(memory_space=pltpu.SMEM)] + [anywhere] * len(sources) + [vmem] * 3
    alias = {}
    if so_far is not None:
        alias = {len(operands): 0}
        operands.append(so_far)
        in_specs.append(anywhere)
    return pl.pallas_call(
        functools.partial(head_kernel, moves=moves, blocks=blocks, shards=shards, aliased=len(alias)),
        in_specs=in_specs,
        out_specs=anywhere,
        out_shape=jax.ShapeDtypeStruct(shape, BF),
        scratch_shapes=[
            pltpu.VMEM((shards, rows + 2, cols // shards, ch), BF),
            pltpu.VMEM((2, STEP + 2, wide, 3 * ch), BF),
            pltpu.VMEM((2, STEP * wide, leads * ch), F32),
            pltpu.VMEM((len(blocks), leads, STEP, cols, ch), BF),
            pltpu.SemaphoreType.DMA((sum(len(m[1]) for m in moves),)),
            pltpu.SemaphoreType.DMA((len(blocks), leads)),
        ],
        input_output_aliases=alias,
        compiler_params=params(24 * -(-cols // 360)),
        cost_estimate=pl.CostEstimate(
            flops=len(blocks) * STEP * cols * leads * ch * 2 * (9 * ch + cols),
            transcendentals=len(blocks) * STEP * cols * leads * ch,
            bytes_accessed=len(blocks) * 8 * 1024 * 1024,
        ),
        name="heads",
    )(*operands)


def neighbours(size, wrap):
    count = size if wrap else size - 1
    up = [(i, (i + 1) % size) for i in range(count)]
    return up, [(j, i) for i, j in up]


def swap(size, bit):
    return [(i, i ^ bit) for i in range(size)]


def shards(inputs, w_enc, w_proj, film_scale, film_shift, lead_ids, w_head, zonal_mix):
    rows, cols, ch = inputs.shape
    tile = jnp.transpose(inputs, (1, 0, 2))
    lat, lon = lax.axis_size("lat"), lax.axis_size("lon")
    lat_at, lon_at = lax.axis_index("lat"), lax.axis_index("lon")
    lat_up, lat_dn = neighbours(lat, False)
    lon_up, lon_dn = neighbours(lon, True)
    two_level = lon == 4
    reach = 2 * EDGE - 1
    leads = lead_ids.shape[0] // lon
    head = w_proj.shape[1]
    band_rows = rows // 2

    west = lax.ppermute(tile[-1], "lon", lon_up)
    east = lax.ppermute(tile[0], "lon", lon_dn)

    mine = lax.dynamic_slice_in_dim(lead_ids, lon_at * leads, leads)
    meta = jnp.stack(
        [lat_at == 0, lat_at == lat - 1, lon_at, lon_at ^ 2, lon_at ^ 1, lon_at ^ 3, 0]
    ).astype(jnp.int32)
    g, ws, vec, zs, up, dn = prepare(
        mine, tile, west, east, w_enc, w_head, film_scale, film_shift, zonal_mix, reach
    )
    above = lax.ppermute(up, "lat", lat_up)
    below = lax.ppermute(dn, "lat", lat_dn)

    middle = band_rows // 2
    group = cols // 4
    plan = [
        (2 * EDGE, middle - EDGE, None),
        (2 * middle, band_rows - EDGE - middle, None),
        (None, 2 * (EDGE + 1), (above, below)),
    ]
    proj = [encode(meta, tile, west, east, halos, g, w_proj, first, n, group) for first, n, halos in plan]

    sent = []
    for k, own in enumerate(proj):
        if two_level:
            across = lax.ppermute(own, "lon", swap(lon, 2))
            beside = lax.ppermute(own, "lon", swap(lon, 1))
            if k == 2:
                both = lax.ppermute(own, "lon", swap(lon, 3))
            else:
                ready, _ = lax.optimization_barrier((across, proj[k + 1]))
                both = lax.ppermute(ready, "lon", swap(lon, 1))
            sent.append([(2, own[None]), (3, across[None]), (4, beside[None]), (5, both[None])])
        else:
            sent.append([(6, lax.all_gather(own, "lon", axis=0, tiled=False))])

    def sources(ranges):
        arrays, moves = [], []
        for group, pieces in zip(sent, ranges):
            for slot, a in group if pieces else ():
                arrays.append(a)
                moves.append((slot, pieces))
        return arrays, moves

    shape = (leads, band_rows, cols // 2 * lon, head)
    upper, lower = middle - EDGE, band_rows - EDGE - middle
    blocks = band_rows // STEP
    arrays, moves = sources([[(0, upper, EDGE + 1)], [(0, lower, middle + 1)], []])
    out = forecast_heads(meta, arrays, moves, ws, vec, zs, None, list(range(1, blocks - 1)), shape)
    keep = STEP + 1 - EDGE
    arrays, moves = sources(
        [
            [(0, keep, EDGE + 1)],
            [(lower - keep, lower, band_rows - EDGE + 1 - keep)],
            [(0, EDGE + 1, 0), (EDGE + 1, 2 * EDGE + 2, band_rows + 1 - EDGE)],
        ]
    )
    return forecast_heads(meta, arrays, moves, ws, vec, zs, out, [0, blocks - 1], shape)


def solution(mesh):
    in_specs = (P("lat", "lon", None), P(), P(), P(), P(), P(), P(), P())
    out_specs = P("lon", "lat", None, None)
    return jax.shard_map(shards, mesh=mesh, in_specs=in_specs, out_specs=out_specs, check_vma=False)
```

```python
import functools

import jax
import jax.numpy as jnp
from jax import lax
from jax.experimental import pallas as pl
from jax.experimental.pallas import tpu as pltpu
from jax.sharding import PartitionSpec as P

BF = jnp.bfloat16
F32 = jnp.float32
MIB = 1024 * 1024
EDGE = 2
STEP = 4
BIAS, GAIN, SHIFT = 0, 3, 4


def up_to(n, unit):
    return -(-n // unit) * unit


def gelu_twice(x):
    inner = x * (0.7978845608028654 + 0.035677408136300125 * (x * x))
    return x + x * jnp.tanh(inner)


def params(mib):
    return pltpu.CompilerParams(vmem_limit_bytes=mib * MIB)


def weights_kernel(
    meta_ref, ids_ref, we_hbm, wh_hbm, scale_hbm, shift_hbm, z_hbm,
    g_ref, ws_ref, vec_ref, zs_ref,
    we_ref, wh_ref, tab, z_ref, sem,
):
    ch = we_ref.shape[-1]
    head = wh_ref.shape[-1]
    leads = ws_ref.shape[1] // head
    cols = z_ref.shape[0]
    ids = [ids_ref[meta_ref[2] * leads + lead] for lead in range(leads)]
    copies = [(we_hbm, we_ref), (z_hbm, z_ref), (wh_hbm, wh_ref)]
    for lead in range(leads):
        block = pl.multiple_of((ids[lead] // 8) * 8, 8)
        copies.append((scale_hbm.at[pl.ds(block, 8)], tab.at[lead, 0]))
        copies.append((shift_hbm.at[pl.ds(block, 8)], tab.at[lead, 1]))
    copies = [pltpu.make_async_copy(one, two, sem.at[i]) for i, (one, two) in enumerate(copies)]
    for c in copies:
        c.start()
    zs_ref[...] = jnp.zeros(zs_ref.shape, BF)
    copies[0].wait()
    for dr in range(3):
        at = slice(dr * ch, (dr + 1) * ch)
        w = [we_ref[dr, dc].astype(F32) for dc in range(3)]
        half = 0.5 * (w[0] + w[2])
        g_ref[0, at] = we_ref[dr, 0]
        g_ref[1, at] = (half + 0.5 * w[1]).astype(BF)
        g_ref[2, at] = (half - 0.5 * w[1]).astype(BF)
        g_ref[3, at] = we_ref[dr, 2]
    for c in copies[1:]:
        c.wait()
    zs_ref[:cols, :cols] = z_ref[...] * jnp.asarray(0.5, BF)
    for lead in range(leads):
        lanes = slice(lead * head, (lead + 1) * head)
        at = ids[lead] % 8
        gain = 1.0 + tab[lead, 0, pl.ds(at, 1), :]
        shift = tab[lead, 1, pl.ds(at, 1), :]
        vec_ref[GAIN : GAIN + 1, lanes] = gain
        vec_ref[SHIFT : SHIFT + 1, lanes] = shift
        gain_t = jnp.transpose(jnp.broadcast_to(gain, (head, head)))
        shift_t = jnp.transpose(jnp.broadcast_to(shift, (head, head)))
        for dr in range(3):
            total = jnp.zeros((head, head), F32)
            for dc in range(3):
                at = (dr * 3 + dc) * head
                w = wh_ref[dr, dc].astype(F32)
                ws_ref[at : at + head, lanes] = (w * gain_t).astype(BF)
                total = total + w * shift_t
            vec_ref[BIAS + dr : BIAS + dr + 1, lanes] = jnp.sum(total, axis=0, keepdims=True)


def prepare(meta, ids, w_enc, w_head, scale, shift, z, leads):
    ch, head, cols = w_enc.shape[-1], w_head.shape[-1], z.shape[0]
    wide = up_to(cols, 16)
    vmem = pl.BlockSpec(memory_space=pltpu.VMEM)
    smem = pl.BlockSpec(memory_space=pltpu.SMEM)
    hbm = pl.BlockSpec(memory_space=pltpu.HBM)
    return pl.pallas_call(
        weights_kernel,
        in_specs=[smem, smem] + [hbm] * 5,
        out_specs=[vmem] * 4,
        out_shape=[
            jax.ShapeDtypeStruct((4, 3 * ch, ch), BF),
            jax.ShapeDtypeStruct((9 * head, leads * head), BF),
            jax.ShapeDtypeStruct((8, leads * head), F32),
            jax.ShapeDtypeStruct((wide, wide), BF),
        ],
        scratch_shapes=[
            pltpu.VMEM(w_enc.shape, BF),
            pltpu.VMEM(w_head.shape, BF),
            pltpu.VMEM((leads, 2, 8, head), F32),
            pltpu.VMEM(z.shape, BF),
            pltpu.SemaphoreType.DMA((3 + 2 * leads,)),
        ],
        compiler_params=params(58),
        name="weights",
    )(meta, ids, w_enc, w_head, scale, shift, z)


def slabs_kernel(x_ref, west_ref, east_ref, up_ref, dn_ref, edge, flat, sem):
    xcols, rows, ch = x_ref.shape
    reach = up_ref.shape[0]
    copies = [
        pltpu.make_async_copy(x_ref.at[:, a : a + 8], edge.at[k], sem.at[k]) for k, a in enumerate((0, rows - 8))
    ]
    for c in copies:
        c.start()
    for k, (slab, start, r) in enumerate(((dn_ref, 0, 0), (up_ref, 8 - reach, rows - reach))):
        copies[k].wait()
        parts = []
        for j in range(ch // 128):
            lanes = slice(j * 128, (j + 1) * 128)
            flat[k, j] = edge[k, :, :, lanes].astype(F32).reshape(xcols * 8, 128)
            parts.append([flat[k, j, pl.ds(start + i, xcols, stride=8), :] for i in range(reach)])
        for i in range(reach):
            row = jnp.concatenate([p[i] for p in parts], axis=1).astype(BF)
            slab[i] = jnp.concatenate([west_ref[r + i : r + i + 1, :], row, east_ref[r + i : r + i + 1, :]], axis=0)


def row_slabs(x, west, east, reach):
    xcols, _, ch = x.shape
    vmem = pl.BlockSpec(memory_space=pltpu.VMEM)
    return pl.pallas_call(
        slabs_kernel,
        in_specs=[pl.BlockSpec(memory_space=pltpu.HBM), vmem, vmem],
        out_specs=[vmem] * 2,
        out_shape=[jax.ShapeDtypeStruct((reach, xcols + 2, ch), BF)] * 2,
        scratch_shapes=[
            pltpu.VMEM((2, xcols, 8, ch), BF),
            pltpu.VMEM((2, ch // 128, xcols * 8, 128), F32),
            pltpu.SemaphoreType.DMA((2,)),
        ],
        compiler_params=params(48),
        name="slabs",
    )(x, west, east)


def encoder_kernel(
    meta_ref, x_ref, west_ref, east_ref, *refs, first, group
):
    halos, refs = (refs[:2], refs[2:]) if first is None else ((), refs)
    g_ref, wp_ref, out_ref, xs, xr, ys, st, pt, sem = refs[:9]
    cols, rows, ch = x_ref.shape
    reach = 2 * EDGE - 1
    starts = (0, rows - 8) if first is None else ((first - 1) // 8 * 8,)
    tall = xr.shape[2]
    block = next(n for n in range(32, 0, -1) if (cols + 2) % n == 0)
    copies = []
    for p in range(0, cols, block):
        to = min(p + block, cols)
        for i, a in enumerate(starts):
            copies.append(
                pltpu.make_async_copy(
                    x_ref.at[p:to, a : a + tall], xr.at[i, p + 1 : to + 1], sem.at[i, p // block]
                )
            )
            copies[-1].start()
    for i, a in enumerate(starts):
        xr[i, 0] = west_ref[a : a + tall, :]
        xr[i, cols + 1] = east_ref[a : a + tall, :]
    if first is None:
        hf = refs[9]
        for k, halo in enumerate(halos):
            for j in range(ch // 128):
                lanes = slice(j * 128, (j + 1) * 128)
                for i in range(reach):
                    at = 8 - reach + i if k == 0 else i
                    hf[k, j, pl.ds(at, cols + 2, stride=8), :] = halo[i, :, lanes].astype(F32)
    for a in range(0, cols + 2, block):
        at = slice(a, a + block)
        for c in copies[: len(starts)]:
            c.wait()
        copies = copies[len(starts) :]
        if first is None:
            far = []
            for k in range(2):
                h = [hf[k, j, a * 8 : (a + block) * 8].astype(BF).reshape(block, 8, 128) for j in range(ch // 128)]
                far.append(jnp.concatenate(h, axis=2))
            top = jnp.concatenate([far[0], xr[0, at]], axis=1)
            low = jnp.concatenate([xr[1, at], far[1]], axis=1)
            pad = jnp.zeros((block, 16 - 4 * (EDGE + 1), ch), BF)
            n = 2 * (EDGE + 1)
            for dr in range(3):
                t = top[:, 8 - reach + dr : 8 - reach + dr + n]
                b = low[:, 8 - reach - 2 + dr : 8 - reach - 2 + dr + n]
                xs[at, :, dr * ch : (dr + 1) * ch] = jnp.concatenate([t, b, pad], axis=1)
        else:
            rows_here = xr[0, at]
            for dr in range(3):
                off = first - 1 - starts[0] + dr
                xs[at, :, dr * ch : (dr + 1) * ch] = rows_here[:, off : off + 16]

    pairs = cols // 2

    def multiply(c):
        for k, (i, j) in enumerate(((0, 2), (1, 2), (2, 1), (1, 3))):
            t = []
            for q in range(c * group, (c + 1) * group):
                one, two = xs[2 * q + i], xs[2 * q + j]
                t.append(one + two if k == 1 else one - two)
            ys[c % 2, k] = jnp.dot(jnp.concatenate(t, axis=0), g_ref[k], preferred_element_type=F32)

    def finish(c):
        n = group * 16
        sub = next(v for v in range(12, 0, -1) if group % v == 0) * 16
        for a in range(0, n, sub):
            part = slice(a, a + sub)
            m = [ys.at[c % 2, k, part] for k in range(4)]
            both = gelu_twice(m[0][...] + m[1][...] + m[2][...])
            both = both + gelu_twice(m[1][...] - m[2][...] - m[3][...])
            for j in range(ch // 128):
                st[j, part] = both[:, j * 128 : (j + 1) * 128]
        pooled = [
            st[j, pl.ds(0, n // 2, stride=2), :] + st[j, pl.ds(1, n // 2, stride=2), :] for j in range(ch // 128)
        ]
        pooled = (jnp.concatenate(pooled, axis=1) * 0.125).astype(BF)
        pt[c * (n // 2) : (c + 1) * (n // 2)] = jnp.dot(pooled, wp_ref[...], preferred_element_type=F32)

    for c in range(pairs // group):
        multiply(c)
        if c:
            finish(c - 1)
    finish(pairs // group - 1)
    count = out_ref.shape[0]
    for r in range(count):
        row = pt[pl.ds(r, pairs, stride=8), :]
        if first is None and r in (0, count - 1):
            row = jnp.where(meta_ref[0 if r == 0 else 1] == 0, row, 0.0)
        out_ref[r] = row.astype(BF)


def encode(meta, x, west, east, halos, g, wp, first, count, group):
    cols, rows, ch = x.shape
    head = wp.shape[1]
    blocks = 1 if halos is None else 2
    tall = 24 if halos is None else 8
    vmem = pl.BlockSpec(memory_space=pltpu.VMEM)
    scratch = [
        pltpu.VMEM((cols + 2, 16, 3 * ch), BF),
        pltpu.VMEM((blocks, cols + 2, tall, ch), BF),
        pltpu.VMEM((2, 4, group * 16, ch), F32),
        pltpu.VMEM((ch // 128, group * 16, 128), F32),
        pltpu.VMEM((cols // 2 * 8, head), F32),
        pltpu.SemaphoreType.DMA((blocks, cols)),
    ]
    if halos is not None:
        scratch.append(pltpu.VMEM((2, ch // 128, (cols + 2) * 8, 128), F32))
    operands = [meta, x, west, east, *(halos or ()), g, wp]
    flops = 2 * cols * 16 * 6 * ch * ch
    return pl.pallas_call(
        functools.partial(encoder_kernel, first=first, group=group),
        in_specs=[pl.BlockSpec(memory_space=pltpu.SMEM), pl.BlockSpec(memory_space=pltpu.HBM)]
        + [vmem] * (len(operands) - 2),
        out_specs=vmem,
        out_shape=jax.ShapeDtypeStruct((count, cols // 2, head), BF),
        scratch_shapes=scratch,
        compiler_params=params(28),
        cost_estimate=pl.CostEstimate(flops=flops, transcendentals=cols * 16 * ch, bytes_accessed=8 * 1024 * 1024),
        name="encode",
    )(*operands)


def head_kernel(meta_ref, *refs, moves, blocks, shards, aliased):
    sources = refs[: len(moves)]
    ws_ref, vec_ref, zs_ref = refs[len(moves) : len(moves) + 3]
    out_ref, band, ps, cs, outs, sem, out_sem = refs[len(moves) + 3 + aliased :]
    ch = ps.shape[2] // 3
    wide = ps.shape[1]
    leads, rows, cols, _ = out_ref.shape

    copies = []
    for source, (slot, pieces) in zip(sources, moves):
        for a, b, to in pieces:
            copies.append(
                pltpu.make_async_copy(
                    source.at[:, a:b],
                    band.at[pl.ds(meta_ref[slot], source.shape[0]), to : to + b - a],
                    sem.at[len(copies)],
                )
            )
    for c in copies:
        c.start()
    if wide > cols:
        ps[:, cols:, :] = jnp.zeros((ps.shape[0], wide - cols, 3 * ch), BF)
    for c in copies:
        c.wait()

    bias = vec_ref[BIAS : BIAS + 1, :] + vec_ref[BIAS + 1 : BIAS + 2, :] + vec_ref[BIAS + 2 : BIAS + 3, :]
    first = (meta_ref[0] == 1).astype(F32) * vec_ref[BIAS : BIAS + 1, :]
    last = (meta_ref[1] == 1).astype(F32) * vec_ref[BIAS + 2 : BIAS + 3, :]

    wanted = [sorted({n * STEP + i for i in range(STEP + 2)}) for n in blocks]
    slots = {r: k for k, r in enumerate(sorted(set(sum(wanted, []))))}
    staged = set()

    def stage(n):
        for r in wanted[n]:
            if r in staged:
                continue
            staged.add(r)
            k = slots[r]
            row = jnp.concatenate([band[s, r] for s in range(shards)], axis=0)
            ps[k, :cols, ch : 2 * ch] = row
            ps[k, :cols, :ch] = jnp.concatenate([row[-1:], row[:-1]], axis=0)
            ps[k, :cols, 2 * ch :] = jnp.concatenate([row[1:], row[:1]], axis=0)

    def conv(n):
        p = [ps[slots[r]] for r in wanted[n]]
        lhs = [jnp.concatenate(p[i : i + 3], axis=1) for i in range(STEP)]
        cs[n % 2] = jnp.dot(jnp.concatenate(lhs, axis=0), ws_ref[...], preferred_element_type=F32)

    def finish(n, i):
        row = blocks[n] * STEP + i
        y = cs[n % 2, i * wide : (i + 1) * wide] + (bias - first if row == 0 else (bias - last if row == rows - 1 else bias))
        mixed = jnp.dot(zs_ref[...], gelu_twice(y).astype(BF), preferred_element_type=F32)
        center = ps[slots[row + 1], :, ch : 2 * ch].astype(F32)
        for lead in range(leads):
            lanes = slice(lead * ch, (lead + 1) * ch)
            mod = center * vec_ref[GAIN : GAIN + 1, lanes] + vec_ref[SHIFT : SHIFT + 1, lanes]
            outs[n, lead, i] = (mod + mixed[:, lanes]).astype(BF)[:cols]

    sends = []

    def send(n):
        for lead in range(leads):
            sends.append(
                pltpu.make_async_copy(
                    outs.at[n, lead],
                    out_ref.at[lead, blocks[n] * STEP : (blocks[n] + 1) * STEP],
                    out_sem.at[n, lead],
                )
            )
            sends[-1].start()

    for n in range(len(blocks) + 1):
        if n < len(blocks):
            stage(n)
            conv(n)
        if n:
            for i in range(STEP):
                finish(n - 1, i)
            send(n - 1)
    for c in sends:
        c.wait()


def forecast_heads(meta, sources, moves, ws, vec, zs, so_far, blocks, shape):
    leads, rows, cols, ch = shape
    shards = cols // sources[0].shape[2]
    wide = zs.shape[0]
    vmem = pl.BlockSpec(memory_space=pltpu.VMEM)
    anywhere = pl.BlockSpec(memory_space=pl.ANY)
    staged = len({n * STEP + i for n in blocks for i in range(STEP + 2)})
    operands = [meta, *sources, ws, vec, zs]
    in_specs = [pl.BlockSpec(memory_space=pltpu.SMEM)] + [anywhere] * len(sources) + [vmem] * 3
    alias = {}
    if so_far is not None:
        alias = {len(operands): 0}
        operands.append(so_far)
        in_specs.append(pl.BlockSpec(memory_space=pltpu.HBM))
    return pl.pallas_call(
        functools.partial(head_kernel, moves=moves, blocks=blocks, shards=shards, aliased=len(alias)),
        in_specs=in_specs,
        out_specs=pl.BlockSpec(memory_space=pltpu.HBM),
        out_shape=jax.ShapeDtypeStruct(shape, BF),
        scratch_shapes=[
            pltpu.VMEM((shards, rows + 2, cols // shards, ch), BF),
            pltpu.VMEM((staged, wide, 3 * ch), BF),
            pltpu.VMEM((2, STEP * wide, leads * ch), F32),
            pltpu.VMEM((len(blocks), leads, STEP, cols, ch), BF),
            pltpu.SemaphoreType.DMA((sum(len(m[1]) for m in moves),)),
            pltpu.SemaphoreType.DMA((len(blocks), leads)),
        ],
        input_output_aliases=alias,
        compiler_params=params(24 * -(-cols // 360)),
        cost_estimate=pl.CostEstimate(
            flops=len(blocks) * STEP * cols * leads * ch * 2 * (9 * ch + cols),
            transcendentals=len(blocks) * STEP * cols * leads * ch,
            bytes_accessed=len(blocks) * 8 * 1024 * 1024,
        ),
        name="heads",
    )(*operands)


def neighbours(size, wrap):
    count = size if wrap else size - 1
    up = [(i, (i + 1) % size) for i in range(count)]
    return up, [(j, i) for i, j in up]


def swap(size, bit):
    return [(i, i ^ bit) for i in range(size)]


def shards(inputs, w_enc, w_proj, film_scale, film_shift, lead_ids, w_head, zonal_mix):
    rows, cols, ch = inputs.shape
    tile = jnp.transpose(inputs, (1, 0, 2))
    lat, lon = lax.axis_size("lat"), lax.axis_size("lon")
    lat_at, lon_at = lax.axis_index("lat"), lax.axis_index("lon")
    lat_up, lat_dn = neighbours(lat, False)
    lon_up, lon_dn = neighbours(lon, True)
    two_level = lon == 4
    reach = 2 * EDGE - 1
    leads = lead_ids.shape[0] // lon
    head = w_proj.shape[1]
    band_rows = rows // 2

    west = lax.ppermute(tile[-1], "lon", lon_up)
    east = lax.ppermute(tile[0], "lon", lon_dn)

    meta = jnp.stack(
        [lat_at == 0, lat_at == lat - 1, lon_at, lon_at ^ 2, lon_at ^ 1, lon_at ^ 3, 0]
    ).astype(jnp.int32)
    g, ws, vec, zs = prepare(meta, lead_ids, w_enc, w_head, film_scale, film_shift, zonal_mix, leads)
    up, dn = row_slabs(tile, west, east, reach)
    above = lax.ppermute(up, "lat", lat_up)
    below = lax.ppermute(dn, "lat", lat_dn)

    middle = band_rows // 2
    group = cols // 4
    plan = [
        (2 * EDGE, middle - EDGE, None),
        (2 * middle, band_rows - EDGE - middle, None),
        (None, 2 * (EDGE + 1), (above, below)),
    ]
    proj = [encode(meta, tile, west, east, halos, g, w_proj, first, n, group) for first, n, halos in plan]

    sent = []
    for k, own in enumerate(proj):
        if two_level:
            across = lax.ppermute(own, "lon", swap(lon, 2))
            beside = lax.ppermute(own, "lon", swap(lon, 1))
            if k == 2:
                both = lax.ppermute(own, "lon", swap(lon, 3))
            else:
                ready, _ = lax.optimization_barrier((across, proj[2]))
                both = lax.ppermute(ready, "lon", swap(lon, 1))
            sent.append([(2, own[None]), (3, across[None]), (4, beside[None]), (5, both[None])])
        else:
            sent.append([(6, lax.all_gather(own, "lon", axis=0, tiled=False))])

    def sources(ranges):
        arrays, moves = [], []
        for group, pieces in zip(sent, ranges):
            for slot, a in group if pieces else ():
                arrays.append(a)
                moves.append((slot, pieces))
        return arrays, moves

    shape = (leads, band_rows, cols // 2 * lon, head)
    upper, lower = middle - EDGE, band_rows - EDGE - middle
    blocks = band_rows // STEP
    arrays, moves = sources([[(0, upper, EDGE + 1)], [(0, lower, middle + 1)], []])
    out = forecast_heads(meta, arrays, moves, ws, vec, zs, None, list(range(1, blocks - 1)), shape)
    keep = STEP + 1 - EDGE
    arrays, moves = sources(
        [
            [(0, keep, EDGE + 1)],
            [(lower - keep, lower, band_rows - EDGE + 1 - keep)],
            [(0, EDGE + 1, 0), (EDGE + 1, 2 * EDGE + 2, band_rows + 1 - EDGE)],
        ]
    )
    return forecast_heads(meta, arrays, moves, ws, vec, zs, out, [0, blocks - 1], shape)


def solution(mesh):
    in_specs = (P("lat", "lon", None), P(), P(), P(), P(), P(), P(), P())
    out_specs = P("lon", "lat", None, None)
    return jax.shard_map(shards, mesh=mesh, in_specs=in_specs, out_specs=out_specs, check_vma=False)
```

```python
import functools

import jax
import jax.numpy as jnp
from jax import lax
from jax.experimental import pallas as pl
from jax.experimental.pallas import tpu as pltpu
from jax.sharding import PartitionSpec as P

BF = jnp.bfloat16
F32 = jnp.float32
MIB = 1024 * 1024
EDGE = 2
STEP = 4
BIAS, GAIN, SHIFT = 0, 3, 4


def up_to(n, unit):
    return -(-n // unit) * unit


def gelu_twice(x):
    inner = x * (0.7978845608028654 + 0.035677408136300125 * (x * x))
    return x + x * jnp.tanh(inner)


def params(mib):
    return pltpu.CompilerParams(vmem_limit_bytes=mib * MIB)


def weights_kernel(
    meta_ref, ids_ref, we_hbm, wh_hbm, scale_hbm, shift_hbm, z_hbm,
    g_ref, ws_ref, vec_ref, zs_ref,
    we_ref, wh_ref, tab, z_ref, sem,
):
    ch = we_ref.shape[-1]
    head = wh_ref.shape[-1]
    leads = ws_ref.shape[1] // head
    cols = z_ref.shape[0]
    ids = [ids_ref[meta_ref[2] * leads + lead] for lead in range(leads)]
    copies = [(we_hbm, we_ref), (z_hbm, z_ref), (wh_hbm, wh_ref)]
    for lead in range(leads):
        block = pl.multiple_of((ids[lead] // 8) * 8, 8)
        copies.append((scale_hbm.at[pl.ds(block, 8)], tab.at[lead, 0]))
        copies.append((shift_hbm.at[pl.ds(block, 8)], tab.at[lead, 1]))
    copies = [pltpu.make_async_copy(one, two, sem.at[i]) for i, (one, two) in enumerate(copies)]
    for c in copies:
        c.start()
    zs_ref[...] = jnp.zeros(zs_ref.shape, BF)
    copies[0].wait()
    for dr in range(3):
        at = slice(dr * ch, (dr + 1) * ch)
        w = [we_ref[dr, dc].astype(F32) for dc in range(3)]
        half = 0.5 * (w[0] + w[2])
        g_ref[0, at] = we_ref[dr, 0]
        g_ref[1, at] = (half + 0.5 * w[1]).astype(BF)
        g_ref[2, at] = (half - 0.5 * w[1]).astype(BF)
        g_ref[3, at] = we_ref[dr, 2]
    for c in copies[1:]:
        c.wait()
    zs_ref[:cols, :cols] = z_ref[...] * jnp.asarray(0.5, BF)
    for lead in range(leads):
        lanes = slice(lead * head, (lead + 1) * head)
        at = ids[lead] % 8
        gain = 1.0 + tab[lead, 0, pl.ds(at, 1), :]
        shift = tab[lead, 1, pl.ds(at, 1), :]
        vec_ref[GAIN : GAIN + 1, lanes] = gain
        vec_ref[SHIFT : SHIFT + 1, lanes] = shift
        gain_t = jnp.transpose(jnp.broadcast_to(gain, (head, head)))
        shift_t = jnp.transpose(jnp.broadcast_to(shift, (head, head)))
        for dr in range(3):
            total = jnp.zeros((head, head), F32)
            for dc in range(3):
                at = (dr * 3 + dc) * head
                w = wh_ref[dr, dc].astype(F32)
                ws_ref[at : at + head, lanes] = (w * gain_t).astype(BF)
                total = total + w * shift_t
            vec_ref[BIAS + dr : BIAS + dr + 1, lanes] = jnp.sum(total, axis=0, keepdims=True)


def prepare(meta, ids, w_enc, w_head, scale, shift, z, leads):
    ch, head, cols = w_enc.shape[-1], w_head.shape[-1], z.shape[0]
    wide = up_to(cols, 16)
    vmem = pl.BlockSpec(memory_space=pltpu.VMEM)
    smem = pl.BlockSpec(memory_space=pltpu.SMEM)
    hbm = pl.BlockSpec(memory_space=pltpu.HBM)
    return pl.pallas_call(
        weights_kernel,
        in_specs=[smem, smem] + [hbm] * 5,
        out_specs=[vmem] * 4,
        out_shape=[
            jax.ShapeDtypeStruct((4, 3 * ch, ch), BF),
            jax.ShapeDtypeStruct((9 * head, leads * head), BF),
            jax.ShapeDtypeStruct((8, leads * head), F32),
            jax.ShapeDtypeStruct((wide, wide), BF),
        ],
        scratch_shapes=[
            pltpu.VMEM(w_enc.shape, BF),
            pltpu.VMEM(w_head.shape, BF),
            pltpu.VMEM((leads, 2, 8, head), F32),
            pltpu.VMEM(z.shape, BF),
            pltpu.SemaphoreType.DMA((3 + 2 * leads,)),
        ],
        compiler_params=params(58),
        name="weights",
    )(meta, ids, w_enc, w_head, scale, shift, z)


def slabs_kernel(first_ref, last_ref, west_ref, east_ref, up_ref, dn_ref, flat):
    xcols, _, ch = first_ref.shape
    rows = west_ref.shape[0]
    reach = up_ref.shape[0]
    for k, (edge, slab, start, r) in enumerate(
        ((first_ref, dn_ref, 0, 0), (last_ref, up_ref, 8 - reach, rows - reach))
    ):
        parts = []
        for j in range(ch // 128):
            lanes = slice(j * 128, (j + 1) * 128)
            flat[k, j] = edge[:, :, lanes].astype(F32).reshape(xcols * 8, 128)
            parts.append([flat[k, j, pl.ds(start + i, xcols, stride=8), :] for i in range(reach)])
        for i in range(reach):
            row = jnp.concatenate([p[i] for p in parts], axis=1).astype(BF)
            slab[i] = jnp.concatenate([west_ref[r + i : r + i + 1, :], row, east_ref[r + i : r + i + 1, :]], axis=0)


def row_slabs(x, west, east, reach):
    xcols, rows, ch = x.shape
    vmem = pl.BlockSpec(memory_space=pltpu.VMEM)
    return pl.pallas_call(
        slabs_kernel,
        in_specs=[vmem] * 4,
        out_specs=[vmem] * 2,
        out_shape=[jax.ShapeDtypeStruct((reach, xcols + 2, ch), BF)] * 2,
        scratch_shapes=[pltpu.VMEM((2, ch // 128, xcols * 8, 128), F32)],
        compiler_params=params(16),
        name="slabs",
    )(x[:, :8], x[:, rows - 8 :], west, east)


def encoder_kernel(
    meta_ref, x_ref, west_ref, east_ref, *refs, first, group
):
    halos, refs = (refs[:2], refs[2:]) if first is None else ((), refs)
    g_ref, wp_ref, out_ref, xs, ys, st, pt = refs[:7]
    cols, rows, ch = x_ref.shape
    reach = 2 * EDGE - 1
    if first is None:
        hf = refs[7]
        for k, halo in enumerate(halos):
            for j in range(ch // 128):
                lanes = slice(j * 128, (j + 1) * 128)
                for i in range(reach):
                    at = 8 - reach + i if k == 0 else i
                    hf[k, j, pl.ds(at, cols + 2, stride=8), :] = halo[i, :, lanes].astype(F32)
    low = 0 if first is None else (first - 1) // 8 * 8

    def stage(at, tile_rows):
        if first is None:
            far = []
            for k in range(2):
                h = [hf[k, j, at.start * 8 : at.stop * 8] for j in range(ch // 128)]
                h = [v.astype(BF).reshape(at.stop - at.start, 8, 128) for v in h]
                far.append(jnp.concatenate(h, axis=2))
            top = jnp.concatenate([far[0], tile_rows(0, 8)], axis=1)
            end = jnp.concatenate([tile_rows(rows - 8, 8), far[1]], axis=1)
            pad = jnp.zeros((at.stop - at.start, 16 - 4 * (EDGE + 1), ch), BF)
            n = 2 * (EDGE + 1)
            for dr in range(3):
                t = top[:, 8 - reach + dr : 8 - reach + dr + n]
                b = end[:, 8 - reach - 2 + dr : 8 - reach - 2 + dr + n]
                xs[at, :, dr * ch : (dr + 1) * ch] = jnp.concatenate([t, b, pad], axis=1)
        else:
            here = tile_rows(low, 24)
            for dr in range(3):
                off = first - 1 - low + dr
                xs[at, :, dr * ch : (dr + 1) * ch] = here[:, off : off + 16]

    stage(slice(0, 1), lambda a, n: west_ref[a : a + n, :].reshape(1, n, ch))
    stage(slice(cols + 1, cols + 2), lambda a, n: east_ref[a : a + n, :].reshape(1, n, ch))
    block = next(n for n in range(32, 0, -1) if cols % n == 0)
    for c in range(0, cols, block):
        stage(slice(c + 1, c + 1 + block), lambda a, n: x_ref[c : c + block, a : a + n, :])

    pairs = cols // 2

    def multiply(c):
        for k, (i, j) in enumerate(((0, 2), (1, 2), (2, 1), (1, 3))):
            t = []
            for q in range(c * group, (c + 1) * group):
                one, two = xs[2 * q + i], xs[2 * q + j]
                t.append(one + two if k == 1 else one - two)
            ys[c % 2, k] = jnp.dot(jnp.concatenate(t, axis=0), g_ref[k], preferred_element_type=F32)

    def finish(c):
        n = group * 16
        sub = next(v for v in range(12, 0, -1) if group % v == 0) * 16
        for a in range(0, n, sub):
            part = slice(a, a + sub)
            m = [ys.at[c % 2, k, part] for k in range(4)]
            both = gelu_twice(m[0][...] + m[1][...] + m[2][...])
            both = both + gelu_twice(m[1][...] - m[2][...] - m[3][...])
            for j in range(ch // 128):
                st[j, part] = both[:, j * 128 : (j + 1) * 128]
        pooled = [
            st[j, pl.ds(0, n // 2, stride=2), :] + st[j, pl.ds(1, n // 2, stride=2), :] for j in range(ch // 128)
        ]
        pooled = (jnp.concatenate(pooled, axis=1) * 0.125).astype(BF)
        pt[c * (n // 2) : (c + 1) * (n // 2)] = jnp.dot(pooled, wp_ref[...], preferred_element_type=F32)

    for c in range(pairs // group):
        multiply(c)
        if c:
            finish(c - 1)
    finish(pairs // group - 1)
    count = out_ref.shape[0]
    for r in range(count):
        row = pt[pl.ds(r, pairs, stride=8), :]
        if first is None and r in (0, count - 1):
            row = jnp.where(meta_ref[0 if r == 0 else 1] == 0, row, 0.0)
        out_ref[r] = row.astype(BF)


def encode(meta, x, west, east, halos, g, wp, first, count, group):
    cols, rows, ch = x.shape
    head = wp.shape[1]
    vmem = pl.BlockSpec(memory_space=pltpu.VMEM)
    scratch = [
        pltpu.VMEM((cols + 2, 16, 3 * ch), BF),
        pltpu.VMEM((2, 4, group * 16, ch), F32),
        pltpu.VMEM((ch // 128, group * 16, 128), F32),
        pltpu.VMEM((cols // 2 * 8, head), F32),
    ]
    if halos is not None:
        scratch.append(pltpu.VMEM((2, ch // 128, (cols + 2) * 8, 128), F32))
    operands = [meta, x, west, east, *(halos or ()), g, wp]
    flops = 2 * cols * 16 * 6 * ch * ch
    return pl.pallas_call(
        functools.partial(encoder_kernel, first=first, group=group),
        in_specs=[pl.BlockSpec(memory_space=pltpu.SMEM)] + [vmem] * (len(operands) - 1),
        out_specs=vmem,
        out_shape=jax.ShapeDtypeStruct((count, cols // 2, head), BF),
        scratch_shapes=scratch,
        compiler_params=params(28),
        cost_estimate=pl.CostEstimate(flops=flops, transcendentals=cols * 16 * ch, bytes_accessed=8 * 1024 * 1024),
        name="encode",
    )(*operands)


def head_kernel(meta_ref, *refs, chunks, blocks, shards, aliased):
    arrays = refs[: sum(n for n, _ in chunks)]
    ws_ref, vec_ref, zs_ref = refs[len(arrays) : len(arrays) + 3]
    out_ref, ps, cs, outs, out_sem = refs[len(arrays) + 3 + aliased :]
    ch = ps.shape[2] // 3
    wide = ps.shape[1]
    leads, rows, cols, _ = out_ref.shape
    odd = meta_ref[2] % 2 == 1
    high = meta_ref[2] // 2 == 1
    if wide > cols:
        ps[:, cols:, :] = jnp.zeros((ps.shape[0], wide - cols, 3 * ch), BF)

    def pieces(r):
        taken = 0
        for count, at in chunks:
            if r in at:
                mine = arrays[taken : taken + count]
                if count == 1:
                    return [mine[0][s, at[r]] for s in range(shards)]
                own, beside, across, both = [a[at[r]] for a in mine]
                here = [jnp.where(odd, beside, own), jnp.where(odd, own, beside)]
                there = [jnp.where(odd, both, across), jnp.where(odd, across, both)]
                lower = [jnp.where(high, t, h) for h, t in zip(here, there)]
                return lower + [jnp.where(high, h, t) for h, t in zip(here, there)]
            taken += count

    bias = vec_ref[BIAS : BIAS + 1, :] + vec_ref[BIAS + 1 : BIAS + 2, :] + vec_ref[BIAS + 2 : BIAS + 3, :]
    first = (meta_ref[0] == 1).astype(F32) * vec_ref[BIAS : BIAS + 1, :]
    last = (meta_ref[1] == 1).astype(F32) * vec_ref[BIAS + 2 : BIAS + 3, :]

    wanted = [sorted({n * STEP + i for i in range(STEP + 2)}) for n in blocks]
    slots = {r: k for k, r in enumerate(sorted(set(sum(wanted, []))))}
    staged = set()

    def stage(n):
        for r in wanted[n]:
            if r in staged:
                continue
            staged.add(r)
            k = slots[r]
            row = jnp.concatenate(pieces(r), axis=0)
            ps[k, :cols, ch : 2 * ch] = row
            ps[k, :cols, :ch] = jnp.concatenate([row[-1:], row[:-1]], axis=0)
            ps[k, :cols, 2 * ch :] = jnp.concatenate([row[1:], row[:1]], axis=0)

    def conv(n):
        p = [ps[slots[r]] for r in wanted[n]]
        lhs = [jnp.concatenate(p[i : i + 3], axis=1) for i in range(STEP)]
        cs[n % 2] = jnp.dot(jnp.concatenate(lhs, axis=0), ws_ref[...], preferred_element_type=F32)

    def finish(n, i):
        row = blocks[n] * STEP + i
        y = cs[n % 2, i * wide : (i + 1) * wide] + (bias - first if row == 0 else (bias - last if row == rows - 1 else bias))
        mixed = jnp.dot(zs_ref[...], gelu_twice(y).astype(BF), preferred_element_type=F32)
        center = ps[slots[row + 1], :, ch : 2 * ch].astype(F32)
        for lead in range(leads):
            lanes = slice(lead * ch, (lead + 1) * ch)
            mod = center * vec_ref[GAIN : GAIN + 1, lanes] + vec_ref[SHIFT : SHIFT + 1, lanes]
            outs[n, lead, i] = (mod + mixed[:, lanes]).astype(BF)[:cols]

    sends = []

    def send(n):
        for lead in range(leads):
            sends.append(
                pltpu.make_async_copy(
                    outs.at[n, lead],
                    out_ref.at[lead, blocks[n] * STEP : (blocks[n] + 1) * STEP],
                    out_sem.at[n, lead],
                )
            )
            sends[-1].start()

    for n in range(len(blocks) + 1):
        if n < len(blocks):
            stage(n)
            conv(n)
        if n:
            for i in range(STEP):
                finish(n - 1, i)
            send(n - 1)
    for c in sends:
        c.wait()


def forecast_heads(meta, arrays, chunks, ws, vec, zs, so_far, blocks, shape):
    leads, rows, cols, ch = shape
    shards = cols // arrays[0].shape[-2]
    wide = zs.shape[0]
    vmem = pl.BlockSpec(memory_space=pltpu.VMEM)
    staged = len({n * STEP + i for n in blocks for i in range(STEP + 2)})
    operands = [meta, *arrays, ws, vec, zs]
    in_specs = [pl.BlockSpec(memory_space=pltpu.SMEM)] + [vmem] * (len(operands) - 1)
    alias = {}
    if so_far is not None:
        alias = {len(operands): 0}
        operands.append(so_far)
        in_specs.append(pl.BlockSpec(memory_space=pltpu.HBM))
    return pl.pallas_call(
        functools.partial(head_kernel, chunks=chunks, blocks=blocks, shards=shards, aliased=len(alias)),
        in_specs=in_specs,
        out_specs=pl.BlockSpec(memory_space=pltpu.HBM),
        out_shape=jax.ShapeDtypeStruct(shape, BF),
        scratch_shapes=[
            pltpu.VMEM((staged, wide, 3 * ch), BF),
            pltpu.VMEM((2, STEP * wide, leads * ch), F32),
            pltpu.VMEM((len(blocks), leads, STEP, cols, ch), BF),
            pltpu.SemaphoreType.DMA((len(blocks), leads)),
        ],
        input_output_aliases=alias,
        compiler_params=params(24 * -(-cols // 360)),
        cost_estimate=pl.CostEstimate(
            flops=len(blocks) * STEP * cols * leads * ch * 2 * (9 * ch + cols),
            transcendentals=len(blocks) * STEP * cols * leads * ch,
            bytes_accessed=len(blocks) * 8 * 1024 * 1024,
        ),
        name="heads",
    )(*operands)


def neighbours(size, wrap):
    count = size if wrap else size - 1
    up = [(i, (i + 1) % size) for i in range(count)]
    return up, [(j, i) for i, j in up]


def swap(size, bit):
    return [(i, i ^ bit) for i in range(size)]


def shards(inputs, w_enc, w_proj, film_scale, film_shift, lead_ids, w_head, zonal_mix):
    rows, cols, ch = inputs.shape
    tile = jnp.transpose(inputs, (1, 0, 2))
    lat, lon = lax.axis_size("lat"), lax.axis_size("lon")
    lat_at, lon_at = lax.axis_index("lat"), lax.axis_index("lon")
    lat_up, lat_dn = neighbours(lat, False)
    lon_up, lon_dn = neighbours(lon, True)
    two_level = lon == 4
    reach = 2 * EDGE - 1
    leads = lead_ids.shape[0] // lon
    head = w_proj.shape[1]
    band_rows = rows // 2

    west = lax.ppermute(tile[-1], "lon", lon_up)
    east = lax.ppermute(tile[0], "lon", lon_dn)

    meta = jnp.stack(
        [lat_at == 0, lat_at == lat - 1, lon_at]
    ).astype(jnp.int32)
    g, ws, vec, zs = prepare(meta, lead_ids, w_enc, w_head, film_scale, film_shift, zonal_mix, leads)
    up, dn = row_slabs(tile, west, east, reach)
    above = lax.ppermute(up, "lat", lat_up)
    below = lax.ppermute(dn, "lat", lat_dn)

    middle = band_rows // 2
    group = cols // 4
    plan = [
        (2 * EDGE, middle - EDGE, None),
        (2 * middle, band_rows - EDGE - middle, None),
        (None, 2 * (EDGE + 1), (above, below)),
    ]
    proj = [encode(meta, tile, west, east, halos, g, w_proj, first, n, group) for first, n, halos in plan]

    sent = []
    for k, own in enumerate(proj):
        if two_level:
            across = lax.ppermute(own, "lon", swap(lon, 2))
            beside = lax.ppermute(own, "lon", swap(lon, 1))
            if k == 2:
                both = lax.ppermute(own, "lon", swap(lon, 3))
            else:
                ready, _ = lax.optimization_barrier((across, proj[2]))
                both = lax.ppermute(ready, "lon", swap(lon, 1))
            sent.append([own, beside, across, both])
        else:
            sent.append([lax.all_gather(own, "lon", axis=0, tiled=False)])

    shape = (leads, band_rows, cols // 2 * lon, head)
    upper, lower = middle - EDGE, band_rows - EDGE - middle
    blocks = band_rows // STEP
    at = [
        {EDGE + 1 + r: r for r in range(upper)},
        {middle + 1 + r: r for r in range(lower)},
        {(r if r <= EDGE else band_rows - EDGE - EDGE - 1 + r + 1): r for r in range(2 * EDGE + 2)},
    ]
    chunks = [(len(a), rows_at) for a, rows_at in zip(sent, at)]
    inner = forecast_heads(
        meta, sent[0] + sent[1], chunks[:2], ws, vec, zs, None, list(range(1, blocks - 1)), shape
    )
    return forecast_heads(
        meta, sent[0] + sent[1] + sent[2], chunks, ws, vec, zs, inner, [0, blocks - 1], shape
    )


def solution(mesh):
    in_specs = (P("lat", "lon", None), P(), P(), P(), P(), P(), P(), P())
    out_specs = P("lon", "lat", None, None)
    return jax.shard_map(shards, mesh=mesh, in_specs=in_specs, out_specs=out_specs, check_vma=False)
```

```python
import functools

import jax
import jax.numpy as jnp
from jax import lax
from jax.experimental import pallas as pl
from jax.experimental.pallas import tpu as pltpu
from jax.sharding import PartitionSpec as P

BF = jnp.bfloat16
F32 = jnp.float32
MIB = 1024 * 1024
EDGE = 2
STEP = 4
BIAS, GAIN, SHIFT = 0, 3, 4


def up_to(n, unit):
    return -(-n // unit) * unit


def gelu_twice(x):
    inner = x * (0.7978845608028654 + 0.035677408136300125 * (x * x))
    return x + x * jnp.tanh(inner)


def params(mib):
    return pltpu.CompilerParams(vmem_limit_bytes=mib * MIB)


def weights_kernel(
    meta_ref, ids_ref, wh_hbm, scale_hbm, shift_hbm, z_hbm,
    ws_ref, vec_ref, zs_ref,
    wh_ref, tab, z_ref, sem,
):
    head = wh_ref.shape[-1]
    leads = ws_ref.shape[1] // head
    cols = z_ref.shape[0]
    ids = [ids_ref[meta_ref[2] * leads + lead] for lead in range(leads)]
    copies = [(z_hbm, z_ref), (wh_hbm, wh_ref)]
    for lead in range(leads):
        block = pl.multiple_of((ids[lead] // 8) * 8, 8)
        copies.append((scale_hbm.at[pl.ds(block, 8)], tab.at[lead, 0]))
        copies.append((shift_hbm.at[pl.ds(block, 8)], tab.at[lead, 1]))
    copies = [pltpu.make_async_copy(one, two, sem.at[i]) for i, (one, two) in enumerate(copies)]
    for c in copies:
        c.start()
    zs_ref[...] = jnp.zeros(zs_ref.shape, BF)
    for c in copies:
        c.wait()
    zs_ref[:cols, :cols] = z_ref[...] * jnp.asarray(0.5, BF)
    for lead in range(leads):
        lanes = slice(lead * head, (lead + 1) * head)
        at = ids[lead] % 8
        gain = 1.0 + tab[lead, 0, pl.ds(at, 1), :]
        shift = tab[lead, 1, pl.ds(at, 1), :]
        vec_ref[GAIN : GAIN + 1, lanes] = gain
        vec_ref[SHIFT : SHIFT + 1, lanes] = shift
        gain_t = jnp.transpose(jnp.broadcast_to(gain, (head, head)))
        shift_t = jnp.transpose(jnp.broadcast_to(shift, (head, head)))
        for dr in range(3):
            total = jnp.zeros((head, head), F32)
            for dc in range(3):
                at = (dr * 3 + dc) * head
                w = wh_ref[dr, dc].astype(F32)
                ws_ref[at : at + head, lanes] = (w * gain_t).astype(BF)
                total = total + w * shift_t
            vec_ref[BIAS + dr : BIAS + dr + 1, lanes] = jnp.sum(total, axis=0, keepdims=True)


def prepare(meta, ids, w_head, scale, shift, z, leads):
    head, cols = w_head.shape[-1], z.shape[0]
    wide = up_to(cols, 16)
    vmem = pl.BlockSpec(memory_space=pltpu.VMEM)
    smem = pl.BlockSpec(memory_space=pltpu.SMEM)
    hbm = pl.BlockSpec(memory_space=pltpu.HBM)
    return pl.pallas_call(
        weights_kernel,
        in_specs=[smem, smem] + [hbm] * 4,
        out_specs=[vmem] * 3,
        out_shape=[
            jax.ShapeDtypeStruct((9 * head, leads * head), BF),
            jax.ShapeDtypeStruct((8, leads * head), F32),
            jax.ShapeDtypeStruct((wide, wide), BF),
        ],
        scratch_shapes=[
            pltpu.VMEM(w_head.shape, BF),
            pltpu.VMEM((leads, 2, 8, head), F32),
            pltpu.VMEM(z.shape, BF),
            pltpu.SemaphoreType.DMA((2 + 2 * leads,)),
        ],
        compiler_params=params(58),
        name="weights",
    )(meta, ids, w_head, scale, shift, z)


def slabs_kernel(x_ref, west_ref, east_ref, up_ref, dn_ref, edge, flat, sem):
    xcols, rows, ch = x_ref.shape
    reach = up_ref.shape[0]
    copies = [
        pltpu.make_async_copy(x_ref.at[:, a : a + 8], edge.at[k], sem.at[k]) for k, a in enumerate((0, rows - 8))
    ]
    for c in copies:
        c.start()
    for k, (slab, start, r) in enumerate(((dn_ref, 0, 0), (up_ref, 8 - reach, rows - reach))):
        copies[k].wait()
        parts = []
        for j in range(ch // 128):
            lanes = slice(j * 128, (j + 1) * 128)
            flat[k, j] = edge[k, :, :, lanes].astype(F32).reshape(xcols * 8, 128)
            parts.append([flat[k, j, pl.ds(start + i, xcols, stride=8), :] for i in range(reach)])
        for i in range(reach):
            row = jnp.concatenate([p[i] for p in parts], axis=1).astype(BF)
            slab[i] = jnp.concatenate([west_ref[r + i : r + i + 1, :], row, east_ref[r + i : r + i + 1, :]], axis=0)


def row_slabs(x, west, east, reach):
    xcols, _, ch = x.shape
    vmem = pl.BlockSpec(memory_space=pltpu.VMEM)
    return pl.pallas_call(
        slabs_kernel,
        in_specs=[pl.BlockSpec(memory_space=pltpu.HBM), vmem, vmem],
        out_specs=[vmem] * 2,
        out_shape=[jax.ShapeDtypeStruct((reach, xcols + 2, ch), BF)] * 2,
        scratch_shapes=[
            pltpu.VMEM((2, xcols, 8, ch), BF),
            pltpu.VMEM((2, ch // 128, xcols * 8, 128), F32),
            pltpu.SemaphoreType.DMA((2,)),
        ],
        compiler_params=params(53),
        name="slabs",
    )(x, west, east)


def encoder_kernel(meta_ref, x_hbm, west_ref, east_ref, *refs, first, group, makes):
    halos, refs = (refs[:2], refs[2:]) if first is None else ((), refs)
    w_hbm, wp_ref, out_ref = refs[:3]
    if makes:
        g_out, w_ref, refs = refs[3], refs[4], refs[5:]
    else:
        refs = refs[3:]
    g_ref, x_ref, xs, ys, st, pt, sem = refs[:7]
    cols, rows, ch = x_hbm.shape
    reach = 2 * EDGE - 1
    low = (0, rows - 8) if first is None else ((first - 1) // 8 * 8,)
    tall = x_ref.shape[2]
    copies = [
        pltpu.make_async_copy(x_hbm.at[:, a : a + tall], x_ref.at[i], sem.at[i]) for i, a in enumerate(low)
    ]
    weights = pltpu.make_async_copy(w_hbm, w_ref if makes else g_ref, sem.at[2])
    if makes:
        weights.start()
    for c in copies:
        c.start()
    if not makes:
        weights.start()
    if makes:
        weights.wait()
        for dr in range(3):
            at = slice(dr * ch, (dr + 1) * ch)
            w = [w_ref[dr, dc].astype(F32) for dc in range(3)]
            half = 0.5 * (w[0] + w[2])
            g_ref[0, at] = w_ref[dr, 0]
            g_ref[1, at] = (half + 0.5 * w[1]).astype(BF)
            g_ref[2, at] = (half - 0.5 * w[1]).astype(BF)
            g_ref[3, at] = w_ref[dr, 2]
        weights = pltpu.make_async_copy(g_ref, g_out, sem.at[3])
        weights.start()
    if first is None:
        hf = refs[7]
        for k, halo in enumerate(halos):
            for j in range(ch // 128):
                lanes = slice(j * 128, (j + 1) * 128)
                for i in range(reach):
                    at = 8 - reach + i if k == 0 else i
                    hf[k, j, pl.ds(at, cols + 2, stride=8), :] = halo[i, :, lanes].astype(F32)
    for c in copies:
        c.wait()

    def stage(at, tile_rows):
        if first is None:
            far = []
            for k in range(2):
                h = [hf[k, j, at.start * 8 : at.stop * 8] for j in range(ch // 128)]
                h = [v.astype(BF).reshape(at.stop - at.start, 8, 128) for v in h]
                far.append(jnp.concatenate(h, axis=2))
            top = jnp.concatenate([far[0], tile_rows(0)], axis=1)
            end = jnp.concatenate([tile_rows(1), far[1]], axis=1)
            pad = jnp.zeros((at.stop - at.start, 16 - 4 * (EDGE + 1), ch), BF)
            n = 2 * (EDGE + 1)
            for dr in range(3):
                t = top[:, 8 - reach + dr : 8 - reach + dr + n]
                b = end[:, 8 - reach - 2 + dr : 8 - reach - 2 + dr + n]
                xs[at, :, dr * ch : (dr + 1) * ch] = jnp.concatenate([t, b, pad], axis=1)
        else:
            here = tile_rows(0)
            for dr in range(3):
                off = first - 1 - low[0] + dr
                xs[at, :, dr * ch : (dr + 1) * ch] = here[:, off : off + 16]

    stage(slice(0, 1), lambda i: west_ref[low[i] : low[i] + tall, :].reshape(1, tall, ch))
    stage(slice(cols + 1, cols + 2), lambda i: east_ref[low[i] : low[i] + tall, :].reshape(1, tall, ch))
    block = next(n for n in range(32, 0, -1) if cols % n == 0)
    for c in range(0, cols, block):
        stage(slice(c + 1, c + 1 + block), lambda i: x_ref[i, c : c + block])

    pairs = cols // 2

    def multiply(c):
        for k, (i, j) in enumerate(((0, 2), (1, 2), (2, 1), (1, 3))):
            t = []
            for q in range(c * group, (c + 1) * group):
                one, two = xs[2 * q + i], xs[2 * q + j]
                t.append(one + two if k == 1 else one - two)
            ys[c % 2, k] = jnp.dot(jnp.concatenate(t, axis=0), g_ref[k], preferred_element_type=F32)

    def finish(c):
        n = group * 16
        sub = next(v for v in range(12, 0, -1) if group % v == 0) * 16
        for a in range(0, n, sub):
            part = slice(a, a + sub)
            m = [ys.at[c % 2, k, part] for k in range(4)]
            both = gelu_twice(m[0][...] + m[1][...] + m[2][...])
            both = both + gelu_twice(m[1][...] - m[2][...] - m[3][...])
            for j in range(ch // 128):
                st[j, part] = both[:, j * 128 : (j + 1) * 128]
        pooled = [
            st[j, pl.ds(0, n // 2, stride=2), :] + st[j, pl.ds(1, n // 2, stride=2), :] for j in range(ch // 128)
        ]
        pooled = (jnp.concatenate(pooled, axis=1) * 0.125).astype(BF)
        pt[c * (n // 2) : (c + 1) * (n // 2)] = jnp.dot(pooled, wp_ref[...], preferred_element_type=F32)

    if not makes:
        weights.wait()
    for c in range(pairs // group):
        multiply(c)
        if c:
            finish(c - 1)
    finish(pairs // group - 1)
    count = out_ref.shape[0]
    for r in range(count):
        row = pt[pl.ds(r, pairs, stride=8), :]
        if first is None and r in (0, count - 1):
            row = jnp.where(meta_ref[0 if r == 0 else 1] == 0, row, 0.0)
        out_ref[r] = row.astype(BF)
    if makes:
        weights.wait()


def encode(meta, x, west, east, halos, w, wp, first, count, group):
    cols, rows, ch = x.shape
    head = wp.shape[1]
    makes = w.ndim == 4
    blocks, tall = (1, 24) if halos is None else (2, 8)
    vmem = pl.BlockSpec(memory_space=pltpu.VMEM)
    hbm = pl.BlockSpec(memory_space=pltpu.HBM)
    form = (4, 3 * ch, ch)
    scratch = [
        pltpu.VMEM(form, BF),
        pltpu.VMEM((blocks, cols, tall, ch), BF),
        pltpu.VMEM((cols + 2, 16, 3 * ch), BF),
        pltpu.VMEM((2, 4, group * 16, ch), F32),
        pltpu.VMEM((ch // 128, group * 16, 128), F32),
        pltpu.VMEM((cols // 2 * 8, head), F32),
        pltpu.SemaphoreType.DMA((4,)),
    ]
    if makes:
        scratch = [pltpu.VMEM(w.shape, BF), *scratch]
    if halos is not None:
        scratch.append(pltpu.VMEM((2, ch // 128, (cols + 2) * 8, 128), F32))
    near = [west, east, *(halos or ())]
    out_shape = [jax.ShapeDtypeStruct((count, cols // 2, head), BF)]
    out_specs = [vmem]
    if makes:
        out_shape.append(jax.ShapeDtypeStruct(form, BF))
        out_specs.append(hbm)
    return pl.pallas_call(
        functools.partial(encoder_kernel, first=first, group=group, makes=makes),
        in_specs=[pl.BlockSpec(memory_space=pltpu.SMEM), hbm] + [vmem] * len(near) + [hbm, vmem],
        out_specs=out_specs,
        out_shape=out_shape,
        scratch_shapes=scratch,
        compiler_params=params(53),
        cost_estimate=pl.CostEstimate(
            flops=2 * cols * 16 * 6 * ch * ch, transcendentals=cols * 16 * ch, bytes_accessed=8 * MIB
        ),
        name="encode",
    )(meta, x, *near, w, wp)


def head_kernel(meta_ref, *refs, chunks, blocks, shards, aliased):
    arrays = refs[: sum(n for n, _ in chunks)]
    ws_ref, vec_ref, zs_ref = refs[len(arrays) : len(arrays) + 3]
    out_ref, ps, cs, outs, out_sem = refs[len(arrays) + 3 + aliased :]
    ch = ps.shape[2] // 3
    wide = ps.shape[1]
    leads, rows, cols, _ = out_ref.shape
    odd = meta_ref[2] % 2 == 1
    high = meta_ref[2] // 2 == 1
    if wide > cols:
        ps[:, cols:, :] = jnp.zeros((ps.shape[0], wide - cols, 3 * ch), BF)

    def pieces(r):
        taken = 0
        for count, at in chunks:
            if r in at:
                mine = arrays[taken : taken + count]
                if count == 1:
                    return [mine[0][s, at[r]] for s in range(shards)]
                own, beside, across, both = [a[at[r]] for a in mine]
                here = [jnp.where(odd, beside, own), jnp.where(odd, own, beside)]
                there = [jnp.where(odd, both, across), jnp.where(odd, across, both)]
                lower = [jnp.where(high, t, h) for h, t in zip(here, there)]
                return lower + [jnp.where(high, h, t) for h, t in zip(here, there)]
            taken += count

    bias = vec_ref[BIAS : BIAS + 1, :] + vec_ref[BIAS + 1 : BIAS + 2, :] + vec_ref[BIAS + 2 : BIAS + 3, :]
    first = (meta_ref[0] == 1).astype(F32) * vec_ref[BIAS : BIAS + 1, :]
    last = (meta_ref[1] == 1).astype(F32) * vec_ref[BIAS + 2 : BIAS + 3, :]

    wanted = [sorted({n * STEP + i for i in range(STEP + 2)}) for n in blocks]
    slots = {r: k for k, r in enumerate(sorted(set(sum(wanted, []))))}
    staged = set()

    def stage(n):
        for r in wanted[n]:
            if r in staged:
                continue
            staged.add(r)
            k = slots[r]
            row = jnp.concatenate(pieces(r), axis=0)
            ps[k, :cols, ch : 2 * ch] = row
            ps[k, :cols, :ch] = jnp.concatenate([row[-1:], row[:-1]], axis=0)
            ps[k, :cols, 2 * ch :] = jnp.concatenate([row[1:], row[:1]], axis=0)

    def conv(n):
        p = [ps[slots[r]] for r in wanted[n]]
        lhs = [jnp.concatenate(p[i : i + 3], axis=1) for i in range(STEP)]
        cs[n % 2] = jnp.dot(jnp.concatenate(lhs, axis=0), ws_ref[...], preferred_element_type=F32)

    def finish(n, i):
        row = blocks[n] * STEP + i
        y = cs[n % 2, i * wide : (i + 1) * wide] + (bias - first if row == 0 else (bias - last if row == rows - 1 else bias))
        mixed = jnp.dot(zs_ref[...], gelu_twice(y).astype(BF), preferred_element_type=F32)
        center = ps[slots[row + 1], :, ch : 2 * ch].astype(F32)
        for lead in range(leads):
            lanes = slice(lead * ch, (lead + 1) * ch)
            mod = center * vec_ref[GAIN : GAIN + 1, lanes] + vec_ref[SHIFT : SHIFT + 1, lanes]
            outs[n, lead, i] = (mod + mixed[:, lanes]).astype(BF)[:cols]

    sends = []

    def send(n):
        for lead in range(leads):
            sends.append(
                pltpu.make_async_copy(
                    outs.at[n, lead],
                    out_ref.at[lead, blocks[n] * STEP : (blocks[n] + 1) * STEP],
                    out_sem.at[n, lead],
                )
            )
            sends[-1].start()

    for n in range(len(blocks) + 1):
        if n < len(blocks):
            stage(n)
            conv(n)
        if n:
            for i in range(STEP):
                finish(n - 1, i)
            send(n - 1)
    for c in sends:
        c.wait()


def forecast_heads(meta, arrays, chunks, ws, vec, zs, so_far, blocks, shape):
    leads, rows, cols, ch = shape
    shards = cols // arrays[0].shape[-2]
    wide = zs.shape[0]
    vmem = pl.BlockSpec(memory_space=pltpu.VMEM)
    staged = len({n * STEP + i for n in blocks for i in range(STEP + 2)})
    operands = [meta, *arrays, ws, vec, zs]
    in_specs = [pl.BlockSpec(memory_space=pltpu.SMEM)] + [vmem] * (len(operands) - 1)
    alias = {}
    if so_far is not None:
        alias = {len(operands): 0}
        operands.append(so_far)
        in_specs.append(pl.BlockSpec(memory_space=pltpu.HBM))
    return pl.pallas_call(
        functools.partial(head_kernel, chunks=chunks, blocks=blocks, shards=shards, aliased=len(alias)),
        in_specs=in_specs,
        out_specs=pl.BlockSpec(memory_space=pltpu.HBM),
        out_shape=jax.ShapeDtypeStruct(shape, BF),
        scratch_shapes=[
            pltpu.VMEM((staged, wide, 3 * ch), BF),
            pltpu.VMEM((2, STEP * wide, leads * ch), F32),
            pltpu.VMEM((len(blocks), leads, STEP, cols, ch), BF),
            pltpu.SemaphoreType.DMA((len(blocks), leads)),
        ],
        input_output_aliases=alias,
        compiler_params=params(24 * -(-cols // 360)),
        cost_estimate=pl.CostEstimate(
            flops=len(blocks) * STEP * cols * leads * ch * 2 * (9 * ch + cols),
            transcendentals=len(blocks) * STEP * cols * leads * ch,
            bytes_accessed=len(blocks) * 8 * 1024 * 1024,
        ),
        name="heads",
    )(*operands)


def neighbours(size, wrap):
    count = size if wrap else size - 1
    up = [(i, (i + 1) % size) for i in range(count)]
    return up, [(j, i) for i, j in up]


def swap(size, bit):
    return [(i, i ^ bit) for i in range(size)]


def shards(inputs, w_enc, w_proj, film_scale, film_shift, lead_ids, w_head, zonal_mix):
    rows, cols, ch = inputs.shape
    tile = jnp.transpose(inputs, (1, 0, 2))
    lat, lon = lax.axis_size("lat"), lax.axis_size("lon")
    lat_at, lon_at = lax.axis_index("lat"), lax.axis_index("lon")
    lat_up, lat_dn = neighbours(lat, False)
    lon_up, lon_dn = neighbours(lon, True)
    two_level = lon == 4
    reach = 2 * EDGE - 1
    leads = lead_ids.shape[0] // lon
    head = w_proj.shape[1]
    band_rows = rows // 2

    west = lax.ppermute(tile[-1], "lon", lon_up)
    east = lax.ppermute(tile[0], "lon", lon_dn)

    meta = jnp.stack(
        [lat_at == 0, lat_at == lat - 1, lon_at]
    ).astype(jnp.int32)
    ws, vec, zs = prepare(meta, lead_ids, w_head, film_scale, film_shift, zonal_mix, leads)
    west, east, ws, vec, zs = lax.optimization_barrier((west, east, ws, vec, zs))
    up, dn = row_slabs(tile, west, east, reach)
    above = lax.ppermute(up, "lat", lat_up)
    below = lax.ppermute(dn, "lat", lat_dn)

    middle = band_rows // 2
    group = cols // 4
    plan = [
        (2 * EDGE, middle - EDGE, None),
        (2 * middle, band_rows - EDGE - middle, None),
        (None, 2 * (EDGE + 1), (above, below)),
    ]
    proj, weights = [], w_enc
    for first, count, halos in plan:
        own, *made = encode(meta, tile, west, east, halos, weights, w_proj, first, count, group)
        proj.append(own)
        weights = made[0] if made else weights

    sent = []
    for k, own in enumerate(proj):
        if two_level:
            across = lax.ppermute(own, "lon", swap(lon, 2))
            beside = lax.ppermute(own, "lon", swap(lon, 1))
            if k == 2:
                both = lax.ppermute(own, "lon", swap(lon, 3))
            else:
                ready, _ = lax.optimization_barrier((across, proj[2]))
                both = lax.ppermute(ready, "lon", swap(lon, 1))
            sent.append([own, beside, across, both])
        else:
            sent.append([lax.all_gather(own, "lon", axis=0, tiled=False)])

    shape = (leads, band_rows, cols // 2 * lon, head)
    upper, lower = middle - EDGE, band_rows - EDGE - middle
    blocks = band_rows // STEP
    at = [
        {EDGE + 1 + r: r for r in range(upper)},
        {middle + 1 + r: r for r in range(lower)},
        {(r if r <= EDGE else band_rows - EDGE - EDGE - 1 + r + 1): r for r in range(2 * EDGE + 2)},
    ]
    chunks = [(len(a), rows_at) for a, rows_at in zip(sent, at)]
    inner = forecast_heads(
        meta, sent[0] + sent[1], chunks[:2], ws, vec, zs, None, list(range(1, blocks - 1)), shape
    )
    return forecast_heads(
        meta, sent[0] + sent[1] + sent[2], chunks, ws, vec, zs, inner, [0, blocks - 1], shape
    )


def solution(mesh):
    in_specs = (P("lat", "lon", None), P(), P(), P(), P(), P(), P(), P())
    out_specs = P("lon", "lat", None, None)
    return jax.shard_map(shards, mesh=mesh, in_specs=in_specs, out_specs=out_specs, check_vma=False)
```

```python
import functools

import jax
import jax.numpy as jnp
from jax import lax
from jax.experimental import pallas as pl
from jax.experimental.pallas import tpu as pltpu
from jax.sharding import PartitionSpec as P

BF = jnp.bfloat16
F32 = jnp.float32
MIB = 1024 * 1024
EDGE = 2
STEP = 4
BIAS, GAIN, SHIFT = 0, 3, 4


def up_to(n, unit):
    return -(-n // unit) * unit


def gelu_twice(x):
    inner = x * (0.7978845608028654 + 0.035677408136300125 * (x * x))
    return x + x * jnp.tanh(inner)


def params(mib):
    return pltpu.CompilerParams(vmem_limit_bytes=mib * MIB)


def weights_kernel(
    meta_ref, ids_ref, x_hbm, we_hbm, wh_hbm, scale_hbm, shift_hbm, z_hbm,
    g_hbm, ws_ref, vec_ref, zs_ref, edge_ref,
    g_ref, we_ref, wh_ref, tab, z_ref, near, flat, sem,
):
    ch = we_ref.shape[-1]
    head = wh_ref.shape[-1]
    leads = ws_ref.shape[1] // head
    cols = z_ref.shape[0]
    xcols, rows, _ = x_hbm.shape
    reach = edge_ref.shape[1]
    ids = [ids_ref[meta_ref[2] * leads + lead] for lead in range(leads)]
    copies = [(we_hbm, we_ref), (x_hbm.at[:, :8], near.at[0]), (x_hbm.at[:, rows - 8 :], near.at[1])]
    copies += [(z_hbm, z_ref), (wh_hbm, wh_ref)]
    for lead in range(leads):
        block = pl.multiple_of((ids[lead] // 8) * 8, 8)
        copies.append((scale_hbm.at[pl.ds(block, 8)], tab.at[lead, 0]))
        copies.append((shift_hbm.at[pl.ds(block, 8)], tab.at[lead, 1]))
    copies = [pltpu.make_async_copy(one, two, sem.at[i]) for i, (one, two) in enumerate(copies)]
    for c in copies:
        c.start()
    zs_ref[...] = jnp.zeros(zs_ref.shape, BF)
    copies[0].wait()
    for dr in range(3):
        at = slice(dr * ch, (dr + 1) * ch)
        w = [we_ref[dr, dc].astype(F32) for dc in range(3)]
        half = 0.5 * (w[0] + w[2])
        g_ref[0, at] = we_ref[dr, 0]
        g_ref[1, at] = (half + 0.5 * w[1]).astype(BF)
        g_ref[2, at] = (half - 0.5 * w[1]).astype(BF)
        g_ref[3, at] = we_ref[dr, 2]
    made = pltpu.make_async_copy(g_ref, g_hbm, sem.at[len(copies)])
    made.start()
    for k in range(2):
        copies[1 + k].wait()
        parts = []
        for j in range(ch // 128):
            flat[k, j] = near[k, :, :, j * 128 : (j + 1) * 128].astype(F32).reshape(xcols * 8, 128)
            first = 0 if k == 0 else 8 - reach
            parts.append([flat[k, j, pl.ds(first + i, xcols, stride=8), :] for i in range(reach)])
        for i in range(reach):
            edge_ref[k, i] = jnp.concatenate([p[i] for p in parts], axis=1).astype(BF)
    for c in copies[3:]:
        c.wait()
    zs_ref[:cols, :cols] = z_ref[...] * jnp.asarray(0.5, BF)
    for lead in range(leads):
        lanes = slice(lead * head, (lead + 1) * head)
        at = ids[lead] % 8
        gain = 1.0 + tab[lead, 0, pl.ds(at, 1), :]
        shift = tab[lead, 1, pl.ds(at, 1), :]
        vec_ref[GAIN : GAIN + 1, lanes] = gain
        vec_ref[SHIFT : SHIFT + 1, lanes] = shift
        gain_t = jnp.transpose(jnp.broadcast_to(gain, (head, head)))
        shift_t = jnp.transpose(jnp.broadcast_to(shift, (head, head)))
        for dr in range(3):
            total = jnp.zeros((head, head), F32)
            for dc in range(3):
                at = (dr * 3 + dc) * head
                w = wh_ref[dr, dc].astype(F32)
                ws_ref[at : at + head, lanes] = (w * gain_t).astype(BF)
                total = total + w * shift_t
            vec_ref[BIAS + dr : BIAS + dr + 1, lanes] = jnp.sum(total, axis=0, keepdims=True)
    made.wait()


def prepare(meta, ids, x, w_enc, w_head, scale, shift, z, leads, reach):
    ch, head, cols = w_enc.shape[-1], w_head.shape[-1], z.shape[0]
    xcols = x.shape[0]
    wide = up_to(cols, 16)
    vmem = pl.BlockSpec(memory_space=pltpu.VMEM)
    smem = pl.BlockSpec(memory_space=pltpu.SMEM)
    hbm = pl.BlockSpec(memory_space=pltpu.HBM)
    form = (4, 3 * ch, ch)
    return pl.pallas_call(
        weights_kernel,
        in_specs=[smem, smem] + [hbm] * 6,
        out_specs=[hbm] + [vmem] * 4,
        out_shape=[
            jax.ShapeDtypeStruct(form, BF),
            jax.ShapeDtypeStruct((9 * head, leads * head), BF),
            jax.ShapeDtypeStruct((8, leads * head), F32),
            jax.ShapeDtypeStruct((wide, wide), BF),
            jax.ShapeDtypeStruct((2, reach, xcols, ch), BF),
        ],
        scratch_shapes=[
            pltpu.VMEM(form, BF),
            pltpu.VMEM(w_enc.shape, BF),
            pltpu.VMEM(w_head.shape, BF),
            pltpu.VMEM((leads, 2, 8, head), F32),
            pltpu.VMEM(z.shape, BF),
            pltpu.VMEM((2, xcols, 8, ch), BF),
            pltpu.VMEM((2, ch // 128, xcols * 8, 128), F32),
            pltpu.SemaphoreType.DMA((6 + 2 * leads,)),
        ],
        compiler_params=params(58),
        cost_estimate=pl.CostEstimate(flops=1 << 31, transcendentals=0, bytes_accessed=12 * MIB),
        name="weights",
    )(meta, ids, x, w_enc, w_head, scale, shift, z)


def slabs_kernel(edge_ref, west_ref, east_ref, up_ref, dn_ref):
    rows = west_ref.shape[0]
    reach = up_ref.shape[0]
    for k, (slab, r) in enumerate(((dn_ref, 0), (up_ref, rows - reach))):
        for i in range(reach):
            ends = [side[r + i : r + i + 1, :] for side in (west_ref, east_ref)]
            slab[i] = jnp.concatenate([ends[0], edge_ref[k, i], ends[1]], axis=0)


def row_slabs(edge, west, east):
    _, reach, xcols, ch = edge.shape
    vmem = pl.BlockSpec(memory_space=pltpu.VMEM)
    return pl.pallas_call(
        slabs_kernel,
        in_specs=[vmem] * 3,
        out_specs=[vmem] * 2,
        out_shape=[jax.ShapeDtypeStruct((reach, xcols + 2, ch), BF)] * 2,
        compiler_params=params(12),
        cost_estimate=pl.CostEstimate(flops=1 << 32, transcendentals=0, bytes_accessed=12 * MIB),
        name="slabs",
    )(edge, west, east)


def encoder_kernel(
    meta_ref, x_ref, west_ref, east_ref, *refs, first, group
):
    halos, refs = (refs[:2], refs[2:]) if first is None else ((), refs)
    g_ref, wp_ref, out_ref, xs, ys, st, pt = refs[:7]
    cols, rows, ch = x_ref.shape
    reach = 2 * EDGE - 1
    if first is None:
        hf = refs[7]
        for k, halo in enumerate(halos):
            for j in range(ch // 128):
                lanes = slice(j * 128, (j + 1) * 128)
                for i in range(reach):
                    at = 8 - reach + i if k == 0 else i
                    hf[k, j, pl.ds(at, cols + 2, stride=8), :] = halo[i, :, lanes].astype(F32)
    low = 0 if first is None else (first - 1) // 8 * 8

    def stage(at, tile_rows):
        if first is None:
            far = []
            for k in range(2):
                h = [hf[k, j, at.start * 8 : at.stop * 8] for j in range(ch // 128)]
                h = [v.astype(BF).reshape(at.stop - at.start, 8, 128) for v in h]
                far.append(jnp.concatenate(h, axis=2))
            top = jnp.concatenate([far[0], tile_rows(0, 8)], axis=1)
            end = jnp.concatenate([tile_rows(rows - 8, 8), far[1]], axis=1)
            pad = jnp.zeros((at.stop - at.start, 16 - 4 * (EDGE + 1), ch), BF)
            n = 2 * (EDGE + 1)
            for dr in range(3):
                t = top[:, 8 - reach + dr : 8 - reach + dr + n]
                b = end[:, 8 - reach - 2 + dr : 8 - reach - 2 + dr + n]
                xs[at, :, dr * ch : (dr + 1) * ch] = jnp.concatenate([t, b, pad], axis=1)
        else:
            here = tile_rows(low, 24)
            for dr in range(3):
                off = first - 1 - low + dr
                xs[at, :, dr * ch : (dr + 1) * ch] = here[:, off : off + 16]

    stage(slice(0, 1), lambda a, n: west_ref[a : a + n, :].reshape(1, n, ch))
    stage(slice(cols + 1, cols + 2), lambda a, n: east_ref[a : a + n, :].reshape(1, n, ch))
    block = next(n for n in range(32, 0, -1) if cols % n == 0)
    for c in range(0, cols, block):
        stage(slice(c + 1, c + 1 + block), lambda a, n: x_ref[c : c + block, a : a + n, :])

    pairs = cols // 2

    def multiply(c):
        for k, (i, j) in enumerate(((0, 2), (1, 2), (2, 1), (1, 3))):
            t = []
            for q in range(c * group, (c + 1) * group):
                one, two = xs[2 * q + i], xs[2 * q + j]
                t.append(one + two if k == 1 else one - two)
            ys[c % 2, k] = jnp.dot(jnp.concatenate(t, axis=0), g_ref[k], preferred_element_type=F32)

    def finish(c):
        n = group * 16
        sub = next(v for v in range(12, 0, -1) if group % v == 0) * 16
        for a in range(0, n, sub):
            part = slice(a, a + sub)
            m = [ys.at[c % 2, k, part] for k in range(4)]
            both = gelu_twice(m[0][...] + m[1][...] + m[2][...])
            both = both + gelu_twice(m[1][...] - m[2][...] - m[3][...])
            for j in range(ch // 128):
                st[j, part] = both[:, j * 128 : (j + 1) * 128]
        pooled = [
            st[j, pl.ds(0, n // 2, stride=2), :] + st[j, pl.ds(1, n // 2, stride=2), :] for j in range(ch // 128)
        ]
        pooled = (jnp.concatenate(pooled, axis=1) * 0.125).astype(BF)
        pt[c * (n // 2) : (c + 1) * (n // 2)] = jnp.dot(pooled, wp_ref[...], preferred_element_type=F32)

    for c in range(pairs // group):
        multiply(c)
        if c:
            finish(c - 1)
    finish(pairs // group - 1)
    count = out_ref.shape[0]
    for r in range(count):
        row = pt[pl.ds(r, pairs, stride=8), :]
        if first is None and r in (0, count - 1):
            row = jnp.where(meta_ref[0 if r == 0 else 1] == 0, row, 0.0)
        out_ref[r] = row.astype(BF)


def encode(meta, x, west, east, halos, g, wp, first, count, group):
    cols, rows, ch = x.shape
    head = wp.shape[1]
    vmem = pl.BlockSpec(memory_space=pltpu.VMEM)
    scratch = [
        pltpu.VMEM((cols + 2, 16, 3 * ch), BF),
        pltpu.VMEM((2, 4, group * 16, ch), F32),
        pltpu.VMEM((ch // 128, group * 16, 128), F32),
        pltpu.VMEM((cols // 2 * 8, head), F32),
    ]
    if halos is not None:
        scratch.append(pltpu.VMEM((2, ch // 128, (cols + 2) * 8, 128), F32))
    operands = [meta, x, west, east, *(halos or ()), g, wp]
    flops = 2 * cols * 16 * 6 * ch * ch
    return pl.pallas_call(
        functools.partial(encoder_kernel, first=first, group=group),
        in_specs=[pl.BlockSpec(memory_space=pltpu.SMEM)] + [vmem] * (len(operands) - 1),
        out_specs=vmem,
        out_shape=jax.ShapeDtypeStruct((count, cols // 2, head), BF),
        scratch_shapes=scratch,
        compiler_params=params(28),
        cost_estimate=pl.CostEstimate(flops=flops, transcendentals=cols * 16 * ch, bytes_accessed=8 * 1024 * 1024),
        name="encode",
    )(*operands)


def head_kernel(meta_ref, *refs, chunks, blocks, shards, aliased):
    arrays = refs[: sum(n for n, _ in chunks)]
    ws_ref, vec_ref, zs_ref = refs[len(arrays) : len(arrays) + 3]
    out_ref, ps, cs, outs, out_sem = refs[len(arrays) + 3 + aliased :]
    ch = ps.shape[2] // 3
    wide = ps.shape[1]
    leads, rows, cols, _ = out_ref.shape
    odd = meta_ref[2] % 2 == 1
    high = meta_ref[2] // 2 == 1
    if wide > cols:
        ps[:, cols:, :] = jnp.zeros((ps.shape[0], wide - cols, 3 * ch), BF)

    def pieces(r):
        taken = 0
        for count, at in chunks:
            if r in at:
                mine = arrays[taken : taken + count]
                if count == 1:
                    return [mine[0][s, at[r]] for s in range(shards)]
                own, beside, across, both = [a[at[r]] for a in mine]
                here = [jnp.where(odd, beside, own), jnp.where(odd, own, beside)]
                there = [jnp.where(odd, both, across), jnp.where(odd, across, both)]
                lower = [jnp.where(high, t, h) for h, t in zip(here, there)]
                return lower + [jnp.where(high, h, t) for h, t in zip(here, there)]
            taken += count

    bias = vec_ref[BIAS : BIAS + 1, :] + vec_ref[BIAS + 1 : BIAS + 2, :] + vec_ref[BIAS + 2 : BIAS + 3, :]
    first = (meta_ref[0] == 1).astype(F32) * vec_ref[BIAS : BIAS + 1, :]
    last = (meta_ref[1] == 1).astype(F32) * vec_ref[BIAS + 2 : BIAS + 3, :]

    wanted = [sorted({n * STEP + i for i in range(STEP + 2)}) for n in blocks]
    slots = {r: k for k, r in enumerate(sorted(set(sum(wanted, []))))}
    staged = set()

    def stage(n):
        for r in wanted[n]:
            if r in staged:
                continue
            staged.add(r)
            k = slots[r]
            row = jnp.concatenate(pieces(r), axis=0)
            ps[k, :cols, ch : 2 * ch] = row
            ps[k, :cols, :ch] = jnp.concatenate([row[-1:], row[:-1]], axis=0)
            ps[k, :cols, 2 * ch :] = jnp.concatenate([row[1:], row[:1]], axis=0)

    def conv(n):
        p = [ps[slots[r]] for r in wanted[n]]
        lhs = [jnp.concatenate(p[i : i + 3], axis=1) for i in range(STEP)]
        cs[n % 2] = jnp.dot(jnp.concatenate(lhs, axis=0), ws_ref[...], preferred_element_type=F32)

    def finish(n, i):
        row = blocks[n] * STEP + i
        y = cs[n % 2, i * wide : (i + 1) * wide] + (bias - first if row == 0 else (bias - last if row == rows - 1 else bias))
        mixed = jnp.dot(zs_ref[...], gelu_twice(y).astype(BF), preferred_element_type=F32)
        center = ps[slots[row + 1], :, ch : 2 * ch].astype(F32)
        for lead in range(leads):
            lanes = slice(lead * ch, (lead + 1) * ch)
            mod = center * vec_ref[GAIN : GAIN + 1, lanes] + vec_ref[SHIFT : SHIFT + 1, lanes]
            outs[n, lead, i] = (mod + mixed[:, lanes]).astype(BF)[:cols]

    sends = []

    def send(n):
        for lead in range(leads):
            sends.append(
                pltpu.make_async_copy(
                    outs.at[n, lead],
                    out_ref.at[lead, blocks[n] * STEP : (blocks[n] + 1) * STEP],
                    out_sem.at[n, lead],
                )
            )
            sends[-1].start()

    for n in range(len(blocks) + 1):
        if n < len(blocks):
            stage(n)
            conv(n)
        if n:
            for i in range(STEP):
                finish(n - 1, i)
            send(n - 1)
    for c in sends:
        c.wait()


def forecast_heads(meta, arrays, chunks, ws, vec, zs, so_far, blocks, shape):
    leads, rows, cols, ch = shape
    shards = cols // arrays[0].shape[-2]
    wide = zs.shape[0]
    vmem = pl.BlockSpec(memory_space=pltpu.VMEM)
    staged = len({n * STEP + i for n in blocks for i in range(STEP + 2)})
    operands = [meta, *arrays, ws, vec, zs]
    in_specs = [pl.BlockSpec(memory_space=pltpu.SMEM)] + [vmem] * (len(operands) - 1)
    alias = {}
    if so_far is not None:
        alias = {len(operands): 0}
        operands.append(so_far)
        in_specs.append(pl.BlockSpec(memory_space=pltpu.HBM))
    return pl.pallas_call(
        functools.partial(head_kernel, chunks=chunks, blocks=blocks, shards=shards, aliased=len(alias)),
        in_specs=in_specs,
        out_specs=pl.BlockSpec(memory_space=pltpu.HBM),
        out_shape=jax.ShapeDtypeStruct(shape, BF),
        scratch_shapes=[
            pltpu.VMEM((staged, wide, 3 * ch), BF),
            pltpu.VMEM((2, STEP * wide, leads * ch), F32),
            pltpu.VMEM((len(blocks), leads, STEP, cols, ch), BF),
            pltpu.SemaphoreType.DMA((len(blocks), leads)),
        ],
        input_output_aliases=alias,
        compiler_params=params(24 * -(-cols // 360)),
        cost_estimate=pl.CostEstimate(
            flops=len(blocks) * STEP * cols * leads * ch * 2 * (9 * ch + cols),
            transcendentals=len(blocks) * STEP * cols * leads * ch,
            bytes_accessed=len(blocks) * 8 * 1024 * 1024,
        ),
        name="heads",
    )(*operands)


def neighbours(size, wrap):
    count = size if wrap else size - 1
    up = [(i, (i + 1) % size) for i in range(count)]
    return up, [(j, i) for i, j in up]


def swap(size, bit):
    return [(i, i ^ bit) for i in range(size)]


def shards(inputs, w_enc, w_proj, film_scale, film_shift, lead_ids, w_head, zonal_mix):
    rows, cols, ch = inputs.shape
    tile = jnp.transpose(inputs, (1, 0, 2))
    lat, lon = lax.axis_size("lat"), lax.axis_size("lon")
    lat_at, lon_at = lax.axis_index("lat"), lax.axis_index("lon")
    lat_up, lat_dn = neighbours(lat, False)
    lon_up, lon_dn = neighbours(lon, True)
    two_level = lon == 4
    reach = 2 * EDGE - 1
    leads = lead_ids.shape[0] // lon
    head = w_proj.shape[1]
    band_rows = rows // 2

    west = lax.ppermute(tile[-1], "lon", lon_up)
    east = lax.ppermute(tile[0], "lon", lon_dn)

    meta = jnp.stack(
        [lat_at == 0, lat_at == lat - 1, lon_at]
    ).astype(jnp.int32)
    g, ws, vec, zs, edge = prepare(
        meta, lead_ids, tile, w_enc, w_head, film_scale, film_shift, zonal_mix, leads, reach
    )
    up, dn = row_slabs(edge, west, east)
    above = lax.ppermute(up, "lat", lat_up)
    below = lax.ppermute(dn, "lat", lat_dn)

    middle = band_rows // 2
    group = cols // 4
    plan = [
        (2 * EDGE, middle - EDGE, None),
        (2 * middle, band_rows - EDGE - middle, None),
        (None, 2 * (EDGE + 1), (above, below)),
    ]
    proj = [encode(meta, tile, west, east, halos, g, w_proj, first, n, group) for first, n, halos in plan]

    sent = []
    for k, own in enumerate(proj):
        if two_level:
            across = lax.ppermute(own, "lon", swap(lon, 2))
            beside = lax.ppermute(own, "lon", swap(lon, 1))
            if k == 2:
                both = lax.ppermute(own, "lon", swap(lon, 3))
            else:
                ready, _ = lax.optimization_barrier((across, proj[2]))
                both = lax.ppermute(ready, "lon", swap(lon, 1))
            sent.append([own, beside, across, both])
        else:
            sent.append([lax.all_gather(own, "lon", axis=0, tiled=False)])

    shape = (leads, band_rows, cols // 2 * lon, head)
    upper, lower = middle - EDGE, band_rows - EDGE - middle
    blocks = band_rows // STEP
    at = [
        {EDGE + 1 + r: r for r in range(upper)},
        {middle + 1 + r: r for r in range(lower)},
        {(r if r <= EDGE else band_rows - EDGE - EDGE - 1 + r + 1): r for r in range(2 * EDGE + 2)},
    ]
    chunks = [(len(a), rows_at) for a, rows_at in zip(sent, at)]
    inner = forecast_heads(
        meta, sent[0] + sent[1], chunks[:2], ws, vec, zs, None, list(range(1, blocks - 1)), shape
    )
    return forecast_heads(
        meta, sent[0] + sent[1] + sent[2], chunks, ws, vec, zs, inner, [0, blocks - 1], shape
    )


def solution(mesh):
    in_specs = (P("lat", "lon", None), P(), P(), P(), P(), P(), P(), P())
    out_specs = P("lon", "lat", None, None)
    return jax.shard_map(shards, mesh=mesh, in_specs=in_specs, out_specs=out_specs, check_vma=False)
```

```python
import functools

import jax
import jax.numpy as jnp
from jax import lax
from jax.experimental import pallas as pl
from jax.experimental.pallas import tpu as pltpu
from jax.sharding import PartitionSpec as P

BF = jnp.bfloat16
F32 = jnp.float32
MIB = 1024 * 1024
EDGE = 2
STEP = 4
BIAS, GAIN, SHIFT = 0, 3, 4


def up_to(n, unit):
    return -(-n // unit) * unit


def gelu_twice(x):
    x = x.astype(BF)
    inner = x * (jnp.asarray(0.7978845608028654, BF) + jnp.asarray(0.035677408136300125, BF) * (x * x))
    return x + x * jnp.tanh(inner)


def params(mib):
    return pltpu.CompilerParams(vmem_limit_bytes=mib * MIB)


def weights_kernel(
    ids_ref, x_hbm, wh_hbm, scale_hbm, shift_hbm, z_hbm,
    ws_ref, vec_ref, zs_ref, edge_ref,
    wh_ref, tab, z_ref, near, flat, sem,
):
    ch = x_hbm.shape[-1]
    head = wh_ref.shape[-1]
    leads = ws_ref.shape[1] // head
    cols = z_ref.shape[0]
    xcols, rows, _ = x_hbm.shape
    reach = edge_ref.shape[1]
    ids = [ids_ref[lax.axis_index("lon") * leads + lead] for lead in range(leads)]
    copies = [(x_hbm.at[:, :8], near.at[0]), (x_hbm.at[:, rows - 8 :], near.at[1])]
    copies += [(z_hbm, z_ref), (wh_hbm, wh_ref)]
    for lead in range(leads):
        block = pl.multiple_of((ids[lead] // 8) * 8, 8)
        copies.append((scale_hbm.at[pl.ds(block, 8)], tab.at[lead, 0]))
        copies.append((shift_hbm.at[pl.ds(block, 8)], tab.at[lead, 1]))
    copies = [pltpu.make_async_copy(one, two, sem.at[i]) for i, (one, two) in enumerate(copies)]
    for c in copies:
        c.start()
    zs_ref[...] = jnp.zeros(zs_ref.shape, BF)
    for k in range(2):
        copies[k].wait()
        parts = []
        for j in range(ch // 128):
            flat[k, j] = near[k, :, :, j * 128 : (j + 1) * 128].astype(F32).reshape(xcols * 8, 128)
            first = 0 if k == 0 else 8 - reach
            parts.append([flat[k, j, pl.ds(first + i, xcols, stride=8), :] for i in range(reach)])
        for i in range(reach):
            edge_ref[k, i] = jnp.concatenate([p[i] for p in parts], axis=1).astype(BF)
    for c in copies[2:]:
        c.wait()
    zs_ref[:cols, :cols] = z_ref[...] * jnp.asarray(0.5, BF)
    for lead in range(leads):
        lanes = slice(lead * head, (lead + 1) * head)
        at = ids[lead] % 8
        gain = 1.0 + tab[lead, 0, pl.ds(at, 1), :]
        shift = tab[lead, 1, pl.ds(at, 1), :]
        vec_ref[GAIN : GAIN + 1, lanes] = gain
        vec_ref[SHIFT : SHIFT + 1, lanes] = shift
        gain_t = jnp.transpose(jnp.broadcast_to(gain, (head, head)))
        shift_t = jnp.transpose(jnp.broadcast_to(shift, (head, head)))
        for dr in range(3):
            total = jnp.zeros((head, head), F32)
            for dc in range(3):
                at = (dr * 3 + dc) * head
                w = wh_ref[dr, dc].astype(F32)
                ws_ref[at : at + head, lanes] = (w * gain_t).astype(BF)
                total = total + w * shift_t
            vec_ref[BIAS + dr : BIAS + dr + 1, lanes] = jnp.sum(total, axis=0, keepdims=True)


def prepare(ids, x, w_head, scale, shift, z, leads, reach):
    head, cols = w_head.shape[-1], z.shape[0]
    xcols, _, ch = x.shape
    wide = up_to(cols, 16)
    vmem = pl.BlockSpec(memory_space=pltpu.VMEM)
    smem = pl.BlockSpec(memory_space=pltpu.SMEM)
    hbm = pl.BlockSpec(memory_space=pltpu.HBM)
    return pl.pallas_call(
        weights_kernel,
        in_specs=[smem] + [hbm] * 5,
        out_specs=[vmem] * 4,
        out_shape=[
            jax.ShapeDtypeStruct((9 * head, leads * head), BF),
            jax.ShapeDtypeStruct((8, leads * head), F32),
            jax.ShapeDtypeStruct((wide, wide), BF),
            jax.ShapeDtypeStruct((2, reach, xcols, ch), BF),
        ],
        scratch_shapes=[
            pltpu.VMEM(w_head.shape, BF),
            pltpu.VMEM((leads, 2, 8, head), F32),
            pltpu.VMEM(z.shape, BF),
            pltpu.VMEM((2, xcols, 8, ch), BF),
            pltpu.VMEM((2, ch // 128, xcols * 8, 128), F32),
            pltpu.SemaphoreType.DMA((4 + 2 * leads,)),
        ],
        compiler_params=params(58),
        cost_estimate=pl.CostEstimate(flops=1 << 31, transcendentals=0, bytes_accessed=12 * MIB),
        name="weights",
    )(ids, x, w_head, scale, shift, z)


def slabs_kernel(edge_ref, west_ref, east_ref, up_ref, dn_ref):
    rows = west_ref.shape[0]
    reach = up_ref.shape[0]
    for k, (slab, r) in enumerate(((dn_ref, 0), (up_ref, rows - reach))):
        for i in range(reach):
            ends = [side[r + i : r + i + 1, :] for side in (west_ref, east_ref)]
            slab[i] = jnp.concatenate([ends[0], edge_ref[k, i], ends[1]], axis=0)


def row_slabs(edge, west, east):
    _, reach, xcols, ch = edge.shape
    vmem = pl.BlockSpec(memory_space=pltpu.VMEM)
    return pl.pallas_call(
        slabs_kernel,
        in_specs=[vmem] * 3,
        out_specs=[vmem] * 2,
        out_shape=[jax.ShapeDtypeStruct((reach, xcols + 2, ch), BF)] * 2,
        compiler_params=params(12),
        cost_estimate=pl.CostEstimate(flops=1 << 32, transcendentals=0, bytes_accessed=12 * MIB),
        name="slabs",
    )(edge, west, east)


def encoder_kernel(x_ref, west_ref, east_ref, *refs, first, group):
    halos, refs = (refs[:2], refs[2:]) if first is None else ((), refs)
    w_ref, wp_ref, out_ref, g_ref, *refs = refs
    ch = x_ref.shape[2]
    for dr in range(3):
        at = slice(dr * ch, (dr + 1) * ch)
        w = [w_ref[dr, dc].astype(F32) for dc in range(3)]
        half = 0.5 * (w[0] + w[2])
        g_ref[0, at] = w_ref[dr, 0]
        g_ref[1, at] = (half + 0.5 * w[1]).astype(BF)
        g_ref[2, at] = (half - 0.5 * w[1]).astype(BF)
        g_ref[3, at] = w_ref[dr, 2]
    xs, ys0, ys1, st0, st1, pt = refs[:6]
    ys, st = (ys0, ys1), (st0, st1)
    cols, rows, ch = x_ref.shape
    reach = 2 * EDGE - 1
    if first is None:
        hf = refs[6]
        for k, halo in enumerate(halos):
            for j in range(ch // 128):
                lanes = slice(j * 128, (j + 1) * 128)
                for i in range(reach):
                    at = 8 - reach + i if k == 0 else i
                    hf[k, j, pl.ds(at, cols + 2, stride=8), :] = halo[i, :, lanes].astype(F32)
    low = 0 if first is None else (first - 1) // 8 * 8

    def stage(at, tile_rows):
        if first is None:
            far = []
            for k in range(2):
                h = [hf[k, j, at.start * 8 : at.stop * 8] for j in range(ch // 128)]
                h = [v.astype(BF).reshape(at.stop - at.start, 8, 128) for v in h]
                far.append(jnp.concatenate(h, axis=2))
            top = jnp.concatenate([far[0], tile_rows(0, 8)], axis=1)
            end = jnp.concatenate([tile_rows(rows - 8, 8), far[1]], axis=1)
            pad = jnp.zeros((at.stop - at.start, 16 - 4 * (EDGE + 1), ch), BF)
            n = 2 * (EDGE + 1)
            for dr in range(3):
                t = top[:, 8 - reach + dr : 8 - reach + dr + n]
                b = end[:, 8 - reach - 2 + dr : 8 - reach - 2 + dr + n]
                xs[at, :, dr * ch : (dr + 1) * ch] = jnp.concatenate([t, b, pad], axis=1)
        else:
            here = tile_rows(low, 24)
            for dr in range(3):
                off = first - 1 - low + dr
                xs[at, :, dr * ch : (dr + 1) * ch] = here[:, off : off + 16]

    stage(slice(0, 1), lambda a, n: west_ref[a : a + n, :].reshape(1, n, ch))
    stage(slice(cols + 1, cols + 2), lambda a, n: east_ref[a : a + n, :].reshape(1, n, ch))
    block = next(n for n in range(32, 0, -1) if cols % n == 0)
    for c in range(0, cols, block):
        stage(slice(c + 1, c + 1 + block), lambda a, n: x_ref[c : c + block, a : a + n, :])

    pairs = cols // 2

    def multiply(c):
        for k, (i, j) in enumerate(((0, 2), (1, 2), (2, 1), (1, 3))):
            t = []
            for q in range(c * group, (c + 1) * group):
                one, two = xs[2 * q + i], xs[2 * q + j]
                t.append(one + two if k == 1 else one - two)
            ys[c % 2][k] = jnp.dot(jnp.concatenate(t, axis=0), g_ref[k], preferred_element_type=F32)

    def finish(c):
        n = group * 16
        sub = next(v for v in range(12, 0, -1) if group % v == 0) * 16
        for a in range(0, n, sub):
            part = slice(a, a + sub)
            m = [ys[c % 2].at[k, part] for k in range(4)]
            both = gelu_twice(m[0][...] + m[1][...] + m[2][...]).astype(F32)
            both = both + gelu_twice(m[1][...] - m[2][...] - m[3][...]).astype(F32)
            for j in range(ch // 128):
                st[c % 2][j, part] = both[:, j * 128 : (j + 1) * 128]
        pooled = [
            st[c % 2][j, pl.ds(0, n // 2, stride=2), :] + st[c % 2][j, pl.ds(1, n // 2, stride=2), :]
            for j in range(ch // 128)
        ]
        pooled = (jnp.concatenate(pooled, axis=1) * 0.125).astype(BF)
        pt[c * (n // 2) : (c + 1) * (n // 2)] = jnp.dot(pooled, wp_ref[...], preferred_element_type=F32)

    for c in range(pairs // group):
        multiply(c)
        if c:
            finish(c - 1)
    finish(pairs // group - 1)
    count = out_ref.shape[0]
    for r in range(count):
        row = pt[pl.ds(r, pairs, stride=8), :]
        if first is None and r in (0, count - 1):
            pole = 0 if r == 0 else lax.axis_size("lat") - 1
            row = jnp.where(lax.axis_index("lat") == pole, 0.0, row)
        out_ref[r] = row.astype(BF)


def encode(x, west, east, halos, w, wp, first, count, group):
    cols, rows, ch = x.shape
    head = wp.shape[1]
    vmem = pl.BlockSpec(memory_space=pltpu.VMEM)
    form = (4, 3 * ch, ch)
    scratch = [
        pltpu.VMEM(form, BF),
        pltpu.VMEM((cols + 2, 16, 3 * ch), BF),
        pltpu.VMEM((4, group * 16, ch), F32),
        pltpu.VMEM((4, group * 16, ch), F32),
        pltpu.VMEM((ch // 128, group * 16, 128), F32),
        pltpu.VMEM((ch // 128, group * 16, 128), F32),
        pltpu.VMEM((cols // 2 * 8, head), F32),
    ]
    if halos is not None:
        scratch.append(pltpu.VMEM((2, ch // 128, (cols + 2) * 8, 128), F32))
    operands = [x, west, east, *(halos or ()), w, wp]
    return pl.pallas_call(
        functools.partial(encoder_kernel, first=first, group=group),
        in_specs=[vmem] * len(operands),
        out_specs=vmem,
        out_shape=jax.ShapeDtypeStruct((count, cols // 2, head), BF),
        scratch_shapes=scratch,
        compiler_params=params(28),
        cost_estimate=pl.CostEstimate(
            flops=2 * cols * 16 * 6 * ch * ch, transcendentals=cols * 16 * ch, bytes_accessed=8 * MIB
        ),
        name="encode",
    )(*operands)


def head_kernel(*refs, chunks, blocks, shards, aliased):
    arrays = refs[: sum(n for n, _ in chunks)]
    ws_ref, vec_ref, zs_ref = refs[len(arrays) : len(arrays) + 3]
    out_ref, ps, cs0, cs1, outs, out_sem = refs[len(arrays) + 3 + aliased :]
    ch = ps.shape[2] // 3
    wide = ps.shape[1]
    leads, rows, cols, _ = out_ref.shape
    cs = (cs0, cs1)
    lat, lon = lax.axis_index("lat"), lax.axis_index("lon")
    odd = lon % 2 == 1
    high = lon // 2 == 1
    if wide > cols:
        ps[:, cols:, :] = jnp.zeros((ps.shape[0], wide - cols, 3 * ch), BF)

    def pieces(r):
        taken = 0
        for count, at in chunks:
            if r in at:
                mine = arrays[taken : taken + count]
                if count == 1:
                    return [mine[0][s, at[r]] for s in range(shards)]
                own, beside, across, both = [a[at[r]] for a in mine]
                here = [jnp.where(odd, beside, own), jnp.where(odd, own, beside)]
                there = [jnp.where(odd, both, across), jnp.where(odd, across, both)]
                lower = [jnp.where(high, t, h) for h, t in zip(here, there)]
                return lower + [jnp.where(high, h, t) for h, t in zip(here, there)]
            taken += count

    bias = vec_ref[BIAS : BIAS + 1, :] + vec_ref[BIAS + 1 : BIAS + 2, :] + vec_ref[BIAS + 2 : BIAS + 3, :]
    first = (lat == 0).astype(F32) * vec_ref[BIAS : BIAS + 1, :]
    last = (lat == lax.axis_size("lat") - 1).astype(F32) * vec_ref[BIAS + 2 : BIAS + 3, :]

    wanted = [sorted({n * STEP + i for i in range(STEP + 2)}) for n in blocks]
    slots = {r: k for k, r in enumerate(sorted(set(sum(wanted, []))))}
    staged = set()

    def stage(n):
        for r in wanted[n]:
            if r in staged:
                continue
            staged.add(r)
            k = slots[r]
            row = jnp.concatenate(pieces(r), axis=0)
            ps[k, :cols, ch : 2 * ch] = row
            ps[k, :cols, :ch] = jnp.concatenate([row[-1:], row[:-1]], axis=0)
            ps[k, :cols, 2 * ch :] = jnp.concatenate([row[1:], row[:1]], axis=0)

    def conv(n):
        p = [ps[slots[r]] for r in wanted[n]]
        lhs = [jnp.concatenate(p[i : i + 3], axis=1) for i in range(STEP)]
        cs[n % 2][...] = jnp.dot(jnp.concatenate(lhs, axis=0), ws_ref[...], preferred_element_type=F32)

    def finish(n, i):
        row = blocks[n] * STEP + i
        y = cs[n % 2][i * wide : (i + 1) * wide] + (bias - first if row == 0 else (bias - last if row == rows - 1 else bias))
        mixed = jnp.dot(zs_ref[...], gelu_twice(y), preferred_element_type=F32)
        center = ps[slots[row + 1], :, ch : 2 * ch].astype(F32)
        for lead in range(leads):
            lanes = slice(lead * ch, (lead + 1) * ch)
            mod = center * vec_ref[GAIN : GAIN + 1, lanes] + vec_ref[SHIFT : SHIFT + 1, lanes]
            outs[n, lead, i] = (mod + mixed[:, lanes]).astype(BF)[:cols]

    sends = []

    def send(n):
        for lead in range(leads):
            sends.append(
                pltpu.make_async_copy(
                    outs.at[n, lead],
                    out_ref.at[lead, blocks[n] * STEP : (blocks[n] + 1) * STEP],
                    out_sem.at[n, lead],
                )
            )
            sends[-1].start()

    for n in range(len(blocks) + 1):
        if n < len(blocks):
            stage(n)
            conv(n)
        if n:
            for i in range(STEP):
                finish(n - 1, i)
            send(n - 1)
    for c in sends:
        c.wait()


def forecast_heads(arrays, chunks, ws, vec, zs, so_far, blocks, shape):
    leads, rows, cols, ch = shape
    shards = cols // arrays[0].shape[-2]
    wide = zs.shape[0]
    vmem = pl.BlockSpec(memory_space=pltpu.VMEM)
    staged = len({n * STEP + i for n in blocks for i in range(STEP + 2)})
    operands = [*arrays, ws, vec, zs]
    in_specs = [vmem] * len(operands)
    alias = {}
    if so_far is not None:
        alias = {len(operands): 0}
        operands.append(so_far)
        in_specs.append(pl.BlockSpec(memory_space=pltpu.HBM))
    return pl.pallas_call(
        functools.partial(head_kernel, chunks=chunks, blocks=blocks, shards=shards, aliased=len(alias)),
        in_specs=in_specs,
        out_specs=pl.BlockSpec(memory_space=pltpu.HBM),
        out_shape=jax.ShapeDtypeStruct(shape, BF),
        scratch_shapes=[
            pltpu.VMEM((staged, wide, 3 * ch), BF),
            pltpu.VMEM((STEP * wide, leads * ch), F32),
            pltpu.VMEM((STEP * wide, leads * ch), F32),
            pltpu.VMEM((len(blocks), leads, STEP, cols, ch), BF),
            pltpu.SemaphoreType.DMA((len(blocks), leads)),
        ],
        input_output_aliases=alias,
        compiler_params=params(24 * -(-cols // 360)),
        cost_estimate=pl.CostEstimate(
            flops=len(blocks) * STEP * cols * leads * ch * 2 * (9 * ch + cols),
            transcendentals=len(blocks) * STEP * cols * leads * ch,
            bytes_accessed=len(blocks) * 8 * 1024 * 1024,
        ),
        name="heads",
    )(*operands)


def neighbours(size, wrap):
    count = size if wrap else size - 1
    up = [(i, (i + 1) % size) for i in range(count)]
    return up, [(j, i) for i, j in up]


def swap(size, bit):
    return [(i, i ^ bit) for i in range(size)]


def shards(inputs, w_enc, w_proj, film_scale, film_shift, lead_ids, w_head, zonal_mix):
    rows, cols, ch = inputs.shape
    tile = jnp.transpose(inputs, (1, 0, 2))
    lat, lon = lax.axis_size("lat"), lax.axis_size("lon")
    lat_up, lat_dn = neighbours(lat, False)
    lon_up, lon_dn = neighbours(lon, True)
    two_level = lon == 4
    reach = 2 * EDGE - 1
    leads = lead_ids.shape[0] // lon
    head = w_proj.shape[1]
    band_rows = rows // 2

    west = lax.ppermute(tile[-1], "lon", lon_up)
    east = lax.ppermute(tile[0], "lon", lon_dn)

    ws, vec, zs, edge = prepare(lead_ids, tile, w_head, film_scale, film_shift, zonal_mix, leads, reach)
    up, dn = row_slabs(edge, west, east)
    above = lax.ppermute(up, "lat", lat_up)
    below = lax.ppermute(dn, "lat", lat_dn)

    middle = band_rows // 2
    group = cols // 4
    plan = [
        (2 * EDGE, middle - EDGE, None),
        (2 * middle, band_rows - EDGE - middle, None),
        (None, 2 * (EDGE + 1), (above, below)),
    ]
    proj = [encode(tile, west, east, halos, w_enc, w_proj, first, n, group) for first, n, halos in plan]

    sent = []
    for k, own in enumerate(proj):
        if two_level:
            across = lax.ppermute(own, "lon", swap(lon, 2))
            beside = lax.ppermute(own, "lon", swap(lon, 1))
            if k == 2:
                both = lax.ppermute(own, "lon", swap(lon, 3))
            else:
                ready, _ = lax.optimization_barrier((across, proj[2]))
                both = lax.ppermute(ready, "lon", swap(lon, 1))
            sent.append([own, beside, across, both])
        else:
            sent.append([lax.all_gather(own, "lon", axis=0, tiled=False)])

    shape = (leads, band_rows, cols // 2 * lon, head)
    upper, lower = middle - EDGE, band_rows - EDGE - middle
    blocks = band_rows // STEP
    at = [
        {EDGE + 1 + r: r for r in range(upper)},
        {middle + 1 + r: r for r in range(lower)},
        {(r if r <= EDGE else band_rows - EDGE - EDGE - 1 + r + 1): r for r in range(2 * EDGE + 2)},
    ]
    chunks = [(len(a), rows_at) for a, rows_at in zip(sent, at)]
    inner = forecast_heads(
        sent[0] + sent[1], chunks[:2], ws, vec, zs, None, list(range(1, blocks - 1)), shape
    )
    return forecast_heads(
        sent[0] + sent[1] + sent[2], chunks, ws, vec, zs, inner, [0, blocks - 1], shape
    )


def solution(mesh):
    in_specs = (P("lat", "lon", None), P(), P(), P(), P(), P(), P(), P())
    out_specs = P("lon", "lat", None, None)
    return jax.shard_map(shards, mesh=mesh, in_specs=in_specs, out_specs=out_specs, check_vma=False)
```

```python
import functools

import jax
import jax.numpy as jnp
from jax import lax
from jax.experimental import pallas as pl
from jax.experimental.pallas import tpu as pltpu
from jax.sharding import PartitionSpec as P

BF = jnp.bfloat16
F32 = jnp.float32
MIB = 1024 * 1024
EDGE = 2
STEP = 4
BIAS, GAIN, SHIFT = 0, 3, 4


def up_to(n, unit):
    return -(-n // unit) * unit


def gelu_twice(x):
    x = x.astype(BF)
    inner = x * (jnp.asarray(0.7978845608028654, BF) + jnp.asarray(0.035677408136300125, BF) * (x * x))
    return x + x * jnp.tanh(inner)


def together(*parts):
    parts = [iter(p) for p in parts]
    while parts:
        parts = [p for p in parts if next(p, parts) is not parts]


def params(mib):
    return pltpu.CompilerParams(vmem_limit_bytes=mib * MIB)


def weights_kernel(
    ids_ref, x_hbm, wh_hbm, scale_hbm, shift_hbm, z_hbm,
    ws_ref, vec_ref, zs_ref, edge_ref,
    wh_ref, tab, z_ref, near, flat, sem,
):
    ch = x_hbm.shape[-1]
    head = wh_ref.shape[-1]
    leads = ws_ref.shape[1] // head
    cols = z_ref.shape[0]
    xcols, rows, _ = x_hbm.shape
    reach = edge_ref.shape[1]
    ids = [ids_ref[lax.axis_index("lon") * leads + lead] for lead in range(leads)]
    copies = [(x_hbm.at[:, :8], near.at[0]), (x_hbm.at[:, rows - 8 :], near.at[1])]
    copies += [(z_hbm, z_ref), (wh_hbm, wh_ref)]
    for lead in range(leads):
        block = pl.multiple_of((ids[lead] // 8) * 8, 8)
        copies.append((scale_hbm.at[pl.ds(block, 8)], tab.at[lead, 0]))
        copies.append((shift_hbm.at[pl.ds(block, 8)], tab.at[lead, 1]))
    copies = [pltpu.make_async_copy(one, two, sem.at[i]) for i, (one, two) in enumerate(copies)]
    for c in copies:
        c.start()
    zs_ref[...] = jnp.zeros(zs_ref.shape, BF)
    for k in range(2):
        copies[k].wait()
        parts = []
        for j in range(ch // 128):
            flat[k, j] = near[k, :, :, j * 128 : (j + 1) * 128].astype(F32).reshape(xcols * 8, 128)
            first = 0 if k == 0 else 8 - reach
            parts.append([flat[k, j, pl.ds(first + i, xcols, stride=8), :] for i in range(reach)])
        for i in range(reach):
            edge_ref[k, i] = jnp.concatenate([p[i] for p in parts], axis=1).astype(BF)
    for c in copies[2:]:
        c.wait()
    zs_ref[:cols, :cols] = z_ref[...] * jnp.asarray(0.5, BF)
    for lead in range(leads):
        lanes = slice(lead * head, (lead + 1) * head)
        at = ids[lead] % 8
        gain = 1.0 + tab[lead, 0, pl.ds(at, 1), :]
        shift = tab[lead, 1, pl.ds(at, 1), :]
        vec_ref[GAIN : GAIN + 1, lanes] = gain
        vec_ref[SHIFT : SHIFT + 1, lanes] = shift
        gain_t = jnp.transpose(jnp.broadcast_to(gain, (head, head)))
        shift_t = jnp.transpose(jnp.broadcast_to(shift, (head, head)))
        for dr in range(3):
            total = jnp.zeros((head, head), F32)
            for dc in range(3):
                at = (dr * 3 + dc) * head
                w = wh_ref[dr, dc].astype(F32)
                ws_ref[at : at + head, lanes] = (w * gain_t).astype(BF)
                total = total + w * shift_t
            vec_ref[BIAS + dr : BIAS + dr + 1, lanes] = jnp.sum(total, axis=0, keepdims=True)


def prepare(ids, x, w_head, scale, shift, z, leads, reach):
    head, cols = w_head.shape[-1], z.shape[0]
    xcols, _, ch = x.shape
    wide = up_to(cols, 16)
    vmem = pl.BlockSpec(memory_space=pltpu.VMEM)
    smem = pl.BlockSpec(memory_space=pltpu.SMEM)
    hbm = pl.BlockSpec(memory_space=pltpu.HBM)
    return pl.pallas_call(
        weights_kernel,
        in_specs=[smem] + [hbm] * 5,
        out_specs=[vmem] * 4,
        out_shape=[
            jax.ShapeDtypeStruct((9 * head, leads * head), BF),
            jax.ShapeDtypeStruct((8, leads * head), F32),
            jax.ShapeDtypeStruct((wide, wide), BF),
            jax.ShapeDtypeStruct((2, reach, xcols, ch), BF),
        ],
        scratch_shapes=[
            pltpu.VMEM(w_head.shape, BF),
            pltpu.VMEM((leads, 2, 8, head), F32),
            pltpu.VMEM(z.shape, BF),
            pltpu.VMEM((2, xcols, 8, ch), BF),
            pltpu.VMEM((2, ch // 128, xcols * 8, 128), F32),
            pltpu.SemaphoreType.DMA((4 + 2 * leads,)),
        ],
        compiler_params=params(58),
        cost_estimate=pl.CostEstimate(flops=1 << 31, transcendentals=0, bytes_accessed=12 * MIB),
        name="weights",
    )(ids, x, w_head, scale, shift, z)


def slabs_kernel(edge_ref, west_ref, east_ref, up_ref, dn_ref):
    rows = west_ref.shape[0]
    reach = up_ref.shape[0]
    for k, (slab, r) in enumerate(((dn_ref, 0), (up_ref, rows - reach))):
        for i in range(reach):
            ends = [side[r + i : r + i + 1, :] for side in (west_ref, east_ref)]
            slab[i] = jnp.concatenate([ends[0], edge_ref[k, i], ends[1]], axis=0)


def row_slabs(edge, west, east):
    _, reach, xcols, ch = edge.shape
    vmem = pl.BlockSpec(memory_space=pltpu.VMEM)
    return pl.pallas_call(
        slabs_kernel,
        in_specs=[vmem] * 3,
        out_specs=[vmem] * 2,
        out_shape=[jax.ShapeDtypeStruct((reach, xcols + 2, ch), BF)] * 2,
        compiler_params=params(12),
        cost_estimate=pl.CostEstimate(flops=1 << 32, transcendentals=0, bytes_accessed=12 * MIB),
        name="slabs",
    )(edge, west, east)


def encoder_kernel(x_ref, west_ref, east_ref, *refs, first, group):
    halos, refs = (refs[:2], refs[2:]) if first is None else ((), refs)
    w_ref, wp_ref, out_ref, g_ref, *refs = refs
    ch = x_ref.shape[2]
    for dr in range(3):
        at = slice(dr * ch, (dr + 1) * ch)
        w = [w_ref[dr, dc].astype(F32) for dc in range(3)]
        half = 0.5 * (w[0] + w[2])
        g_ref[0, at] = w_ref[dr, 0]
        g_ref[1, at] = (half + 0.5 * w[1]).astype(BF)
        g_ref[2, at] = (half - 0.5 * w[1]).astype(BF)
        g_ref[3, at] = w_ref[dr, 2]
    xs, ys0, ys1, st0, st1, pt = refs[:6]
    ys, st = (ys0, ys1), (st0, st1)
    cols, rows, ch = x_ref.shape
    reach = 2 * EDGE - 1
    if first is None:
        hf = refs[6]
        for k, halo in enumerate(halos):
            for j in range(ch // 128):
                lanes = slice(j * 128, (j + 1) * 128)
                for i in range(reach):
                    at = 8 - reach + i if k == 0 else i
                    hf[k, j, pl.ds(at, cols + 2, stride=8), :] = halo[i, :, lanes].astype(F32)
    low = 0 if first is None else (first - 1) // 8 * 8

    def stage(at, tile_rows):
        if first is None:
            far = []
            for k in range(2):
                h = [hf[k, j, at.start * 8 : at.stop * 8] for j in range(ch // 128)]
                h = [v.astype(BF).reshape(at.stop - at.start, 8, 128) for v in h]
                far.append(jnp.concatenate(h, axis=2))
            top = jnp.concatenate([far[0], tile_rows(0, 8)], axis=1)
            end = jnp.concatenate([tile_rows(rows - 8, 8), far[1]], axis=1)
            pad = jnp.zeros((at.stop - at.start, 16 - 4 * (EDGE + 1), ch), BF)
            n = 2 * (EDGE + 1)
            for dr in range(3):
                t = top[:, 8 - reach + dr : 8 - reach + dr + n]
                b = end[:, 8 - reach - 2 + dr : 8 - reach - 2 + dr + n]
                xs[at, :, dr * ch : (dr + 1) * ch] = jnp.concatenate([t, b, pad], axis=1)
        else:
            here = tile_rows(low, 24)
            for dr in range(3):
                off = first - 1 - low + dr
                xs[at, :, dr * ch : (dr + 1) * ch] = here[:, off : off + 16]

    pairs = cols // 2
    groups = pairs // group

    def stage_group(c):
        start, stop = 2 * c * group + (2 if c else 1), 2 * (c + 1) * group + 2
        if c == 0:
            stage(slice(0, 1), lambda a, n: west_ref[a : a + n, :].reshape(1, n, ch))
        if c == groups - 1:
            stage(slice(cols + 1, cols + 2), lambda a, n: east_ref[a : a + n, :].reshape(1, n, ch))
            stop = cols + 1
        size = -(-(stop - start) // 4)
        for p in range(start, stop, size):
            e = min(p + size, stop)
            stage(slice(p, e), lambda a, n: x_ref[p - 1 : e - 1, a : a + n, :])
            yield

    def multiply(c):
        for k, (i, j) in enumerate(((0, 2), (1, 2), (2, 1), (1, 3))):
            t = []
            for q in range(c * group, (c + 1) * group):
                one, two = xs[2 * q + i], xs[2 * q + j]
                t.append(one + two if k == 1 else one - two)
            ys[c % 2][k] = jnp.dot(jnp.concatenate(t, axis=0), g_ref[k], preferred_element_type=F32)
            yield

    def finish(c):
        n = group * 16
        sub = next(v for v in range(12, 0, -1) if group % v == 0) * 16
        for a in range(0, n, sub):
            part = slice(a, a + sub)
            m = [ys[c % 2].at[k, part] for k in range(4)]
            both = gelu_twice(m[0][...] + m[1][...] + m[2][...]).astype(F32)
            both = both + gelu_twice(m[1][...] - m[2][...] - m[3][...]).astype(F32)
            for j in range(ch // 128):
                st[c % 2][j, part] = both[:, j * 128 : (j + 1) * 128]
            yield
        pooled = [
            st[c % 2][j, pl.ds(0, n // 2, stride=2), :] + st[c % 2][j, pl.ds(1, n // 2, stride=2), :]
            for j in range(ch // 128)
        ]
        pooled = (jnp.concatenate(pooled, axis=1) * 0.125).astype(BF)
        pt[c * (n // 2) : (c + 1) * (n // 2)] = jnp.dot(pooled, wp_ref[...], preferred_element_type=F32)
        yield

    together(stage_group(0))
    for c in range(groups + 1):
        together(
            multiply(c) if c < groups else (),
            finish(c - 1) if c else (),
            stage_group(c + 1) if c + 1 < groups else (),
        )
    count = out_ref.shape[0]
    for r in range(count):
        row = pt[pl.ds(r, pairs, stride=8), :]
        if first is None and r in (0, count - 1):
            pole = 0 if r == 0 else lax.axis_size("lat") - 1
            row = jnp.where(lax.axis_index("lat") == pole, 0.0, row)
        out_ref[r] = row.astype(BF)


def encode(x, west, east, halos, w, wp, first, count, group):
    cols, rows, ch = x.shape
    head = wp.shape[1]
    vmem = pl.BlockSpec(memory_space=pltpu.VMEM)
    form = (4, 3 * ch, ch)
    scratch = [
        pltpu.VMEM(form, BF),
        pltpu.VMEM((cols + 2, 16, 3 * ch), BF),
        pltpu.VMEM((4, group * 16, ch), F32),
        pltpu.VMEM((4, group * 16, ch), F32),
        pltpu.VMEM((ch // 128, group * 16, 128), F32),
        pltpu.VMEM((ch // 128, group * 16, 128), F32),
        pltpu.VMEM((cols // 2 * 8, head), F32),
    ]
    if halos is not None:
        scratch.append(pltpu.VMEM((2, ch // 128, (cols + 2) * 8, 128), F32))
    operands = [x, west, east, *(halos or ()), w, wp]
    return pl.pallas_call(
        functools.partial(encoder_kernel, first=first, group=group),
        in_specs=[vmem] * len(operands),
        out_specs=vmem,
        out_shape=jax.ShapeDtypeStruct((count, cols // 2, head), BF),
        scratch_shapes=scratch,
        compiler_params=params(28),
        cost_estimate=pl.CostEstimate(
            flops=2 * cols * 16 * 6 * ch * ch, transcendentals=cols * 16 * ch, bytes_accessed=8 * MIB
        ),
        name="encode",
    )(*operands)


def head_kernel(*refs, chunks, blocks, shards, aliased):
    arrays = refs[: sum(n for n, _ in chunks)]
    ws_ref, vec_ref, zs_ref = refs[len(arrays) : len(arrays) + 3]
    out_ref, ps, cs0, cs1, outs, out_sem = refs[len(arrays) + 3 + aliased :]
    ch = ps.shape[2] // 3
    wide = ps.shape[1]
    leads, rows, cols, _ = out_ref.shape
    cs = (cs0, cs1)
    lat, lon = lax.axis_index("lat"), lax.axis_index("lon")
    odd = lon % 2 == 1
    high = lon // 2 == 1
    if wide > cols:
        ps[:, cols:, :] = jnp.zeros((ps.shape[0], wide - cols, 3 * ch), BF)

    def pieces(r):
        taken = 0
        for count, at in chunks:
            if r in at:
                mine = arrays[taken : taken + count]
                if count == 1:
                    return [mine[0][s, at[r]] for s in range(shards)]
                own, beside, across, both = [a[at[r]] for a in mine]
                here = [jnp.where(odd, beside, own), jnp.where(odd, own, beside)]
                there = [jnp.where(odd, both, across), jnp.where(odd, across, both)]
                lower = [jnp.where(high, t, h) for h, t in zip(here, there)]
                return lower + [jnp.where(high, h, t) for h, t in zip(here, there)]
            taken += count

    bias = vec_ref[BIAS : BIAS + 1, :] + vec_ref[BIAS + 1 : BIAS + 2, :] + vec_ref[BIAS + 2 : BIAS + 3, :]
    first = (lat == 0).astype(F32) * vec_ref[BIAS : BIAS + 1, :]
    last = (lat == lax.axis_size("lat") - 1).astype(F32) * vec_ref[BIAS + 2 : BIAS + 3, :]

    wanted = [sorted({n * STEP + i for i in range(STEP + 2)}) for n in blocks]
    slots = {r: k for k, r in enumerate(sorted(set(sum(wanted, []))))}
    staged = set()

    def stage(n):
        for r in wanted[n]:
            if r in staged:
                continue
            staged.add(r)
            k = slots[r]
            row = jnp.concatenate(pieces(r), axis=0)
            ps[k, :cols, ch : 2 * ch] = row
            ps[k, :cols, :ch] = jnp.concatenate([row[-1:], row[:-1]], axis=0)
            ps[k, :cols, 2 * ch :] = jnp.concatenate([row[1:], row[:1]], axis=0)
            yield

    def conv(n):
        half = STEP // 2
        for h in range(2):
            p = [ps[slots[r]] for r in wanted[n][h * half : (h + 1) * half + 2]]
            lhs = [jnp.concatenate(p[i : i + 3], axis=1) for i in range(half)]
            at = slice(h * half * wide, (h + 1) * half * wide)
            cs[n % 2][at] = jnp.dot(jnp.concatenate(lhs, axis=0), ws_ref[...], preferred_element_type=F32)
            yield
            yield

    def finish(n):
        for i in range(STEP):
            row = blocks[n] * STEP + i
            near = bias - first if row == 0 else (bias - last if row == rows - 1 else bias)
            y = cs[n % 2][i * wide : (i + 1) * wide] + near
            mixed = jnp.dot(zs_ref[...], gelu_twice(y), preferred_element_type=F32)
            center = ps[slots[row + 1], :, ch : 2 * ch].astype(F32)
            for lead in range(leads):
                lanes = slice(lead * ch, (lead + 1) * ch)
                mod = center * vec_ref[GAIN : GAIN + 1, lanes] + vec_ref[SHIFT : SHIFT + 1, lanes]
                outs[n, lead, i] = (mod + mixed[:, lanes]).astype(BF)[:cols]
            yield

    sends = []

    def send(n):
        for lead in range(leads):
            sends.append(
                pltpu.make_async_copy(
                    outs.at[n, lead],
                    out_ref.at[lead, blocks[n] * STEP : (blocks[n] + 1) * STEP],
                    out_sem.at[n, lead],
                )
            )
            sends[-1].start()

    together(stage(0))
    for n in range(len(blocks) + 1):
        together(
            conv(n) if n < len(blocks) else (),
            finish(n - 1) if n else (),
            stage(n + 1) if n + 1 < len(blocks) else (),
        )
        if n:
            send(n - 1)
    for c in sends:
        c.wait()


def forecast_heads(arrays, chunks, ws, vec, zs, so_far, blocks, shape):
    leads, rows, cols, ch = shape
    shards = cols // arrays[0].shape[-2]
    wide = zs.shape[0]
    vmem = pl.BlockSpec(memory_space=pltpu.VMEM)
    staged = len({n * STEP + i for n in blocks for i in range(STEP + 2)})
    operands = [*arrays, ws, vec, zs]
    in_specs = [vmem] * len(operands)
    alias = {}
    if so_far is not None:
        alias = {len(operands): 0}
        operands.append(so_far)
        in_specs.append(pl.BlockSpec(memory_space=pltpu.HBM))
    return pl.pallas_call(
        functools.partial(head_kernel, chunks=chunks, blocks=blocks, shards=shards, aliased=len(alias)),
        in_specs=in_specs,
        out_specs=pl.BlockSpec(memory_space=pltpu.HBM),
        out_shape=jax.ShapeDtypeStruct(shape, BF),
        scratch_shapes=[
            pltpu.VMEM((staged, wide, 3 * ch), BF),
            pltpu.VMEM((STEP * wide, leads * ch), F32),
            pltpu.VMEM((STEP * wide, leads * ch), F32),
            pltpu.VMEM((len(blocks), leads, STEP, cols, ch), BF),
            pltpu.SemaphoreType.DMA((len(blocks), leads)),
        ],
        input_output_aliases=alias,
        compiler_params=params(24 * -(-cols // 360)),
        cost_estimate=pl.CostEstimate(
            flops=len(blocks) * STEP * cols * leads * ch * 2 * (9 * ch + cols),
            transcendentals=len(blocks) * STEP * cols * leads * ch,
            bytes_accessed=len(blocks) * 8 * 1024 * 1024,
        ),
        name="heads",
    )(*operands)


def neighbours(size, wrap):
    count = size if wrap else size - 1
    up = [(i, (i + 1) % size) for i in range(count)]
    return up, [(j, i) for i, j in up]


def swap(size, bit):
    return [(i, i ^ bit) for i in range(size)]


def shards(inputs, w_enc, w_proj, film_scale, film_shift, lead_ids, w_head, zonal_mix):
    rows, cols, ch = inputs.shape
    tile = jnp.transpose(inputs, (1, 0, 2))
    lat, lon = lax.axis_size("lat"), lax.axis_size("lon")
    lat_up, lat_dn = neighbours(lat, False)
    lon_up, lon_dn = neighbours(lon, True)
    two_level = lon == 4
    reach = 2 * EDGE - 1
    leads = lead_ids.shape[0] // lon
    head = w_proj.shape[1]
    band_rows = rows // 2

    west = lax.ppermute(tile[-1], "lon", lon_up)
    east = lax.ppermute(tile[0], "lon", lon_dn)

    ws, vec, zs, edge = prepare(lead_ids, tile, w_head, film_scale, film_shift, zonal_mix, leads, reach)
    up, dn = row_slabs(edge, west, east)
    above = lax.ppermute(up, "lat", lat_up)
    below = lax.ppermute(dn, "lat", lat_dn)

    middle = band_rows // 2
    group = cols // 6
    plan = [
        (2 * EDGE, middle - EDGE, None),
        (2 * middle, band_rows - EDGE - middle, None),
        (None, 2 * (EDGE + 1), (above, below)),
    ]
    proj = [encode(tile, west, east, halos, w_enc, w_proj, first, n, group) for first, n, halos in plan]

    sent = []
    for k, own in enumerate(proj):
        if two_level:
            across = lax.ppermute(own, "lon", swap(lon, 2))
            beside = lax.ppermute(own, "lon", swap(lon, 1))
            if k == 2:
                both = lax.ppermute(own, "lon", swap(lon, 3))
            else:
                ready, _ = lax.optimization_barrier((across, proj[2]))
                both = lax.ppermute(ready, "lon", swap(lon, 1))
            sent.append([own, beside, across, both])
        else:
            sent.append([lax.all_gather(own, "lon", axis=0, tiled=False)])

    shape = (leads, band_rows, cols // 2 * lon, head)
    upper, lower = middle - EDGE, band_rows - EDGE - middle
    blocks = band_rows // STEP
    at = [
        {EDGE + 1 + r: r for r in range(upper)},
        {middle + 1 + r: r for r in range(lower)},
        {(r if r <= EDGE else band_rows - EDGE - EDGE - 1 + r + 1): r for r in range(2 * EDGE + 2)},
    ]
    chunks = [(len(a), rows_at) for a, rows_at in zip(sent, at)]
    inner = forecast_heads(
        sent[0] + sent[1], chunks[:2], ws, vec, zs, None, list(range(1, blocks - 1)), shape
    )
    return forecast_heads(
        sent[0] + sent[1] + sent[2], chunks, ws, vec, zs, inner, [0, blocks - 1], shape
    )


def solution(mesh):
    in_specs = (P("lat", "lon", None), P(), P(), P(), P(), P(), P(), P())
    out_specs = P("lon", "lat", None, None)
    return jax.shard_map(shards, mesh=mesh, in_specs=in_specs, out_specs=out_specs, check_vma=False)
```

```python
import functools

import jax
import jax.numpy as jnp
from jax import lax
from jax.experimental import pallas as pl
from jax.experimental.pallas import tpu as pltpu
from jax.sharding import PartitionSpec as P

BF = jnp.bfloat16
F32 = jnp.float32
MIB = 1024 * 1024
EDGE = 2
STEP = 4
BIAS, GAIN, SHIFT = 0, 3, 4


def up_to(n, unit):
    return -(-n // unit) * unit


def gelu_twice(x):
    x = x.astype(BF)
    inner = x * (jnp.asarray(0.7978845608028654, BF) + jnp.asarray(0.035677408136300125, BF) * (x * x))
    return x + x * jnp.tanh(inner)


def together(*parts):
    parts = [iter(p) for p in parts]
    while parts:
        parts = [p for p in parts if next(p, parts) is not parts]


def params(mib):
    return pltpu.CompilerParams(vmem_limit_bytes=mib * MIB)


def weights_kernel(
    ids_ref, x_hbm, wh_hbm, scale_hbm, shift_hbm, z_hbm,
    ws_ref, vec_ref, zs_ref, edge_ref,
    wh_ref, tab, z_ref, near, flat, sem,
):
    ch = x_hbm.shape[-1]
    head = wh_ref.shape[-1]
    leads = ws_ref.shape[1] // head
    cols = z_ref.shape[0]
    xcols, rows, _ = x_hbm.shape
    reach = edge_ref.shape[1]
    ids = [ids_ref[lax.axis_index("lon") * leads + lead] for lead in range(leads)]
    copies = [(x_hbm.at[:, :8], near.at[0]), (x_hbm.at[:, rows - 8 :], near.at[1])]
    copies += [(z_hbm, z_ref), (wh_hbm, wh_ref)]
    for lead in range(leads):
        block = pl.multiple_of((ids[lead] // 8) * 8, 8)
        copies.append((scale_hbm.at[pl.ds(block, 8)], tab.at[lead, 0]))
        copies.append((shift_hbm.at[pl.ds(block, 8)], tab.at[lead, 1]))
    copies = [pltpu.make_async_copy(one, two, sem.at[i]) for i, (one, two) in enumerate(copies)]
    for c in copies:
        c.start()
    zs_ref[...] = jnp.zeros(zs_ref.shape, BF)
    for k in range(2):
        copies[k].wait()
        parts = []
        for j in range(ch // 128):
            flat[k, j] = near[k, :, :, j * 128 : (j + 1) * 128].astype(F32).reshape(xcols * 8, 128)
            first = 0 if k == 0 else 8 - reach
            parts.append([flat[k, j, pl.ds(first + i, xcols, stride=8), :] for i in range(reach)])
        for i in range(reach):
            edge_ref[k, i] = jnp.concatenate([p[i] for p in parts], axis=1).astype(BF)
    for c in copies[2:]:
        c.wait()
    zs_ref[:cols, :cols] = z_ref[...] * jnp.asarray(0.5, BF)
    for lead in range(leads):
        lanes = slice(lead * head, (lead + 1) * head)
        at = ids[lead] % 8
        gain = 1.0 + tab[lead, 0, pl.ds(at, 1), :]
        shift = tab[lead, 1, pl.ds(at, 1), :]
        vec_ref[GAIN : GAIN + 1, lanes] = gain
        vec_ref[SHIFT : SHIFT + 1, lanes] = shift
        gain_t = jnp.transpose(jnp.broadcast_to(gain, (head, head)))
        shift_t = jnp.transpose(jnp.broadcast_to(shift, (head, head)))
        for dr in range(3):
            total = jnp.zeros((head, head), F32)
            for dc in range(3):
                at = (dr * 3 + dc) * head
                w = wh_ref[dr, dc].astype(F32)
                ws_ref[at : at + head, lanes] = (w * gain_t).astype(BF)
                total = total + w * shift_t
            vec_ref[BIAS + dr : BIAS + dr + 1, lanes] = jnp.sum(total, axis=0, keepdims=True)


def prepare(ids, x, w_head, scale, shift, z, leads, reach):
    head, cols = w_head.shape[-1], z.shape[0]
    xcols, _, ch = x.shape
    wide = up_to(cols, 16)
    vmem = pl.BlockSpec(memory_space=pltpu.VMEM)
    smem = pl.BlockSpec(memory_space=pltpu.SMEM)
    hbm = pl.BlockSpec(memory_space=pltpu.HBM)
    return pl.pallas_call(
        weights_kernel,
        in_specs=[smem] + [hbm] * 5,
        out_specs=[vmem] * 4,
        out_shape=[
            jax.ShapeDtypeStruct((9 * head, leads * head), BF),
            jax.ShapeDtypeStruct((8, leads * head), F32),
            jax.ShapeDtypeStruct((wide, wide), BF),
            jax.ShapeDtypeStruct((2, reach, xcols, ch), BF),
        ],
        scratch_shapes=[
            pltpu.VMEM(w_head.shape, BF),
            pltpu.VMEM((leads, 2, 8, head), F32),
            pltpu.VMEM(z.shape, BF),
            pltpu.VMEM((2, xcols, 8, ch), BF),
            pltpu.VMEM((2, ch // 128, xcols * 8, 128), F32),
            pltpu.SemaphoreType.DMA((4 + 2 * leads,)),
        ],
        compiler_params=params(58),
        cost_estimate=pl.CostEstimate(flops=1 << 31, transcendentals=0, bytes_accessed=12 * MIB),
        name="weights",
    )(ids, x, w_head, scale, shift, z)


def slabs_kernel(edge_ref, west_ref, east_ref, up_ref, dn_ref):
    rows = west_ref.shape[0]
    reach = up_ref.shape[0]
    for k, (slab, r) in enumerate(((dn_ref, 0), (up_ref, rows - reach))):
        for i in range(reach):
            ends = [side[r + i : r + i + 1, :] for side in (west_ref, east_ref)]
            slab[i] = jnp.concatenate([ends[0], edge_ref[k, i], ends[1]], axis=0)


def row_slabs(edge, west, east):
    _, reach, xcols, ch = edge.shape
    vmem = pl.BlockSpec(memory_space=pltpu.VMEM)
    return pl.pallas_call(
        slabs_kernel,
        in_specs=[vmem] * 3,
        out_specs=[vmem] * 2,
        out_shape=[jax.ShapeDtypeStruct((reach, xcols + 2, ch), BF)] * 2,
        compiler_params=params(12),
        cost_estimate=pl.CostEstimate(flops=1 << 32, transcendentals=0, bytes_accessed=12 * MIB),
        name="slabs",
    )(edge, west, east)


def encoder_kernel(x_ref, west_ref, east_ref, *refs, first, group):
    halos, refs = (refs[:2], refs[2:]) if first is None else ((), refs)
    w_ref, wp_ref, out_ref, g_ref, *refs = refs
    ch = x_ref.shape[2]
    for dr in range(3):
        at = slice(dr * ch, (dr + 1) * ch)
        w = [w_ref[dr, dc].astype(F32) for dc in range(3)]
        half = 0.5 * (w[0] + w[2])
        g_ref[0, at] = w_ref[dr, 0]
        g_ref[1, at] = (half + 0.5 * w[1]).astype(BF)
        g_ref[2, at] = (half - 0.5 * w[1]).astype(BF)
        g_ref[3, at] = w_ref[dr, 2]
    xs, ys0, ys1, st0, st1, pt = refs[:6]
    ys, st = (ys0, ys1), (st0, st1)
    cols, rows, ch = x_ref.shape
    reach = 2 * EDGE - 1
    if first is None:
        hf = refs[6]
        for k, halo in enumerate(halos):
            for j in range(ch // 128):
                lanes = slice(j * 128, (j + 1) * 128)
                for i in range(reach):
                    at = 8 - reach + i if k == 0 else i
                    hf[k, j, pl.ds(at, cols + 2, stride=8), :] = halo[i, :, lanes].astype(F32)
    low = 0 if first is None else (first - 1) // 8 * 8

    def stage(at, tile_rows):
        if first is None:
            far = []
            for k in range(2):
                h = [hf[k, j, at.start * 8 : at.stop * 8] for j in range(ch // 128)]
                h = [v.astype(BF).reshape(at.stop - at.start, 8, 128) for v in h]
                far.append(jnp.concatenate(h, axis=2))
            top = jnp.concatenate([far[0], tile_rows(0, 8)], axis=1)
            end = jnp.concatenate([tile_rows(rows - 8, 8), far[1]], axis=1)
            pad = jnp.zeros((at.stop - at.start, 16 - 4 * (EDGE + 1), ch), BF)
            n = 2 * (EDGE + 1)
            for dr in range(3):
                t = top[:, 8 - reach + dr : 8 - reach + dr + n]
                b = end[:, 8 - reach - 2 + dr : 8 - reach - 2 + dr + n]
                xs[at, :, dr * ch : (dr + 1) * ch] = jnp.concatenate([t, b, pad], axis=1)
        else:
            here = tile_rows(low, 24)
            for dr in range(3):
                off = first - 1 - low + dr
                xs[at, :, dr * ch : (dr + 1) * ch] = here[:, off : off + 16]

    pairs = cols // 2
    groups = pairs // group

    def stage_group(c):
        start, stop = 2 * c * group + (2 if c else 1), 2 * (c + 1) * group + 2
        if c == 0:
            stage(slice(0, 1), lambda a, n: west_ref[a : a + n, :].reshape(1, n, ch))
        if c == groups - 1:
            stage(slice(cols + 1, cols + 2), lambda a, n: east_ref[a : a + n, :].reshape(1, n, ch))
            stop = cols + 1
        size = -(-(stop - start) // 4)
        for p in range(start, stop, size):
            e = min(p + size, stop)
            stage(slice(p, e), lambda a, n: x_ref[p - 1 : e - 1, a : a + n, :])
            yield

    def multiply(c):
        for k, (i, j) in enumerate(((0, 2), (1, 2), (2, 1), (1, 3))):
            t = []
            for q in range(c * group, (c + 1) * group):
                one, two = xs[2 * q + i], xs[2 * q + j]
                t.append(one + two if k == 1 else one - two)
            ys[c % 2][k] = jnp.dot(jnp.concatenate(t, axis=0), g_ref[k], preferred_element_type=F32)
            yield

    def finish(c):
        n = group * 16
        sub = next(v for v in range(12, 0, -1) if group % v == 0) * 16
        for a in range(0, n, sub):
            part = slice(a, a + sub)
            m = [ys[c % 2].at[k, part] for k in range(4)]
            both = gelu_twice(m[0][...] + m[1][...] + m[2][...]).astype(F32)
            both = both + gelu_twice(m[1][...] - m[2][...] - m[3][...]).astype(F32)
            for j in range(ch // 128):
                st[c % 2][j, part] = both[:, j * 128 : (j + 1) * 128]
            yield
        pooled = [
            st[c % 2][j, pl.ds(0, n // 2, stride=2), :] + st[c % 2][j, pl.ds(1, n // 2, stride=2), :]
            for j in range(ch // 128)
        ]
        pooled = (jnp.concatenate(pooled, axis=1) * 0.125).astype(BF)
        pt[c * (n // 2) : (c + 1) * (n // 2)] = jnp.dot(pooled, wp_ref[...], preferred_element_type=F32)
        yield

    together(stage_group(0))
    for c in range(groups + 1):
        together(
            multiply(c) if c < groups else (),
            finish(c - 1) if c else (),
            stage_group(c + 1) if c + 1 < groups else (),
        )
    count = out_ref.shape[0]
    for r in range(count):
        row = pt[pl.ds(r, pairs, stride=8), :]
        if first is None and r in (0, count - 1):
            pole = 0 if r == 0 else lax.axis_size("lat") - 1
            row = jnp.where(lax.axis_index("lat") == pole, 0.0, row)
        out_ref[r] = row.astype(BF)


def encode(x, west, east, halos, w, wp, first, count, group):
    cols, rows, ch = x.shape
    head = wp.shape[1]
    vmem = pl.BlockSpec(memory_space=pltpu.VMEM)
    form = (4, 3 * ch, ch)
    scratch = [
        pltpu.VMEM(form, BF),
        pltpu.VMEM((cols + 2, 16, 3 * ch), BF),
        pltpu.VMEM((4, group * 16, ch), F32),
        pltpu.VMEM((4, group * 16, ch), F32),
        pltpu.VMEM((ch // 128, group * 16, 128), F32),
        pltpu.VMEM((ch // 128, group * 16, 128), F32),
        pltpu.VMEM((cols // 2 * 8, head), F32),
    ]
    if halos is not None:
        scratch.append(pltpu.VMEM((2, ch // 128, (cols + 2) * 8, 128), F32))
    operands = [x, west, east, *(halos or ()), w, wp]
    return pl.pallas_call(
        functools.partial(encoder_kernel, first=first, group=group),
        in_specs=[vmem] * len(operands),
        out_specs=vmem,
        out_shape=jax.ShapeDtypeStruct((count, cols // 2, head), BF),
        scratch_shapes=scratch,
        compiler_params=params(28),
        cost_estimate=pl.CostEstimate(
            flops=2 * cols * 16 * 6 * ch * ch, transcendentals=cols * 16 * ch, bytes_accessed=8 * MIB
        ),
        name="encode",
    )(*operands)


def head_kernel(*refs, chunks, blocks, shards, aliased):
    arrays = refs[: sum(n for n, _ in chunks)]
    ws_ref, vec_ref, zs_ref = refs[len(arrays) : len(arrays) + 3]
    out_ref, ps, cs0, cs1, outs, out_sem = refs[len(arrays) + 3 + aliased :]
    ch = ps.shape[2] // 3
    wide = ps.shape[1]
    leads, rows, cols, _ = out_ref.shape
    cs = (cs0, cs1)
    lat, lon = lax.axis_index("lat"), lax.axis_index("lon")
    odd = lon % 2 == 1
    high = lon // 2 == 1
    if wide > cols:
        ps[:, cols:, :] = jnp.zeros((ps.shape[0], wide - cols, 3 * ch), BF)

    def pieces(r):
        taken = 0
        for count, at in chunks:
            if r in at:
                mine = arrays[taken : taken + count]
                if count == 1:
                    return [mine[0][s, at[r]] for s in range(shards)]
                own, beside, across, both = [a[at[r]] for a in mine]
                here = [jnp.where(odd, beside, own), jnp.where(odd, own, beside)]
                there = [jnp.where(odd, both, across), jnp.where(odd, across, both)]
                lower = [jnp.where(high, t, h) for h, t in zip(here, there)]
                return lower + [jnp.where(high, h, t) for h, t in zip(here, there)]
            taken += count

    bias = vec_ref[BIAS : BIAS + 1, :] + vec_ref[BIAS + 1 : BIAS + 2, :] + vec_ref[BIAS + 2 : BIAS + 3, :]
    first = (lat == 0).astype(F32) * vec_ref[BIAS : BIAS + 1, :]
    last = (lat == lax.axis_size("lat") - 1).astype(F32) * vec_ref[BIAS + 2 : BIAS + 3, :]

    wanted = [list(range(a, a + n + 2)) for a, n in blocks]
    slots = {r: k for k, r in enumerate(sorted(set(sum(wanted, []))))}
    staged = set()

    def stage(n):
        for r in wanted[n]:
            if r in staged:
                continue
            staged.add(r)
            k = slots[r]
            row = jnp.concatenate(pieces(r), axis=0)
            ps[k, :cols, ch : 2 * ch] = row
            ps[k, :cols, :ch] = jnp.concatenate([row[-1:], row[:-1]], axis=0)
            ps[k, :cols, 2 * ch :] = jnp.concatenate([row[1:], row[:1]], axis=0)
            yield

    def conv(n):
        count = blocks[n][1]
        half = -(-count // 2)
        for lo, hi in ((0, half), (half, count)):
            p = [ps[slots[r]] for r in wanted[n][lo : hi + 2]]
            lhs = [jnp.concatenate(p[i : i + 3], axis=1) for i in range(hi - lo)]
            at = slice(lo * wide, hi * wide)
            cs[n % 2][at] = jnp.dot(jnp.concatenate(lhs, axis=0), ws_ref[...], preferred_element_type=F32)
            yield
            yield

    def finish(n):
        for i in range(blocks[n][1]):
            row = blocks[n][0] + i
            near = bias - first if row == 0 else (bias - last if row == rows - 1 else bias)
            y = cs[n % 2][i * wide : (i + 1) * wide] + near
            mixed = jnp.dot(zs_ref[...], gelu_twice(y), preferred_element_type=F32)
            center = ps[slots[row + 1], :, ch : 2 * ch].astype(F32)
            for lead in range(leads):
                lanes = slice(lead * ch, (lead + 1) * ch)
                mod = center * vec_ref[GAIN : GAIN + 1, lanes] + vec_ref[SHIFT : SHIFT + 1, lanes]
                outs[n, lead, i] = (mod + mixed[:, lanes]).astype(BF)[:cols]
            yield

    sends = []

    def send(n):
        for lead in range(leads):
            sends.append(
                pltpu.make_async_copy(
                    outs.at[n, lead, : blocks[n][1]],
                    out_ref.at[lead, blocks[n][0] : sum(blocks[n])],
                    out_sem.at[n, lead],
                )
            )
            sends[-1].start()

    together(stage(0))
    for n in range(len(blocks) + 1):
        together(
            conv(n) if n < len(blocks) else (),
            finish(n - 1) if n else (),
            stage(n + 1) if n + 1 < len(blocks) else (),
        )
        if n:
            send(n - 1)
    for c in sends:
        c.wait()


def forecast_heads(arrays, chunks, ws, vec, zs, so_far, blocks, shape):
    leads, rows, cols, ch = shape
    shards = cols // arrays[0].shape[-2]
    wide = zs.shape[0]
    vmem = pl.BlockSpec(memory_space=pltpu.VMEM)
    staged = len({a + i for a, n in blocks for i in range(n + 2)})
    tall = max(n for _, n in blocks)
    operands = [*arrays, ws, vec, zs]
    in_specs = [vmem] * len(operands)
    alias = {}
    if so_far is not None:
        alias = {len(operands): 0}
        operands.append(so_far)
        in_specs.append(pl.BlockSpec(memory_space=pltpu.HBM))
    return pl.pallas_call(
        functools.partial(head_kernel, chunks=chunks, blocks=blocks, shards=shards, aliased=len(alias)),
        in_specs=in_specs,
        out_specs=pl.BlockSpec(memory_space=pltpu.HBM),
        out_shape=jax.ShapeDtypeStruct(shape, BF),
        scratch_shapes=[
            pltpu.VMEM((staged, wide, 3 * ch), BF),
            pltpu.VMEM((tall * wide, leads * ch), F32),
            pltpu.VMEM((tall * wide, leads * ch), F32),
            pltpu.VMEM((len(blocks), leads, tall, cols, ch), BF),
            pltpu.SemaphoreType.DMA((len(blocks), leads)),
        ],
        input_output_aliases=alias,
        compiler_params=params(24 * -(-cols // 360)),
        cost_estimate=pl.CostEstimate(
            flops=sum(n for _, n in blocks) * cols * leads * ch * 2 * (9 * ch + cols),
            transcendentals=sum(n for _, n in blocks) * cols * leads * ch,
            bytes_accessed=len(blocks) * 8 * 1024 * 1024,
        ),
        name="heads",
    )(*operands)


def neighbours(size, wrap):
    count = size if wrap else size - 1
    up = [(i, (i + 1) % size) for i in range(count)]
    return up, [(j, i) for i, j in up]


def swap(size, bit):
    return [(i, i ^ bit) for i in range(size)]


def shards(inputs, w_enc, w_proj, film_scale, film_shift, lead_ids, w_head, zonal_mix):
    rows, cols, ch = inputs.shape
    tile = jnp.transpose(inputs, (1, 0, 2))
    lat, lon = lax.axis_size("lat"), lax.axis_size("lon")
    lat_up, lat_dn = neighbours(lat, False)
    lon_up, lon_dn = neighbours(lon, True)
    two_level = lon == 4
    reach = 2 * EDGE - 1
    leads = lead_ids.shape[0] // lon
    head = w_proj.shape[1]
    band_rows = rows // 2

    west = lax.ppermute(tile[-1], "lon", lon_up)
    east = lax.ppermute(tile[0], "lon", lon_dn)

    ws, vec, zs, edge = prepare(lead_ids, tile, w_head, film_scale, film_shift, zonal_mix, leads, reach)
    up, dn = row_slabs(edge, west, east)
    above = lax.ppermute(up, "lat", lat_up)
    below = lax.ppermute(dn, "lat", lat_dn)

    middle = band_rows // 2
    group = cols // 6
    plan = [
        (2 * EDGE, middle - EDGE, None),
        (2 * middle, band_rows - EDGE - middle, None),
        (None, 2 * (EDGE + 1), (above, below)),
    ]
    proj = [encode(tile, west, east, halos, w_enc, w_proj, first, n, group) for first, n, halos in plan]

    sent = []
    for k, own in enumerate(proj):
        if two_level:
            across = lax.ppermute(own, "lon", swap(lon, 2))
            beside = lax.ppermute(own, "lon", swap(lon, 1))
            if k == 2:
                both = lax.ppermute(own, "lon", swap(lon, 3))
            else:
                ready, _ = lax.optimization_barrier((across, proj[2]))
                both = lax.ppermute(ready, "lon", swap(lon, 1))
            sent.append([own, beside, across, both])
        else:
            sent.append([lax.all_gather(own, "lon", axis=0, tiled=False)])

    shape = (leads, band_rows, cols // 2 * lon, head)
    upper, lower = middle - EDGE, band_rows - EDGE - middle
    near = EDGE + 1
    count = band_rows - 2 * near
    parts = -(-count // STEP)
    cuts = [near + -(-count * i // parts) for i in range(parts + 1)]
    inside = [(a, b - a) for a, b in zip(cuts, cuts[1:])]
    at = [
        {EDGE + 1 + r: r for r in range(upper)},
        {middle + 1 + r: r for r in range(lower)},
        {(r if r <= EDGE else band_rows - EDGE - EDGE - 1 + r + 1): r for r in range(2 * EDGE + 2)},
    ]
    chunks = [(len(a), rows_at) for a, rows_at in zip(sent, at)]
    inner = forecast_heads(
        sent[0] + sent[1], chunks[:2], ws, vec, zs, None, inside, shape
    )
    return forecast_heads(
        sent[0] + sent[1] + sent[2], chunks, ws, vec, zs, inner, [(0, near), (band_rows - near, near)], shape
    )


def solution(mesh):
    in_specs = (P("lat", "lon", None), P(), P(), P(), P(), P(), P(), P())
    out_specs = P("lon", "lat", None, None)
    return jax.shard_map(shards, mesh=mesh, in_specs=in_specs, out_specs=out_specs, check_vma=False)
```

```python
import functools

import jax
import jax.numpy as jnp
from jax import lax
from jax.experimental import pallas as pl
from jax.experimental.pallas import tpu as pltpu
from jax.sharding import PartitionSpec as P

BF = jnp.bfloat16
F32 = jnp.float32
MIB = 1024 * 1024
EDGE = 2
STEP = 4
BIAS, GAIN, SHIFT = 0, 3, 4


def up_to(n, unit):
    return -(-n // unit) * unit


def gelu_twice(x):
    x = x.astype(BF)
    inner = x * (jnp.asarray(0.7978845608028654, BF) + jnp.asarray(0.035677408136300125, BF) * (x * x))
    return x + x * jnp.tanh(inner)


def together(*parts):
    parts = [iter(p) for p in parts]
    while parts:
        parts = [p for p in parts if next(p, parts) is not parts]


def params(mib):
    return pltpu.CompilerParams(vmem_limit_bytes=mib * MIB)


def edges_kernel(x_hbm, edge_ref, near, flat, sem):
    xcols, rows, ch = x_hbm.shape
    reach = edge_ref.shape[1]
    copies = [
        pltpu.make_async_copy(x_hbm.at[:, a : a + 8], near.at[k], sem.at[k]) for k, a in enumerate((0, rows - 8))
    ]
    for c in copies:
        c.start()
    for k in range(2):
        copies[k].wait()
        parts = []
        for j in range(ch // 128):
            flat[k, j] = near[k, :, :, j * 128 : (j + 1) * 128].astype(F32).reshape(xcols * 8, 128)
            first = 0 if k == 0 else 8 - reach
            parts.append([flat[k, j, pl.ds(first + i, xcols, stride=8), :] for i in range(reach)])
        for i in range(reach):
            edge_ref[k, i] = jnp.concatenate([p[i] for p in parts], axis=1).astype(BF)


def edge_rows(x, reach):
    xcols, _, ch = x.shape
    return pl.pallas_call(
        edges_kernel,
        in_specs=[pl.BlockSpec(memory_space=pltpu.HBM)],
        out_specs=pl.BlockSpec(memory_space=pltpu.VMEM),
        out_shape=jax.ShapeDtypeStruct((2, reach, xcols, ch), BF),
        scratch_shapes=[
            pltpu.VMEM((2, xcols, 8, ch), BF),
            pltpu.VMEM((2, ch // 128, xcols * 8, 128), F32),
            pltpu.SemaphoreType.DMA((2,)),
        ],
        compiler_params=params(58),
        cost_estimate=pl.CostEstimate(flops=1 << 31, transcendentals=0, bytes_accessed=12 * MIB),
        name="edges",
    )(x)


def weights_kernel(ids_ref, wh_ref, scale_ref, shift_ref, z_ref, ws_ref, vec_ref, zs_ref):
    head = wh_ref.shape[-1]
    leads = ws_ref.shape[1] // head
    cols = z_ref.shape[0]
    zs_ref[...] = jnp.zeros(zs_ref.shape, BF)
    zs_ref[:cols, :cols] = z_ref[...] * jnp.asarray(0.5, BF)
    for lead in range(leads):
        lanes = slice(lead * head, (lead + 1) * head)
        at = ids_ref[lax.axis_index("lon") * leads + lead]
        gain = 1.0 + scale_ref[pl.ds(at, 1), :]
        shift = shift_ref[pl.ds(at, 1), :]
        vec_ref[GAIN : GAIN + 1, lanes] = gain
        vec_ref[SHIFT : SHIFT + 1, lanes] = shift
        gain_t = jnp.transpose(jnp.broadcast_to(gain, (head, head)))
        shift_t = jnp.transpose(jnp.broadcast_to(shift, (head, head)))
        for dr in range(3):
            total = jnp.zeros((head, head), F32)
            for dc in range(3):
                at = (dr * 3 + dc) * head
                w = wh_ref[dr, dc].astype(F32)
                ws_ref[at : at + head, lanes] = (w * gain_t).astype(BF)
                total = total + w * shift_t
            vec_ref[BIAS + dr : BIAS + dr + 1, lanes] = jnp.sum(total, axis=0, keepdims=True)


def prepare(ids, w_head, scale, shift, z, leads):
    head, cols = w_head.shape[-1], z.shape[0]
    wide = up_to(cols, 16)
    vmem = pl.BlockSpec(memory_space=pltpu.VMEM)
    return pl.pallas_call(
        weights_kernel,
        in_specs=[pl.BlockSpec(memory_space=pltpu.SMEM)] + [vmem] * 4,
        out_specs=[vmem] * 3,
        out_shape=[
            jax.ShapeDtypeStruct((9 * head, leads * head), BF),
            jax.ShapeDtypeStruct((8, leads * head), F32),
            jax.ShapeDtypeStruct((wide, wide), BF),
        ],
        compiler_params=params(16),
        name="weights",
    )(ids, w_head, scale, shift, z)


def slabs_kernel(edge_ref, west_ref, east_ref, up_ref, dn_ref):
    rows = west_ref.shape[0]
    reach = up_ref.shape[0]
    for k, (slab, r) in enumerate(((dn_ref, 0), (up_ref, rows - reach))):
        for i in range(reach):
            ends = [side[r + i : r + i + 1, :] for side in (west_ref, east_ref)]
            slab[i] = jnp.concatenate([ends[0], edge_ref[k, i], ends[1]], axis=0)


def row_slabs(edge, west, east):
    _, reach, xcols, ch = edge.shape
    vmem = pl.BlockSpec(memory_space=pltpu.VMEM)
    return pl.pallas_call(
        slabs_kernel,
        in_specs=[vmem] * 3,
        out_specs=[vmem] * 2,
        out_shape=[jax.ShapeDtypeStruct((reach, xcols + 2, ch), BF)] * 2,
        compiler_params=params(12),
        cost_estimate=pl.CostEstimate(flops=1 << 32, transcendentals=0, bytes_accessed=12 * MIB),
        name="slabs",
    )(edge, west, east)


def encoder_kernel(x_ref, west_ref, east_ref, *refs, first, group):
    halos, refs = (refs[:2], refs[2:]) if first is None else ((), refs)
    w_ref, wp_ref, out_ref, g_ref, *refs = refs
    ch = x_ref.shape[2]
    for dr in range(3):
        at = slice(dr * ch, (dr + 1) * ch)
        w = [w_ref[dr, dc].astype(F32) for dc in range(3)]
        half = 0.5 * (w[0] + w[2])
        g_ref[0, at] = w_ref[dr, 0]
        g_ref[1, at] = (half + 0.5 * w[1]).astype(BF)
        g_ref[2, at] = (half - 0.5 * w[1]).astype(BF)
        g_ref[3, at] = w_ref[dr, 2]
    xs, ys0, ys1, st0, st1, pt = refs[:6]
    ys, st = (ys0, ys1), (st0, st1)
    cols, rows, ch = x_ref.shape
    reach = 2 * EDGE - 1
    if first is None:
        hf = refs[6]
        for k, halo in enumerate(halos):
            for j in range(ch // 128):
                lanes = slice(j * 128, (j + 1) * 128)
                for i in range(reach):
                    at = 8 - reach + i if k == 0 else i
                    hf[k, j, pl.ds(at, cols + 2, stride=8), :] = halo[i, :, lanes].astype(F32)
    low = 0 if first is None else (first - 1) // 8 * 8

    def stage(at, tile_rows):
        if first is None:
            far = []
            for k in range(2):
                h = [hf[k, j, at.start * 8 : at.stop * 8] for j in range(ch // 128)]
                h = [v.astype(BF).reshape(at.stop - at.start, 8, 128) for v in h]
                far.append(jnp.concatenate(h, axis=2))
            top = jnp.concatenate([far[0], tile_rows(0, 8)], axis=1)
            end = jnp.concatenate([tile_rows(rows - 8, 8), far[1]], axis=1)
            pad = jnp.zeros((at.stop - at.start, 16 - 4 * (EDGE + 1), ch), BF)
            n = 2 * (EDGE + 1)
            for dr in range(3):
                t = top[:, 8 - reach + dr : 8 - reach + dr + n]
                b = end[:, 8 - reach - 2 + dr : 8 - reach - 2 + dr + n]
                xs[at, :, dr * ch : (dr + 1) * ch] = jnp.concatenate([t, b, pad], axis=1)
        else:
            here = tile_rows(low, 24)
            for dr in range(3):
                off = first - 1 - low + dr
                xs[at, :, dr * ch : (dr + 1) * ch] = here[:, off : off + 16]

    pairs = cols // 2
    groups = pairs // group

    def stage_group(c):
        start, stop = 2 * c * group + (2 if c else 1), 2 * (c + 1) * group + 2
        if c == 0:
            stage(slice(0, 1), lambda a, n: west_ref[a : a + n, :].reshape(1, n, ch))
        if c == groups - 1:
            stage(slice(cols + 1, cols + 2), lambda a, n: east_ref[a : a + n, :].reshape(1, n, ch))
            stop = cols + 1
        size = -(-(stop - start) // 4)
        for p in range(start, stop, size):
            e = min(p + size, stop)
            stage(slice(p, e), lambda a, n: x_ref[p - 1 : e - 1, a : a + n, :])
            yield

    def multiply(c):
        for k, (i, j) in enumerate(((0, 2), (1, 2), (2, 1), (1, 3))):
            t = []
            for q in range(c * group, (c + 1) * group):
                one, two = xs[2 * q + i], xs[2 * q + j]
                t.append(one + two if k == 1 else one - two)
            ys[c % 2][k] = jnp.dot(jnp.concatenate(t, axis=0), g_ref[k], preferred_element_type=F32)
            yield

    def finish(c):
        n = group * 16
        sub = next(v for v in range(12, 0, -1) if group % v == 0) * 16
        for a in range(0, n, sub):
            part = slice(a, a + sub)
            m = [ys[c % 2].at[k, part] for k in range(4)]
            both = gelu_twice(m[0][...] + m[1][...] + m[2][...]).astype(F32)
            both = both + gelu_twice(m[1][...] - m[2][...] - m[3][...]).astype(F32)
            for j in range(ch // 128):
                st[c % 2][j, part] = both[:, j * 128 : (j + 1) * 128]
            yield
        pooled = [
            st[c % 2][j, pl.ds(0, n // 2, stride=2), :] + st[c % 2][j, pl.ds(1, n // 2, stride=2), :]
            for j in range(ch // 128)
        ]
        pooled = (jnp.concatenate(pooled, axis=1) * 0.125).astype(BF)
        pt[c * (n // 2) : (c + 1) * (n // 2)] = jnp.dot(pooled, wp_ref[...], preferred_element_type=F32)
        yield

    together(stage_group(0))
    for c in range(groups + 1):
        together(
            multiply(c) if c < groups else (),
            finish(c - 1) if c else (),
            stage_group(c + 1) if c + 1 < groups else (),
        )
    count = out_ref.shape[0]
    for r in range(count):
        row = pt[pl.ds(r, pairs, stride=8), :]
        if first is None and r in (0, count - 1):
            pole = 0 if r == 0 else lax.axis_size("lat") - 1
            row = jnp.where(lax.axis_index("lat") == pole, 0.0, row)
        out_ref[r] = row.astype(BF)


def encode(x, west, east, halos, w, wp, first, count, group):
    cols, rows, ch = x.shape
    head = wp.shape[1]
    vmem = pl.BlockSpec(memory_space=pltpu.VMEM)
    form = (4, 3 * ch, ch)
    scratch = [
        pltpu.VMEM(form, BF),
        pltpu.VMEM((cols + 2, 16, 3 * ch), BF),
        pltpu.VMEM((4, group * 16, ch), F32),
        pltpu.VMEM((4, group * 16, ch), F32),
        pltpu.VMEM((ch // 128, group * 16, 128), F32),
        pltpu.VMEM((ch // 128, group * 16, 128), F32),
        pltpu.VMEM((cols // 2 * 8, head), F32),
    ]
    if halos is not None:
        scratch.append(pltpu.VMEM((2, ch // 128, (cols + 2) * 8, 128), F32))
    operands = [x, west, east, *(halos or ()), w, wp]
    return pl.pallas_call(
        functools.partial(encoder_kernel, first=first, group=group),
        in_specs=[vmem] * len(operands),
        out_specs=vmem,
        out_shape=jax.ShapeDtypeStruct((count, cols // 2, head), BF),
        scratch_shapes=scratch,
        compiler_params=params(28),
        cost_estimate=pl.CostEstimate(
            flops=2 * cols * 16 * 6 * ch * ch, transcendentals=cols * 16 * ch, bytes_accessed=8 * MIB
        ),
        name="encode",
    )(*operands)


def head_kernel(*refs, chunks, blocks, shards, aliased):
    arrays = refs[: sum(n for n, _ in chunks)]
    ws_ref, vec_ref, zs_ref = refs[len(arrays) : len(arrays) + 3]
    out_ref, ps, cs0, cs1, outs, out_sem = refs[len(arrays) + 3 + aliased :]
    ch = ps.shape[2] // 3
    wide = ps.shape[1]
    leads, rows, cols, _ = out_ref.shape
    cs = (cs0, cs1)
    lat, lon = lax.axis_index("lat"), lax.axis_index("lon")
    odd = lon % 2 == 1
    high = lon // 2 == 1
    if wide > cols:
        ps[:, cols:, :] = jnp.zeros((ps.shape[0], wide - cols, 3 * ch), BF)

    def pieces(r):
        taken = 0
        for count, at in chunks:
            if r in at:
                mine = arrays[taken : taken + count]
                if count == 1:
                    return [mine[0][s, at[r]] for s in range(shards)]
                own, beside, across, both = [a[at[r]] for a in mine]
                here = [jnp.where(odd, beside, own), jnp.where(odd, own, beside)]
                there = [jnp.where(odd, both, across), jnp.where(odd, across, both)]
                lower = [jnp.where(high, t, h) for h, t in zip(here, there)]
                return lower + [jnp.where(high, h, t) for h, t in zip(here, there)]
            taken += count

    bias = vec_ref[BIAS : BIAS + 1, :] + vec_ref[BIAS + 1 : BIAS + 2, :] + vec_ref[BIAS + 2 : BIAS + 3, :]
    first = (lat == 0).astype(F32) * vec_ref[BIAS : BIAS + 1, :]
    last = (lat == lax.axis_size("lat") - 1).astype(F32) * vec_ref[BIAS + 2 : BIAS + 3, :]

    wanted = [list(range(a, a + n + 2)) for a, n in blocks]
    slots = {r: k for k, r in enumerate(sorted(set(sum(wanted, []))))}
    staged = set()

    def stage(n):
        for r in wanted[n]:
            if r in staged:
                continue
            staged.add(r)
            k = slots[r]
            row = jnp.concatenate(pieces(r), axis=0)
            ps[k, :cols, ch : 2 * ch] = row
            ps[k, :cols, :ch] = jnp.concatenate([row[-1:], row[:-1]], axis=0)
            ps[k, :cols, 2 * ch :] = jnp.concatenate([row[1:], row[:1]], axis=0)
            yield

    def conv(n):
        count = blocks[n][1]
        half = -(-count // 2)
        for lo, hi in ((0, half), (half, count)):
            p = [ps[slots[r]] for r in wanted[n][lo : hi + 2]]
            lhs = [jnp.concatenate(p[i : i + 3], axis=1) for i in range(hi - lo)]
            at = slice(lo * wide, hi * wide)
            cs[n % 2][at] = jnp.dot(jnp.concatenate(lhs, axis=0), ws_ref[...], preferred_element_type=F32)
            yield
            yield

    def finish(n):
        for i in range(blocks[n][1]):
            row = blocks[n][0] + i
            near = bias - first if row == 0 else (bias - last if row == rows - 1 else bias)
            y = cs[n % 2][i * wide : (i + 1) * wide] + near
            mixed = jnp.dot(zs_ref[...], gelu_twice(y), preferred_element_type=F32)
            center = ps[slots[row + 1], :, ch : 2 * ch].astype(F32)
            for lead in range(leads):
                lanes = slice(lead * ch, (lead + 1) * ch)
                mod = center * vec_ref[GAIN : GAIN + 1, lanes] + vec_ref[SHIFT : SHIFT + 1, lanes]
                outs[n, lead, i] = (mod + mixed[:, lanes]).astype(BF)[:cols]
            yield

    sends = []

    def send(n):
        for lead in range(leads):
            sends.append(
                pltpu.make_async_copy(
                    outs.at[n, lead, : blocks[n][1]],
                    out_ref.at[lead, blocks[n][0] : sum(blocks[n])],
                    out_sem.at[n, lead],
                )
            )
            sends[-1].start()

    together(stage(0))
    for n in range(len(blocks) + 1):
        together(
            conv(n) if n < len(blocks) else (),
            finish(n - 1) if n else (),
            stage(n + 1) if n + 1 < len(blocks) else (),
        )
        if n:
            send(n - 1)
    for c in sends:
        c.wait()


def forecast_heads(arrays, chunks, ws, vec, zs, so_far, blocks, shape):
    leads, rows, cols, ch = shape
    shards = cols // arrays[0].shape[-2]
    wide = zs.shape[0]
    vmem = pl.BlockSpec(memory_space=pltpu.VMEM)
    staged = len({a + i for a, n in blocks for i in range(n + 2)})
    tall = max(n for _, n in blocks)
    operands = [*arrays, ws, vec, zs]
    in_specs = [vmem] * len(operands)
    alias = {}
    if so_far is not None:
        alias = {len(operands): 0}
        operands.append(so_far)
        in_specs.append(pl.BlockSpec(memory_space=pltpu.HBM))
    return pl.pallas_call(
        functools.partial(head_kernel, chunks=chunks, blocks=blocks, shards=shards, aliased=len(alias)),
        in_specs=in_specs,
        out_specs=pl.BlockSpec(memory_space=pltpu.HBM),
        out_shape=jax.ShapeDtypeStruct(shape, BF),
        scratch_shapes=[
            pltpu.VMEM((staged, wide, 3 * ch), BF),
            pltpu.VMEM((tall * wide, leads * ch), F32),
            pltpu.VMEM((tall * wide, leads * ch), F32),
            pltpu.VMEM((len(blocks), leads, tall, cols, ch), BF),
            pltpu.SemaphoreType.DMA((len(blocks), leads)),
        ],
        input_output_aliases=alias,
        compiler_params=params(24 * -(-cols // 360)),
        cost_estimate=pl.CostEstimate(
            flops=sum(n for _, n in blocks) * cols * leads * ch * 2 * (9 * ch + cols),
            transcendentals=sum(n for _, n in blocks) * cols * leads * ch,
            bytes_accessed=len(blocks) * 8 * 1024 * 1024,
        ),
        name="heads",
    )(*operands)


def neighbours(size, wrap):
    count = size if wrap else size - 1
    up = [(i, (i + 1) % size) for i in range(count)]
    return up, [(j, i) for i, j in up]


def swap(size, bit):
    return [(i, i ^ bit) for i in range(size)]


def shards(inputs, w_enc, w_proj, film_scale, film_shift, lead_ids, w_head, zonal_mix):
    rows, cols, ch = inputs.shape
    tile = jnp.transpose(inputs, (1, 0, 2))
    lat, lon = lax.axis_size("lat"), lax.axis_size("lon")
    lat_up, lat_dn = neighbours(lat, False)
    lon_up, lon_dn = neighbours(lon, True)
    two_level = lon == 4
    reach = 2 * EDGE - 1
    leads = lead_ids.shape[0] // lon
    head = w_proj.shape[1]
    band_rows = rows // 2

    west = lax.ppermute(tile[-1], "lon", lon_up)
    east = lax.ppermute(tile[0], "lon", lon_dn)

    edge = edge_rows(tile, reach)
    up, dn = row_slabs(edge, west, east)
    west, east, up, dn = lax.optimization_barrier((west, east, up, dn))
    above = lax.ppermute(up, "lat", lat_up)
    below = lax.ppermute(dn, "lat", lat_dn)

    middle = band_rows // 2
    group = cols // 6
    upper = encode(tile, west, east, None, w_enc, w_proj, 2 * EDGE, middle - EDGE, group)
    lower = encode(tile, west, east, None, w_enc, w_proj, 2 * middle, band_rows - EDGE - middle, group)
    ids, _ = lax.optimization_barrier((lead_ids, lower))
    ws, vec, zs = prepare(ids, w_head, film_scale, film_shift, zonal_mix, leads)
    wp, ws, vec, zs = lax.optimization_barrier((w_proj, ws, vec, zs))
    edges = encode(tile, west, east, (above, below), w_enc, wp, None, 2 * (EDGE + 1), group)
    proj = [upper, lower, edges]

    sent = []
    for k, own in enumerate(proj):
        if two_level:
            across = lax.ppermute(own, "lon", swap(lon, 2))
            beside = lax.ppermute(own, "lon", swap(lon, 1))
            if k == 2:
                both = lax.ppermute(own, "lon", swap(lon, 3))
            else:
                ready, _ = lax.optimization_barrier((across, proj[2]))
                both = lax.ppermute(ready, "lon", swap(lon, 1))
            sent.append([own, beside, across, both])
        else:
            sent.append([lax.all_gather(own, "lon", axis=0, tiled=False)])

    shape = (leads, band_rows, cols // 2 * lon, head)
    upper, lower = middle - EDGE, band_rows - EDGE - middle
    near = EDGE + 1
    count = band_rows - 2 * near
    parts = -(-count // STEP)
    cuts = [near + -(-count * i // parts) for i in range(parts + 1)]
    inside = [(a, b - a) for a, b in zip(cuts, cuts[1:])]
    at = [
        {EDGE + 1 + r: r for r in range(upper)},
        {middle + 1 + r: r for r in range(lower)},
        {(r if r <= EDGE else band_rows - EDGE - EDGE - 1 + r + 1): r for r in range(2 * EDGE + 2)},
    ]
    chunks = [(len(a), rows_at) for a, rows_at in zip(sent, at)]
    inner = forecast_heads(
        sent[0] + sent[1], chunks[:2], ws, vec, zs, None, inside, shape
    )
    return forecast_heads(
        sent[0] + sent[1] + sent[2], chunks, ws, vec, zs, inner, [(0, near), (band_rows - near, near)], shape
    )


def solution(mesh):
    in_specs = (P("lat", "lon", None), P(), P(), P(), P(), P(), P(), P())
    out_specs = P("lon", "lat", None, None)
    return jax.shard_map(shards, mesh=mesh, in_specs=in_specs, out_specs=out_specs, check_vma=False)
```

```python
import functools

import jax
import jax.numpy as jnp
from jax import lax
from jax.experimental import pallas as pl
from jax.experimental.pallas import tpu as pltpu
from jax.sharding import PartitionSpec as P

BF = jnp.bfloat16
F32 = jnp.float32
MIB = 1024 * 1024
EDGE = 2
STEP = 4
BIAS, GAIN, SHIFT = 0, 3, 4


def up_to(n, unit):
    return -(-n // unit) * unit


def gelu_twice(x):
    x = x.astype(BF)
    inner = x * (jnp.asarray(0.7978845608028654, BF) + jnp.asarray(0.035677408136300125, BF) * (x * x))
    return x + x * jnp.tanh(inner)


def together(*parts):
    parts = [iter(p) for p in parts]
    while parts:
        parts = [p for p in parts if next(p, parts) is not parts]


def params(mib):
    return pltpu.CompilerParams(vmem_limit_bytes=mib * MIB)


def edges_kernel(x_hbm, edge_ref, near, flat, sem):
    xcols, rows, ch = x_hbm.shape
    reach = edge_ref.shape[1]
    copies = [
        pltpu.make_async_copy(x_hbm.at[:, a : a + 8], near.at[k], sem.at[k]) for k, a in enumerate((0, rows - 8))
    ]
    for c in copies:
        c.start()
    for k in range(2):
        copies[k].wait()
        parts = []
        for j in range(ch // 128):
            flat[k, j] = near[k, :, :, j * 128 : (j + 1) * 128].astype(F32).reshape(xcols * 8, 128)
            first = 0 if k == 0 else 8 - reach
            parts.append([flat[k, j, pl.ds(first + i, xcols, stride=8), :] for i in range(reach)])
        for i in range(reach):
            edge_ref[k, i] = jnp.concatenate([p[i] for p in parts], axis=1).astype(BF)


def edge_rows(x, reach):
    xcols, _, ch = x.shape
    return pl.pallas_call(
        edges_kernel,
        in_specs=[pl.BlockSpec(memory_space=pltpu.HBM)],
        out_specs=pl.BlockSpec(memory_space=pltpu.VMEM),
        out_shape=jax.ShapeDtypeStruct((2, reach, xcols, ch), BF),
        scratch_shapes=[
            pltpu.VMEM((2, xcols, 8, ch), BF),
            pltpu.VMEM((2, ch // 128, xcols * 8, 128), F32),
            pltpu.SemaphoreType.DMA((2,)),
        ],
        compiler_params=params(51),
        cost_estimate=pl.CostEstimate(flops=1 << 31, transcendentals=0, bytes_accessed=12 * MIB),
        name="edges",
    )(x)


def weights_kernel(ids_ref, wh_ref, scale_ref, shift_ref, z_ref, ws_ref, vec_ref, zs_ref):
    head = wh_ref.shape[-1]
    leads = ws_ref.shape[1] // head
    cols = z_ref.shape[0]
    zs_ref[...] = jnp.zeros(zs_ref.shape, BF)
    zs_ref[:cols, :cols] = z_ref[...] * jnp.asarray(0.5, BF)
    for lead in range(leads):
        lanes = slice(lead * head, (lead + 1) * head)
        at = ids_ref[lax.axis_index("lon") * leads + lead]
        gain = 1.0 + scale_ref[pl.ds(at, 1), :]
        shift = shift_ref[pl.ds(at, 1), :]
        vec_ref[GAIN : GAIN + 1, lanes] = gain
        vec_ref[SHIFT : SHIFT + 1, lanes] = shift
        gain_t = jnp.transpose(jnp.broadcast_to(gain, (head, head)))
        shift_t = jnp.transpose(jnp.broadcast_to(shift, (head, head)))
        for dr in range(3):
            total = jnp.zeros((head, head), F32)
            for dc in range(3):
                at = (dr * 3 + dc) * head
                w = wh_ref[dr, dc].astype(F32)
                ws_ref[at : at + head, lanes] = (w * gain_t).astype(BF)
                total = total + w * shift_t
            vec_ref[BIAS + dr : BIAS + dr + 1, lanes] = jnp.sum(total, axis=0, keepdims=True)


def prepare(ids, w_head, scale, shift, z, leads):
    head, cols = w_head.shape[-1], z.shape[0]
    wide = up_to(cols, 16)
    vmem = pl.BlockSpec(memory_space=pltpu.VMEM)
    return pl.pallas_call(
        weights_kernel,
        in_specs=[pl.BlockSpec(memory_space=pltpu.SMEM)] + [vmem] * 4,
        out_specs=[vmem] * 3,
        out_shape=[
            jax.ShapeDtypeStruct((9 * head, leads * head), BF),
            jax.ShapeDtypeStruct((8, leads * head), F32),
            jax.ShapeDtypeStruct((wide, wide), BF),
        ],
        compiler_params=params(16),
        name="weights",
    )(ids, w_head, scale, shift, z)


def slabs_kernel(edge_ref, west_ref, east_ref, up_ref, dn_ref):
    rows = west_ref.shape[0]
    reach = up_ref.shape[0]
    for k, (slab, r) in enumerate(((dn_ref, 0), (up_ref, rows - reach))):
        for i in range(reach):
            ends = [side[r + i : r + i + 1, :] for side in (west_ref, east_ref)]
            slab[i] = jnp.concatenate([ends[0], edge_ref[k, i], ends[1]], axis=0)


def row_slabs(edge, west, east):
    _, reach, xcols, ch = edge.shape
    vmem = pl.BlockSpec(memory_space=pltpu.VMEM)
    return pl.pallas_call(
        slabs_kernel,
        in_specs=[vmem] * 3,
        out_specs=[vmem] * 2,
        out_shape=[jax.ShapeDtypeStruct((reach, xcols + 2, ch), BF)] * 2,
        compiler_params=params(12),
        cost_estimate=pl.CostEstimate(flops=1 << 32, transcendentals=0, bytes_accessed=12 * MIB),
        name="slabs",
    )(edge, west, east)


def encoder_kernel(x_ref, west_ref, east_ref, *refs, first, group):
    halos, refs = (refs[:2], refs[2:]) if first is None else ((), refs)
    w_ref, wp_ref, out_ref, g_ref, *refs = refs
    ch = x_ref.shape[2]
    for dr in range(3):
        at = slice(dr * ch, (dr + 1) * ch)
        w = [w_ref[dr, dc].astype(F32) for dc in range(3)]
        half = 0.5 * (w[0] + w[2])
        g_ref[0, at] = w_ref[dr, 0]
        g_ref[1, at] = (half + 0.5 * w[1]).astype(BF)
        g_ref[2, at] = (half - 0.5 * w[1]).astype(BF)
        g_ref[3, at] = w_ref[dr, 2]
    xs, ys0, ys1, st0, st1, pt = refs[:6]
    ys, st = (ys0, ys1), (st0, st1)
    cols, rows, ch = x_ref.shape
    reach = 2 * EDGE - 1
    if first is None:
        hf = refs[6]
        for k, halo in enumerate(halos):
            for j in range(ch // 128):
                lanes = slice(j * 128, (j + 1) * 128)
                for i in range(reach):
                    at = 8 - reach + i if k == 0 else i
                    hf[k, j, pl.ds(at, cols + 2, stride=8), :] = halo[i, :, lanes].astype(F32)
    low = 0 if first is None else (first - 1) // 8 * 8

    def stage(at, tile_rows):
        if first is None:
            far = []
            for k in range(2):
                h = [hf[k, j, at.start * 8 : at.stop * 8] for j in range(ch // 128)]
                h = [v.astype(BF).reshape(at.stop - at.start, 8, 128) for v in h]
                far.append(jnp.concatenate(h, axis=2))
            top = jnp.concatenate([far[0], tile_rows(0, 8)], axis=1)
            end = jnp.concatenate([tile_rows(rows - 8, 8), far[1]], axis=1)
            pad = jnp.zeros((at.stop - at.start, 16 - 4 * (EDGE + 1), ch), BF)
            n = 2 * (EDGE + 1)
            for dr in range(3):
                t = top[:, 8 - reach + dr : 8 - reach + dr + n]
                b = end[:, 8 - reach - 2 + dr : 8 - reach - 2 + dr + n]
                xs[at, :, dr * ch : (dr + 1) * ch] = jnp.concatenate([t, b, pad], axis=1)
        else:
            here = tile_rows(low, 24)
            for dr in range(3):
                off = first - 1 - low + dr
                xs[at, :, dr * ch : (dr + 1) * ch] = here[:, off : off + 16]

    pairs = cols // 2
    groups = pairs // group

    def stage_group(c):
        start, stop = 2 * c * group + (2 if c else 1), 2 * (c + 1) * group + 2
        if c == 0:
            stage(slice(0, 1), lambda a, n: west_ref[a : a + n, :].reshape(1, n, ch))
        if c == groups - 1:
            stage(slice(cols + 1, cols + 2), lambda a, n: east_ref[a : a + n, :].reshape(1, n, ch))
            stop = cols + 1
        size = -(-(stop - start) // 4)
        for p in range(start, stop, size):
            e = min(p + size, stop)
            stage(slice(p, e), lambda a, n: x_ref[p - 1 : e - 1, a : a + n, :])
            yield

    def multiply(c):
        for k, (i, j) in enumerate(((0, 2), (1, 2), (2, 1), (1, 3))):
            t = []
            for q in range(c * group, (c + 1) * group):
                one, two = xs[2 * q + i], xs[2 * q + j]
                t.append(one + two if k == 1 else one - two)
            ys[c % 2][k] = jnp.dot(jnp.concatenate(t, axis=0), g_ref[k], preferred_element_type=F32)
            yield

    def finish(c):
        n = group * 16
        sub = next(v for v in range(12, 0, -1) if group % v == 0) * 16
        for a in range(0, n, sub):
            part = slice(a, a + sub)
            m = [ys[c % 2].at[k, part] for k in range(4)]
            both = gelu_twice(m[0][...] + m[1][...] + m[2][...]).astype(F32)
            both = both + gelu_twice(m[1][...] - m[2][...] - m[3][...]).astype(F32)
            for j in range(ch // 128):
                st[c % 2][j, part] = both[:, j * 128 : (j + 1) * 128]
            yield
        pooled = [
            st[c % 2][j, pl.ds(0, n // 2, stride=2), :] + st[c % 2][j, pl.ds(1, n // 2, stride=2), :]
            for j in range(ch // 128)
        ]
        pooled = (jnp.concatenate(pooled, axis=1) * 0.125).astype(BF)
        pt[c * (n // 2) : (c + 1) * (n // 2)] = jnp.dot(pooled, wp_ref[...], preferred_element_type=F32)
        yield

    together(stage_group(0))
    for c in range(groups + 1):
        together(
            multiply(c) if c < groups else (),
            finish(c - 1) if c else (),
            stage_group(c + 1) if c + 1 < groups else (),
        )
    count = out_ref.shape[0]
    for r in range(count):
        row = pt[pl.ds(r, pairs, stride=8), :]
        if first is None and r in (0, count - 1):
            pole = 0 if r == 0 else lax.axis_size("lat") - 1
            row = jnp.where(lax.axis_index("lat") == pole, 0.0, row)
        out_ref[r] = row.astype(BF)


def encode(x, west, east, halos, w, wp, first, count, group):
    cols, rows, ch = x.shape
    head = wp.shape[1]
    vmem = pl.BlockSpec(memory_space=pltpu.VMEM)
    form = (4, 3 * ch, ch)
    scratch = [
        pltpu.VMEM(form, BF),
        pltpu.VMEM((cols + 2, 16, 3 * ch), BF),
        pltpu.VMEM((4, group * 16, ch), F32),
        pltpu.VMEM((4, group * 16, ch), F32),
        pltpu.VMEM((ch // 128, group * 16, 128), F32),
        pltpu.VMEM((ch // 128, group * 16, 128), F32),
        pltpu.VMEM((cols // 2 * 8, head), F32),
    ]
    if halos is not None:
        scratch.append(pltpu.VMEM((2, ch // 128, (cols + 2) * 8, 128), F32))
    operands = [x, west, east, *(halos or ()), w, wp]
    return pl.pallas_call(
        functools.partial(encoder_kernel, first=first, group=group),
        in_specs=[vmem] * len(operands),
        out_specs=vmem,
        out_shape=jax.ShapeDtypeStruct((count, cols // 2, head), BF),
        scratch_shapes=scratch,
        compiler_params=params(28),
        cost_estimate=pl.CostEstimate(
            flops=2 * cols * 16 * 6 * ch * ch, transcendentals=cols * 16 * ch, bytes_accessed=8 * MIB
        ),
        name="encode",
    )(*operands)


def head_kernel(*refs, chunks, blocks, shards, aliased):
    arrays = refs[: sum(n for n, _ in chunks)]
    ws_ref, vec_ref, zs_ref = refs[len(arrays) : len(arrays) + 3]
    out_ref, ps, cs0, cs1, outs, out_sem = refs[len(arrays) + 3 + aliased :]
    ch = ps.shape[2] // 3
    wide = ps.shape[1]
    leads, rows, cols, _ = out_ref.shape
    cs = (cs0, cs1)
    lat, lon = lax.axis_index("lat"), lax.axis_index("lon")
    odd = lon % 2 == 1
    high = lon // 2 == 1
    if wide > cols:
        ps[:, cols:, :] = jnp.zeros((ps.shape[0], wide - cols, 3 * ch), BF)

    def pieces(r):
        taken = 0
        for count, at in chunks:
            if r in at:
                mine = arrays[taken : taken + count]
                if count == 1:
                    return [mine[0][s, at[r]] for s in range(shards)]
                own, beside, across, both = [a[at[r]] for a in mine]
                here = [jnp.where(odd, beside, own), jnp.where(odd, own, beside)]
                there = [jnp.where(odd, both, across), jnp.where(odd, across, both)]
                lower = [jnp.where(high, t, h) for h, t in zip(here, there)]
                return lower + [jnp.where(high, h, t) for h, t in zip(here, there)]
            taken += count

    bias = vec_ref[BIAS : BIAS + 1, :] + vec_ref[BIAS + 1 : BIAS + 2, :] + vec_ref[BIAS + 2 : BIAS + 3, :]
    first = (lat == 0).astype(F32) * vec_ref[BIAS : BIAS + 1, :]
    last = (lat == lax.axis_size("lat") - 1).astype(F32) * vec_ref[BIAS + 2 : BIAS + 3, :]

    wanted = [list(range(a, a + n + 2)) for a, n in blocks]
    slots = {r: k for k, r in enumerate(sorted(set(sum(wanted, []))))}
    staged = set()

    def stage(n):
        for r in wanted[n]:
            if r in staged:
                continue
            staged.add(r)
            k = slots[r]
            row = jnp.concatenate(pieces(r), axis=0)
            ps[k, :cols, ch : 2 * ch] = row
            ps[k, :cols, :ch] = jnp.concatenate([row[-1:], row[:-1]], axis=0)
            ps[k, :cols, 2 * ch :] = jnp.concatenate([row[1:], row[:1]], axis=0)
            yield

    def conv(n):
        count = blocks[n][1]
        half = -(-count // 2)
        for lo, hi in ((0, half), (half, count)):
            p = [ps[slots[r]] for r in wanted[n][lo : hi + 2]]
            lhs = [jnp.concatenate(p[i : i + 3], axis=1) for i in range(hi - lo)]
            at = slice(lo * wide, hi * wide)
            cs[n % 2][at] = jnp.dot(jnp.concatenate(lhs, axis=0), ws_ref[...], preferred_element_type=F32)
            yield
            yield

    def finish(n):
        for i in range(blocks[n][1]):
            row = blocks[n][0] + i
            near = bias - first if row == 0 else (bias - last if row == rows - 1 else bias)
            y = cs[n % 2][i * wide : (i + 1) * wide] + near
            mixed = jnp.dot(zs_ref[...], gelu_twice(y), preferred_element_type=F32)
            center = ps[slots[row + 1], :, ch : 2 * ch].astype(F32)
            for lead in range(leads):
                lanes = slice(lead * ch, (lead + 1) * ch)
                mod = center * vec_ref[GAIN : GAIN + 1, lanes] + vec_ref[SHIFT : SHIFT + 1, lanes]
                outs[n, lead, i] = (mod + mixed[:, lanes]).astype(BF)[:cols]
            yield

    sends = []

    def send(n):
        for lead in range(leads):
            sends.append(
                pltpu.make_async_copy(
                    outs.at[n, lead, : blocks[n][1]],
                    out_ref.at[lead, blocks[n][0] : sum(blocks[n])],
                    out_sem.at[n, lead],
                )
            )
            sends[-1].start()

    together(stage(0))
    for n in range(len(blocks) + 1):
        together(
            conv(n) if n < len(blocks) else (),
            finish(n - 1) if n else (),
            stage(n + 1) if n + 1 < len(blocks) else (),
        )
        if n:
            send(n - 1)
    for c in sends:
        c.wait()


def forecast_heads(arrays, chunks, ws, vec, zs, so_far, blocks, shape):
    leads, rows, cols, ch = shape
    shards = cols // arrays[0].shape[-2]
    wide = zs.shape[0]
    vmem = pl.BlockSpec(memory_space=pltpu.VMEM)
    staged = len({a + i for a, n in blocks for i in range(n + 2)})
    tall = max(n for _, n in blocks)
    operands = [*arrays, ws, vec, zs]
    in_specs = [vmem] * len(operands)
    alias = {}
    if so_far is not None:
        alias = {len(operands): 0}
        operands.append(so_far)
        in_specs.append(pl.BlockSpec(memory_space=pltpu.HBM))
    return pl.pallas_call(
        functools.partial(head_kernel, chunks=chunks, blocks=blocks, shards=shards, aliased=len(alias)),
        in_specs=in_specs,
        out_specs=pl.BlockSpec(memory_space=pltpu.HBM),
        out_shape=jax.ShapeDtypeStruct(shape, BF),
        scratch_shapes=[
            pltpu.VMEM((staged, wide, 3 * ch), BF),
            pltpu.VMEM((tall * wide, leads * ch), F32),
            pltpu.VMEM((tall * wide, leads * ch), F32),
            pltpu.VMEM((len(blocks), leads, tall, cols, ch), BF),
            pltpu.SemaphoreType.DMA((len(blocks), leads)),
        ],
        input_output_aliases=alias,
        compiler_params=params(24 * -(-cols // 360)),
        cost_estimate=pl.CostEstimate(
            flops=sum(n for _, n in blocks) * cols * leads * ch * 2 * (9 * ch + cols),
            transcendentals=sum(n for _, n in blocks) * cols * leads * ch,
            bytes_accessed=len(blocks) * 8 * 1024 * 1024,
        ),
        name="heads",
    )(*operands)


def neighbours(size, wrap):
    count = size if wrap else size - 1
    up = [(i, (i + 1) % size) for i in range(count)]
    return up, [(j, i) for i, j in up]


def swap(size, bit):
    return [(i, i ^ bit) for i in range(size)]


def shards(inputs, w_enc, w_proj, film_scale, film_shift, lead_ids, w_head, zonal_mix):
    rows, cols, ch = inputs.shape
    tile = jnp.transpose(inputs, (1, 0, 2))
    lat, lon = lax.axis_size("lat"), lax.axis_size("lon")
    lat_up, lat_dn = neighbours(lat, False)
    lon_up, lon_dn = neighbours(lon, True)
    two_level = lon == 4
    reach = 2 * EDGE - 1
    leads = lead_ids.shape[0] // lon
    head = w_proj.shape[1]
    band_rows = rows // 2

    west = lax.ppermute(tile[-1], "lon", lon_up)
    east = lax.ppermute(tile[0], "lon", lon_dn)

    edge = edge_rows(tile, reach)
    up, dn = row_slabs(edge, west, east)
    west, east, up, dn = lax.optimization_barrier((west, east, up, dn))
    above = lax.ppermute(up, "lat", lat_up)
    below = lax.ppermute(dn, "lat", lat_dn)

    middle = band_rows // 2
    group = cols // 6
    upper = encode(tile, west, east, None, w_enc, w_proj, 2 * EDGE, middle - EDGE, group)
    lower = encode(tile, west, east, None, w_enc, w_proj, 2 * middle, band_rows - EDGE - middle, group)
    ids, _ = lax.optimization_barrier((lead_ids, lower))
    ws, vec, zs = prepare(ids, w_head, film_scale, film_shift, zonal_mix, leads)
    wp, ws, vec, zs = lax.optimization_barrier((w_proj, ws, vec, zs))
    edges = encode(tile, west, east, (above, below), w_enc, wp, None, 2 * (EDGE + 1), group)
    proj = [upper, lower, edges]

    sent = []
    for k, own in enumerate(proj):
        if two_level:
            across = lax.ppermute(own, "lon", swap(lon, 2))
            beside = lax.ppermute(own, "lon", swap(lon, 1))
            if k == 2:
                both = lax.ppermute(own, "lon", swap(lon, 3))
            else:
                ready, _ = lax.optimization_barrier((across, proj[2]))
                both = lax.ppermute(ready, "lon", swap(lon, 1))
            sent.append([own, beside, across, both])
        else:
            sent.append([lax.all_gather(own, "lon", axis=0, tiled=False)])

    shape = (leads, band_rows, cols // 2 * lon, head)
    upper, lower = middle - EDGE, band_rows - EDGE - middle
    near = EDGE + 1
    count = band_rows - 2 * near
    parts = -(-count // STEP)
    cuts = [near + -(-count * i // parts) for i in range(parts + 1)]
    inside = [(a, b - a) for a, b in zip(cuts, cuts[1:])]
    at = [
        {EDGE + 1 + r: r for r in range(upper)},
        {middle + 1 + r: r for r in range(lower)},
        {(r if r <= EDGE else band_rows - EDGE - EDGE - 1 + r + 1): r for r in range(2 * EDGE + 2)},
    ]
    chunks = [(len(a), rows_at) for a, rows_at in zip(sent, at)]
    inner = forecast_heads(
        sent[0] + sent[1], chunks[:2], ws, vec, zs, None, inside, shape
    )
    return forecast_heads(
        sent[0] + sent[1] + sent[2], chunks, ws, vec, zs, inner, [(0, near), (band_rows - near, near)], shape
    )


def solution(mesh):
    in_specs = (P("lat", "lon", None), P(), P(), P(), P(), P(), P(), P())
    out_specs = P("lon", "lat", None, None)
    return jax.shard_map(shards, mesh=mesh, in_specs=in_specs, out_specs=out_specs, check_vma=False)
```

```python
import functools

import jax
import jax.numpy as jnp
from jax import lax
from jax.experimental import pallas as pl
from jax.experimental.pallas import tpu as pltpu
from jax.sharding import PartitionSpec as P

BF = jnp.bfloat16
F32 = jnp.float32
MIB = 1024 * 1024
EDGE = 2
STEP = 5
BIAS, GAIN, SHIFT = 0, 3, 4


def up_to(n, unit):
    return -(-n // unit) * unit


def gelu_twice(x):
    x = x.astype(BF)
    inner = x * (jnp.asarray(0.7978845608028654, BF) + jnp.asarray(0.035677408136300125, BF) * (x * x))
    return x + x * jnp.tanh(inner)


def together(*parts):
    parts = [iter(p) for p in parts]
    while parts:
        parts = [p for p in parts if next(p, parts) is not parts]


def params(mib):
    return pltpu.CompilerParams(vmem_limit_bytes=mib * MIB)


def edges_kernel(x_hbm, edge_ref, near, flat, sem):
    xcols, rows, ch = x_hbm.shape
    reach = edge_ref.shape[1]
    copies = [
        pltpu.make_async_copy(x_hbm.at[:, a : a + 8], near.at[k], sem.at[k]) for k, a in enumerate((0, rows - 8))
    ]
    for c in copies:
        c.start()
    for k in range(2):
        copies[k].wait()
        parts = []
        for j in range(ch // 128):
            flat[k, j] = near[k, :, :, j * 128 : (j + 1) * 128].astype(F32).reshape(xcols * 8, 128)
            first = 0 if k == 0 else 8 - reach
            parts.append([flat[k, j, pl.ds(first + i, xcols, stride=8), :] for i in range(reach)])
        for i in range(reach):
            edge_ref[k, i] = jnp.concatenate([p[i] for p in parts], axis=1).astype(BF)


def edge_rows(x, reach):
    xcols, _, ch = x.shape
    return pl.pallas_call(
        edges_kernel,
        in_specs=[pl.BlockSpec(memory_space=pltpu.HBM)],
        out_specs=pl.BlockSpec(memory_space=pltpu.VMEM),
        out_shape=jax.ShapeDtypeStruct((2, reach, xcols, ch), BF),
        scratch_shapes=[
            pltpu.VMEM((2, xcols, 8, ch), BF),
            pltpu.VMEM((2, ch // 128, xcols * 8, 128), F32),
            pltpu.SemaphoreType.DMA((2,)),
        ],
        compiler_params=params(51),
        cost_estimate=pl.CostEstimate(flops=1 << 31, transcendentals=0, bytes_accessed=12 * MIB),
        name="edges",
    )(x)


def weights_kernel(ids_ref, wh_ref, scale_ref, shift_ref, z_ref, ws_ref, vec_ref, zs_ref):
    head = wh_ref.shape[-1]
    leads = ws_ref.shape[1] // head
    cols = z_ref.shape[0]
    zs_ref[...] = jnp.zeros(zs_ref.shape, BF)
    zs_ref[:cols, :cols] = z_ref[...] * jnp.asarray(0.5, BF)
    for lead in range(leads):
        lanes = slice(lead * head, (lead + 1) * head)
        at = ids_ref[lax.axis_index("lon") * leads + lead]
        gain = 1.0 + scale_ref[pl.ds(at, 1), :]
        shift = shift_ref[pl.ds(at, 1), :]
        vec_ref[GAIN : GAIN + 1, lanes] = gain
        vec_ref[SHIFT : SHIFT + 1, lanes] = shift
        gain_t = jnp.transpose(jnp.broadcast_to(gain, (head, head)))
        shift_t = jnp.transpose(jnp.broadcast_to(shift, (head, head)))
        for dr in range(3):
            total = jnp.zeros((head, head), F32)
            for dc in range(3):
                at = (dr * 3 + dc) * head
                w = wh_ref[dr, dc].astype(F32)
                ws_ref[at : at + head, lanes] = (w * gain_t).astype(BF)
                total = total + w * shift_t
            vec_ref[BIAS + dr : BIAS + dr + 1, lanes] = jnp.sum(total, axis=0, keepdims=True)


def prepare(ids, w_head, scale, shift, z, leads):
    head, cols = w_head.shape[-1], z.shape[0]
    wide = up_to(cols, 16)
    vmem = pl.BlockSpec(memory_space=pltpu.VMEM)
    return pl.pallas_call(
        weights_kernel,
        in_specs=[pl.BlockSpec(memory_space=pltpu.SMEM)] + [vmem] * 4,
        out_specs=[vmem] * 3,
        out_shape=[
            jax.ShapeDtypeStruct((9 * head, leads * head), BF),
            jax.ShapeDtypeStruct((8, leads * head), F32),
            jax.ShapeDtypeStruct((wide, wide), BF),
        ],
        compiler_params=params(16),
        name="weights",
    )(ids, w_head, scale, shift, z)


def slabs_kernel(edge_ref, west_ref, east_ref, up_ref, dn_ref):
    rows = west_ref.shape[0]
    reach = up_ref.shape[0]
    for k, (slab, r) in enumerate(((dn_ref, 0), (up_ref, rows - reach))):
        for i in range(reach):
            ends = [side[r + i : r + i + 1, :] for side in (west_ref, east_ref)]
            slab[i] = jnp.concatenate([ends[0], edge_ref[k, i], ends[1]], axis=0)


def row_slabs(edge, west, east):
    _, reach, xcols, ch = edge.shape
    vmem = pl.BlockSpec(memory_space=pltpu.VMEM)
    return pl.pallas_call(
        slabs_kernel,
        in_specs=[vmem] * 3,
        out_specs=[vmem] * 2,
        out_shape=[jax.ShapeDtypeStruct((reach, xcols + 2, ch), BF)] * 2,
        compiler_params=params(12),
        cost_estimate=pl.CostEstimate(flops=1 << 32, transcendentals=0, bytes_accessed=12 * MIB),
        name="slabs",
    )(edge, west, east)


def encoder_kernel(x_ref, west_ref, east_ref, *refs, first, group):
    halos, refs = (refs[:2], refs[2:]) if first is None else ((), refs)
    w_ref, wp_ref, out_ref, g_ref, *refs = refs
    ch = x_ref.shape[2]
    for dr in range(3):
        at = slice(dr * ch, (dr + 1) * ch)
        w = [w_ref[dr, dc].astype(F32) for dc in range(3)]
        half = 0.5 * (w[0] + w[2])
        g_ref[0, at] = w_ref[dr, 0]
        g_ref[1, at] = (half + 0.5 * w[1]).astype(BF)
        g_ref[2, at] = (half - 0.5 * w[1]).astype(BF)
        g_ref[3, at] = w_ref[dr, 2]
    xs, ys0, ys1, st0, st1, pt = refs[:6]
    ys, st = (ys0, ys1), (st0, st1)
    cols, rows, ch = x_ref.shape
    reach = 2 * EDGE - 1
    if first is None:
        hf = refs[6]
        for k, halo in enumerate(halos):
            for j in range(ch // 128):
                lanes = slice(j * 128, (j + 1) * 128)
                for i in range(reach):
                    at = 8 - reach + i if k == 0 else i
                    hf[k, j, pl.ds(at, cols + 2, stride=8), :] = halo[i, :, lanes].astype(F32)
    low = 0 if first is None else (first - 1) // 8 * 8

    def stage(at, tile_rows):
        if first is None:
            far = []
            for k in range(2):
                h = [hf[k, j, at.start * 8 : at.stop * 8] for j in range(ch // 128)]
                h = [v.astype(BF).reshape(at.stop - at.start, 8, 128) for v in h]
                far.append(jnp.concatenate(h, axis=2))
            top = jnp.concatenate([far[0], tile_rows(0, 8)], axis=1)
            end = jnp.concatenate([tile_rows(rows - 8, 8), far[1]], axis=1)
            pad = jnp.zeros((at.stop - at.start, 16 - 4 * (EDGE + 1), ch), BF)
            n = 2 * (EDGE + 1)
            for dr in range(3):
                t = top[:, 8 - reach + dr : 8 - reach + dr + n]
                b = end[:, 8 - reach - 2 + dr : 8 - reach - 2 + dr + n]
                xs[at, :, dr * ch : (dr + 1) * ch] = jnp.concatenate([t, b, pad], axis=1)
        else:
            here = tile_rows(low, 24)
            for dr in range(3):
                off = first - 1 - low + dr
                xs[at, :, dr * ch : (dr + 1) * ch] = here[:, off : off + 16]

    pairs = cols // 2
    groups = pairs // group

    def stage_group(c):
        start, stop = 2 * c * group + (2 if c else 1), 2 * (c + 1) * group + 2
        if c == 0:
            stage(slice(0, 1), lambda a, n: west_ref[a : a + n, :].reshape(1, n, ch))
        if c == groups - 1:
            stage(slice(cols + 1, cols + 2), lambda a, n: east_ref[a : a + n, :].reshape(1, n, ch))
            stop = cols + 1
        size = -(-(stop - start) // 4)
        for p in range(start, stop, size):
            e = min(p + size, stop)
            stage(slice(p, e), lambda a, n: x_ref[p - 1 : e - 1, a : a + n, :])
            yield

    def multiply(c):
        for k, (i, j) in enumerate(((0, 2), (1, 2), (2, 1), (1, 3))):
            t = []
            for q in range(c * group, (c + 1) * group):
                one, two = xs[2 * q + i], xs[2 * q + j]
                t.append(one + two if k == 1 else one - two)
            ys[c % 2][k] = jnp.dot(jnp.concatenate(t, axis=0), g_ref[k], preferred_element_type=F32)
            yield

    def finish(c):
        n = group * 16
        sub = next(v for v in range(12, 0, -1) if group % v == 0) * 16
        for a in range(0, n, sub):
            part = slice(a, a + sub)
            m = [ys[c % 2].at[k, part] for k in range(4)]
            both = gelu_twice(m[0][...] + m[1][...] + m[2][...]).astype(F32)
            both = both + gelu_twice(m[1][...] - m[2][...] - m[3][...]).astype(F32)
            for j in range(ch // 128):
                st[c % 2][j, part] = both[:, j * 128 : (j + 1) * 128]
            yield
        pooled = [
            st[c % 2][j, pl.ds(0, n // 2, stride=2), :] + st[c % 2][j, pl.ds(1, n // 2, stride=2), :]
            for j in range(ch // 128)
        ]
        pooled = (jnp.concatenate(pooled, axis=1) * 0.125).astype(BF)
        pt[c * (n // 2) : (c + 1) * (n // 2)] = jnp.dot(pooled, wp_ref[...], preferred_element_type=F32)
        yield

    together(stage_group(0))
    for c in range(groups + 1):
        together(
            multiply(c) if c < groups else (),
            finish(c - 1) if c else (),
            stage_group(c + 1) if c + 1 < groups else (),
        )
    count = out_ref.shape[0]
    for r in range(count):
        row = pt[pl.ds(r, pairs, stride=8), :]
        if first is None and r in (0, count - 1):
            pole = 0 if r == 0 else lax.axis_size("lat") - 1
            row = jnp.where(lax.axis_index("lat") == pole, 0.0, row)
        out_ref[r] = row.astype(BF)


def encode(x, west, east, halos, w, wp, first, count, group):
    cols, rows, ch = x.shape
    head = wp.shape[1]
    vmem = pl.BlockSpec(memory_space=pltpu.VMEM)
    form = (4, 3 * ch, ch)
    scratch = [
        pltpu.VMEM(form, BF),
        pltpu.VMEM((cols + 2, 16, 3 * ch), BF),
        pltpu.VMEM((4, group * 16, ch), F32),
        pltpu.VMEM((4, group * 16, ch), F32),
        pltpu.VMEM((ch // 128, group * 16, 128), F32),
        pltpu.VMEM((ch // 128, group * 16, 128), F32),
        pltpu.VMEM((cols // 2 * 8, head), F32),
    ]
    if halos is not None:
        scratch.append(pltpu.VMEM((2, ch // 128, (cols + 2) * 8, 128), F32))
    operands = [x, west, east, *(halos or ()), w, wp]
    return pl.pallas_call(
        functools.partial(encoder_kernel, first=first, group=group),
        in_specs=[vmem] * len(operands),
        out_specs=vmem,
        out_shape=jax.ShapeDtypeStruct((count, cols // 2, head), BF),
        scratch_shapes=scratch,
        compiler_params=params(28),
        cost_estimate=pl.CostEstimate(
            flops=2 * cols * 16 * 6 * ch * ch, transcendentals=cols * 16 * ch, bytes_accessed=8 * MIB
        ),
        name="encode",
    )(*operands)


def head_kernel(*refs, chunks, blocks, shards, aliased):
    arrays = refs[: sum(n for n, _ in chunks)]
    ws_ref, vec_ref, zs_ref = refs[len(arrays) : len(arrays) + 3]
    out_ref, ps, cs0, cs1, outs, out_sem = refs[len(arrays) + 3 + aliased :]
    ch = ps.shape[2] // 3
    wide = ps.shape[1]
    leads, rows, cols, _ = out_ref.shape
    cs = (cs0, cs1)
    lat, lon = lax.axis_index("lat"), lax.axis_index("lon")
    odd = lon % 2 == 1
    high = lon // 2 == 1
    if wide > cols:
        ps[:, cols:, :] = jnp.zeros((ps.shape[0], wide - cols, 3 * ch), BF)

    def pieces(r):
        taken = 0
        for count, at in chunks:
            if r in at:
                mine = arrays[taken : taken + count]
                if count == 1:
                    return [mine[0][s, at[r]] for s in range(shards)]
                own, beside, across, both = [a[at[r]] for a in mine]
                here = [jnp.where(odd, beside, own), jnp.where(odd, own, beside)]
                there = [jnp.where(odd, both, across), jnp.where(odd, across, both)]
                lower = [jnp.where(high, t, h) for h, t in zip(here, there)]
                return lower + [jnp.where(high, h, t) for h, t in zip(here, there)]
            taken += count

    bias = vec_ref[BIAS : BIAS + 1, :] + vec_ref[BIAS + 1 : BIAS + 2, :] + vec_ref[BIAS + 2 : BIAS + 3, :]
    first = (lat == 0).astype(F32) * vec_ref[BIAS : BIAS + 1, :]
    last = (lat == lax.axis_size("lat") - 1).astype(F32) * vec_ref[BIAS + 2 : BIAS + 3, :]

    wanted = [list(range(a, a + n + 2)) for a, n in blocks]
    slots = {r: k for k, r in enumerate(sorted(set(sum(wanted, []))))}
    staged = set()

    def stage(n):
        for r in wanted[n]:
            if r in staged:
                continue
            staged.add(r)
            k = slots[r]
            row = jnp.concatenate(pieces(r), axis=0)
            ps[k, :cols, ch : 2 * ch] = row
            ps[k, :cols, :ch] = jnp.concatenate([row[-1:], row[:-1]], axis=0)
            ps[k, :cols, 2 * ch :] = jnp.concatenate([row[1:], row[:1]], axis=0)
            yield

    def conv(n):
        count = blocks[n][1]
        half = -(-count // 2)
        for lo, hi in ((0, half), (half, count)):
            p = [ps[slots[r]] for r in wanted[n][lo : hi + 2]]
            lhs = [jnp.concatenate(p[i : i + 3], axis=1) for i in range(hi - lo)]
            at = slice(lo * wide, hi * wide)
            cs[n % 2][at] = jnp.dot(jnp.concatenate(lhs, axis=0), ws_ref[...], preferred_element_type=F32)
            yield
            yield

    def finish(n):
        for i in range(blocks[n][1]):
            row = blocks[n][0] + i
            near = bias - first if row == 0 else (bias - last if row == rows - 1 else bias)
            y = cs[n % 2][i * wide : (i + 1) * wide] + near
            mixed = jnp.dot(zs_ref[...], gelu_twice(y), preferred_element_type=F32)
            center = ps[slots[row + 1], :, ch : 2 * ch].astype(F32)
            for lead in range(leads):
                lanes = slice(lead * ch, (lead + 1) * ch)
                mod = center * vec_ref[GAIN : GAIN + 1, lanes] + vec_ref[SHIFT : SHIFT + 1, lanes]
                outs[n, lead, i] = (mod + mixed[:, lanes]).astype(BF)[:cols]
            yield

    sends = []

    def send(n):
        for lead in range(leads):
            sends.append(
                pltpu.make_async_copy(
                    outs.at[n, lead, : blocks[n][1]],
                    out_ref.at[lead, blocks[n][0] : sum(blocks[n])],
                    out_sem.at[n, lead],
                )
            )
            sends[-1].start()

    together(stage(0))
    for n in range(len(blocks) + 1):
        together(
            conv(n) if n < len(blocks) else (),
            finish(n - 1) if n else (),
            stage(n + 1) if n + 1 < len(blocks) else (),
        )
        if n:
            send(n - 1)
    for c in sends:
        c.wait()


def forecast_heads(arrays, chunks, ws, vec, zs, so_far, blocks, shape):
    leads, rows, cols, ch = shape
    shards = cols // arrays[0].shape[-2]
    wide = zs.shape[0]
    vmem = pl.BlockSpec(memory_space=pltpu.VMEM)
    staged = len({a + i for a, n in blocks for i in range(n + 2)})
    tall = max(n for _, n in blocks)
    operands = [*arrays, ws, vec, zs]
    in_specs = [vmem] * len(operands)
    alias = {}
    if so_far is not None:
        alias = {len(operands): 0}
        operands.append(so_far)
        in_specs.append(pl.BlockSpec(memory_space=pltpu.HBM))
    return pl.pallas_call(
        functools.partial(head_kernel, chunks=chunks, blocks=blocks, shards=shards, aliased=len(alias)),
        in_specs=in_specs,
        out_specs=pl.BlockSpec(memory_space=pltpu.HBM),
        out_shape=jax.ShapeDtypeStruct(shape, BF),
        scratch_shapes=[
            pltpu.VMEM((staged, wide, 3 * ch), BF),
            pltpu.VMEM((tall * wide, leads * ch), F32),
            pltpu.VMEM((tall * wide, leads * ch), F32),
            pltpu.VMEM((len(blocks), leads, tall, cols, ch), BF),
            pltpu.SemaphoreType.DMA((len(blocks), leads)),
        ],
        input_output_aliases=alias,
        compiler_params=params(24 * -(-cols // 360)),
        cost_estimate=pl.CostEstimate(
            flops=sum(n for _, n in blocks) * cols * leads * ch * 2 * (9 * ch + cols),
            transcendentals=sum(n for _, n in blocks) * cols * leads * ch,
            bytes_accessed=len(blocks) * 8 * 1024 * 1024,
        ),
        name="heads",
    )(*operands)


def neighbours(size, wrap):
    count = size if wrap else size - 1
    up = [(i, (i + 1) % size) for i in range(count)]
    return up, [(j, i) for i, j in up]


def swap(size, bit):
    return [(i, i ^ bit) for i in range(size)]


def shards(inputs, w_enc, w_proj, film_scale, film_shift, lead_ids, w_head, zonal_mix):
    rows, cols, ch = inputs.shape
    tile = jnp.transpose(inputs, (1, 0, 2))
    lat, lon = lax.axis_size("lat"), lax.axis_size("lon")
    lat_up, lat_dn = neighbours(lat, False)
    lon_up, lon_dn = neighbours(lon, True)
    two_level = lon == 4
    reach = 2 * EDGE - 1
    leads = lead_ids.shape[0] // lon
    head = w_proj.shape[1]
    band_rows = rows // 2

    west = lax.ppermute(tile[-1], "lon", lon_up)
    east = lax.ppermute(tile[0], "lon", lon_dn)

    edge = edge_rows(tile, reach)
    up, dn = row_slabs(edge, west, east)
    west, east, up, dn = lax.optimization_barrier((west, east, up, dn))
    above = lax.ppermute(up, "lat", lat_up)
    below = lax.ppermute(dn, "lat", lat_dn)

    middle = band_rows // 2
    group = cols // 6
    upper = encode(tile, west, east, None, w_enc, w_proj, 2 * EDGE, middle - EDGE, group)
    lower = encode(tile, west, east, None, w_enc, w_proj, 2 * middle, band_rows - EDGE - middle, group)
    ids, _ = lax.optimization_barrier((lead_ids, lower))
    ws, vec, zs = prepare(ids, w_head, film_scale, film_shift, zonal_mix, leads)
    wp, ws, vec, zs = lax.optimization_barrier((w_proj, ws, vec, zs))
    edges = encode(tile, west, east, (above, below), w_enc, wp, None, 2 * (EDGE + 1), group)
    proj = [upper, lower, edges]

    sent = []
    for k, own in enumerate(proj):
        if two_level:
            across = lax.ppermute(own, "lon", swap(lon, 2))
            beside = lax.ppermute(own, "lon", swap(lon, 1))
            if k == 2:
                both = lax.ppermute(own, "lon", swap(lon, 3))
            else:
                ready, _ = lax.optimization_barrier((across, proj[2]))
                both = lax.ppermute(ready, "lon", swap(lon, 1))
            sent.append([own, beside, across, both])
        else:
            sent.append([lax.all_gather(own, "lon", axis=0, tiled=False)])

    shape = (leads, band_rows, cols // 2 * lon, head)
    upper, lower = middle - EDGE, band_rows - EDGE - middle
    near = EDGE + 1
    count = band_rows - 2 * near
    parts = -(-count // STEP)
    cuts = [near + -(-count * i // parts) for i in range(parts + 1)]
    inside = [(a, b - a) for a, b in zip(cuts, cuts[1:])]
    at = [
        {EDGE + 1 + r: r for r in range(upper)},
        {middle + 1 + r: r for r in range(lower)},
        {(r if r <= EDGE else band_rows - EDGE - EDGE - 1 + r + 1): r for r in range(2 * EDGE + 2)},
    ]
    chunks = [(len(a), rows_at) for a, rows_at in zip(sent, at)]
    inner = forecast_heads(
        sent[0] + sent[1], chunks[:2], ws, vec, zs, None, inside, shape
    )
    return forecast_heads(
        sent[0] + sent[1] + sent[2], chunks, ws, vec, zs, inner, [(0, near), (band_rows - near, near)], shape
    )


def solution(mesh):
    in_specs = (P("lat", "lon", None), P(), P(), P(), P(), P(), P(), P())
    out_specs = P("lon", "lat", None, None)
    return jax.shard_map(shards, mesh=mesh, in_specs=in_specs, out_specs=out_specs, check_vma=False)
```
